32 devices in a mesh: section: 2 (over y), rep: 4 (over z), shard: 4 (over x, core).
Axes of the slice: x: 2, y: 2, z: 4, core: 2. Of those that a mesh axis runs over, the one named last changes fastest.
Arguments:
- tokens: bfloat16 [3072, 2560], P(('rep', 'shard')), may hold values from -6 to 6
- segment_ids: int32 [32, 96], P(('rep', 'shard')), may hold values from 0 to 5, never falling along the last dimension, each value on 1 to 64 neighbouring positions
- input_gain: float32 [2, 2560], P('section'), may hold values from 0.25 to 1.75
- query_gain: float32 [2, 768], P('section'), may hold values from 0.25 to 1.75
- latent_gain: float32 [2, 256], P('section'), may hold values from 0.25 to 1.75
- post_gain: float32 [2, 2560], P('section'), may hold values from 0.25 to 1.75
- query_down: bfloat16 [2, 2560, 768], P('section', 'shard'), may hold values from -0.125 to 0.125
- query_up: bfloat16 [2, 768, 3840], P('section', 'shard'), may hold values from -0.21875 to 0.21875
- latent_down: bfloat16 [2, 2560, 288], P('section', 'shard'), may hold values from -0.125 to 0.125
- latent_up: bfloat16 [2, 256, 5120], P('section', 'shard'), may hold values from -0.375 to 0.375
- output_weight: bfloat16 [2, 2560, 2560], P('section', 'shard'), may hold values from -2 to 2
- gate_weight: bfloat16 [2, 2560, 6400], P('section', 'shard'), may hold values from -0.125 to 0.125
- up_weight: bfloat16 [2, 2560, 6400], P('section', 'shard'), may hold values from -0.125 to 0.125
- down_weight: bfloat16 [2, 6400, 2560], P('section', 'shard'), may hold values from -0.625 to 0.625
- cotangent: bfloat16 [3072, 2560], P(('rep', 'shard')), may hold values from -6 to 6
Outputs:
- boundary: bfloat16 [2, 3072, 2560], P('section', ('rep', 'shard'))
- input_grads: float32 [2, 3072, 2560], P('section', ('rep', 'shard'))
- grad_input_gain: float32 [2, 2560], P('section')
- grad_query_gain: float32 [2, 768], P('section')
- grad_latent_gain: float32 [2, 256], P('section')
- grad_post_gain: float32 [2, 2560], P('section')
- grad_query_down: float32 [2, 2560, 768], P('section', 'shard')
- grad_query_up: float32 [2, 768, 3840], P('section', 'shard')
- grad_latent_down: float32 [2, 2560, 288], P('section', 'shard')
- grad_latent_up: float32 [2, 256, 5120], P('section', 'shard')
- grad_output_weight: float32 [2, 2560, 2560], P('section', 'shard')
- grad_gate_weight: float32 [2, 2560, 6400], P('section', 'shard')
- grad_up_weight: float32 [2, 2560, 6400], P('section', 'shard')
- grad_down_weight: float32 [2, 6400, 2560], P('section', 'shard')
The draws below stay inside these ranges and needn't reach their ends.
Inputs may be any that keep to these rules, and one draw needn't show every extreme that they name: `segment_ids`: each row holds the sequence numbers of the 96 packed positions of one slot; they never fall along a row, and each sequence spans 1 to 64 positions.
All inputs are finite; a program needn't handle non-finite values.
Results may differ from the reference program's by a relative error of at most 0.03.
Values may be sent and summed in bfloat16 or wider, within the bound.
A program may use at most 576 MiB of HBM per device.

```python
import math
import jax
import jax.numpy as jnp
import numpy as np
from jax import lax

D = 2560
HEADS = 40
NOPE = 64
ROPE = 32
VDIM = 64
QRANK = 768
KVRANK = 256
FF = 6400
SLOT = 96
SEQ_MOST = 64
SLOTS = 32
TOKENS = 3072


def block_levels(stream_key, extent, pieces, smallest, high):
    loudness = 1.0
    for axis_at, shards_of in pieces:
        steps = jax.random.uniform(jax.random.fold_in(jax.random.fold_in(stream_key, 6), axis_at), (shards_of,), jnp.float32, smallest / len(pieces), high / len(pieces))
        loudness = loudness * jnp.repeat(jnp.exp(steps), extent[axis_at] // shards_of).reshape((-1,) + (1,) * (len(extent) - 1 - axis_at))
    return loudness


def profile(amount, total, most, slope):
    weights = [(1 << 20) // math.isqrt(grade ** slope) + 1 for grade in range(2, amount + 1)]
    rest, given = total - most - (amount - 1), [1] * (amount - 1)
    while rest > 0:
        free = [i for i in range(amount - 1) if given[i] < most]
        mass, remaining = sum([weights[i] for i in free]), rest
        for i in free:
            extra = min(most - given[i], max(1, remaining * weights[i] // mass), rest)
            given[i] = given[i] + extra
            rest = rest - extra
    return np.array([most] + given)


def uneven(key, count, total, bound, slope):
    if count == 2:
        one = jax.random.randint(key, (), max(1, total - bound), min(bound, total - 1) + 1)
        return jnp.stack([one, total - one])
    sizes = jnp.asarray(profile(count, total, bound, slope), jnp.int32)
    twos = (count - 1) // 2
    giver, receiver = sizes[1:1 + 2 * twos:2], sizes[2:2 + 2 * twos:2]
    margin = jnp.minimum(giver - 1, bound - receiver)
    shifted = jax.random.randint(jax.random.fold_in(key, 1), (twos,), 0, 1 << 20) % (margin + 1)
    sizes = sizes.at[1:1 + 2 * twos:2].set(giver - shifted).at[2:2 + 2 * twos:2].set(receiver + shifted)
    return sizes[jax.random.permutation(jax.random.fold_in(key, 2), count)]


def bell_draw(key, extent, spread, bound, split=(), held_as=jnp.bfloat16):
    array = spread * jax.random.normal(key, extent, jnp.float32)
    if split:
        array = array * block_levels(key, extent, split, -0.22, 0.18)
    return jnp.clip(array, -bound, bound).astype(held_as)


def setup_inputs(seed: int = 0) -> dict:
    key_of = jax.random.split(jax.random.key(seed), 16)
    return {
        "tokens": bell_draw(key_of[0], (TOKENS, D), 1.0, 6.0, ((0, 16),)),
        "segment_ids": jax.vmap(lambda own: jnp.searchsorted(jnp.cumsum(uneven(own, SLOT // 16, SLOT, SEQ_MOST, 2)), jnp.arange(SLOT), side="right"))(jax.random.split(key_of[1], SLOTS)).reshape((SLOTS, SLOT)).astype(jnp.int32),
        "input_gain": jnp.clip(1.0 + 0.15 * jax.random.normal(key_of[2], (2, D), jnp.float32), 0.25, 1.75),
        "query_gain": jnp.clip(1.0 + 0.15 * jax.random.normal(key_of[3], (2, QRANK), jnp.float32), 0.25, 1.75),
        "latent_gain": jnp.clip(1.0 + 0.15 * jax.random.normal(key_of[4], (2, KVRANK), jnp.float32), 0.25, 1.75),
        "post_gain": jnp.clip(1.0 + 0.15 * jax.random.normal(key_of[5], (2, D), jnp.float32), 0.25, 1.75),
        "query_down": bell_draw(key_of[6], (2, D, QRANK), D ** -0.5, 0.125, ((0, 2), (1, 4))),
        "query_up": bell_draw(key_of[7], (2, QRANK, HEADS * (NOPE + ROPE)), QRANK ** -0.5, 0.21875, ((0, 2), (1, 4))),
        "latent_down": bell_draw(key_of[8], (2, D, KVRANK + ROPE), D ** -0.5, 0.125, ((0, 2), (1, 4))),
        "latent_up": bell_draw(key_of[9], (2, KVRANK, HEADS * (NOPE + VDIM)), KVRANK ** -0.5, 0.375, ((0, 2), (1, 4))),
        "output_weight": bell_draw(key_of[10], (2, HEADS * VDIM, D), (max(HEADS * VDIM // 256, 1)) ** -0.5, 2.0, ((0, 2), (1, 4))),
        "gate_weight": bell_draw(key_of[11], (2, D, FF), D ** -0.5, 0.125, ((0, 2), (1, 4))),
        "up_weight": bell_draw(key_of[12], (2, D, FF), D ** -0.5, 0.125, ((0, 2), (1, 4))),
        "down_weight": bell_draw(key_of[13], (2, FF, D), (FF // 64) ** -0.5, 0.625, ((0, 2), (1, 4))),
        "cotangent": bell_draw(key_of[14], (TOKENS, D), 1.0, 6.0, ((0, 16),)),
    }


@jax.custom_vjp
def low(v):
    return lax.optimization_barrier(v.astype(jnp.bfloat16)).astype(jnp.float32)

@jax.custom_vjp
def low_back(v):
    return v

def low_keep(v):
    return (low(v), None)

def low_pass(kept, grad):
    return (grad,)

def back_keep(v):
    return (v, None)

def back_low(kept, grad):
    return (low(grad),)
low.defvjp(low_keep, low_pass)
low_back.defvjp(back_keep, back_low)
epsilon = 1e-05
residual_scale = 1.4 / math.sqrt(62.0)
masked_score = -1e+30
highest = lax.Precision.HIGHEST

def matmul(left, right):
    return jnp.dot(left, right, precision=highest, preferred_element_type=jnp.float32)

def rms_norm(value, gain):
    return value * lax.rsqrt(lax.optimization_barrier(jnp.mean(value * value, axis=-1, keepdims=True)) + epsilon) * gain

def rotate(value, cosine, sine):
    half = value.shape[-1] // 2
    front = value[..., :half]
    back = value[..., half:]
    return jnp.concatenate([front * cosine - back * sine, back * cosine + front * sine], axis=-1)

def slot_tables(segments):
    length = segments.shape[-1]
    index = jnp.arange(length, dtype=jnp.int32)
    starts = jnp.concatenate([jnp.ones(segments.shape[:-1] + (1,), dtype=jnp.bool_), segments[..., 1:] != segments[..., :-1]], axis=-1)
    first_index = lax.cummax(jnp.where(starts, index, 0), axis=segments.ndim - 1)
    position = (index - first_index).astype(jnp.float32)
    freq = jnp.exp(jnp.arange(ROPE // 2, dtype=jnp.float32) * (-2.0 * math.log(10000.0) / ROPE))
    angle = position[..., None] * freq
    return (jnp.cos(angle), jnp.sin(angle))

def attend(queries, keys, values, segments):
    length = segments.shape[0]
    index = jnp.arange(length, dtype=jnp.int32)
    allowed = (segments[:, None] == segments[None, :]) & (index[None, :] <= index[:, None])
    raw_scores = low_back(jnp.einsum('shd,thd->hst', queries, keys, precision=highest))
    scores = jnp.where(allowed, raw_scores * (1.0 / math.sqrt(NOPE + ROPE)), masked_score)
    row_max = lax.optimization_barrier(jnp.max(scores, axis=-1, keepdims=True))
    exp_terms = jnp.exp(scores - row_max)
    probs = exp_terms / lax.optimization_barrier(jnp.sum(exp_terms, axis=-1, keepdims=True))
    return jnp.einsum('hst,thd->shd', low(probs), values, precision=highest)

def slot_attention(parts):
    return attend(parts[0], parts[1], parts[2], parts[3])

def layer(hidden, weights, gains, cosine, sine, segments):
    query_down, query_up, latent_down, latent_up, output_weight, gate_weight, up_weight, down_weight = weights
    input_gain, query_gain, latent_gain, post_gain = gains
    count = hidden.shape[0]
    slots = count // SLOT
    normed = low(rms_norm(hidden, input_gain))
    latent_q = low_back(matmul(normed, query_down))
    latent_kv = low_back(matmul(normed, latent_down))
    query_in = low(rms_norm(latent_q, query_gain))
    kv_in = low(rms_norm(latent_kv[:, :KVRANK], latent_gain))
    query = low_back(matmul(query_in, query_up)).reshape(count, HEADS, NOPE + ROPE)
    keyval = low_back(matmul(kv_in, latent_up)).reshape(count, HEADS, NOPE + VDIM)
    queries = low(jnp.concatenate([query[..., :NOPE], rotate(query[..., NOPE:], cosine[:, None, :], sine[:, None, :])], axis=-1))
    shared = rotate(latent_kv[:, KVRANK:], cosine, sine)
    keys = low(jnp.concatenate([keyval[..., :NOPE], jnp.broadcast_to(shared[:, None, :], (count, HEADS, ROPE))], axis=-1))
    values = low(keyval[..., NOPE:])
    attended = lax.map(jax.checkpoint(slot_attention), (queries.reshape(slots, SLOT, HEADS, NOPE + ROPE), keys.reshape(slots, SLOT, HEADS, NOPE + ROPE), values.reshape(slots, SLOT, HEADS, VDIM), segments))
    attended = low(low_back(attended.reshape(count, HEADS * VDIM)))
    mixed = hidden + residual_scale * low_back(matmul(attended, output_weight))
    normed_two = low(rms_norm(mixed, post_gain))
    gate = low_back(matmul(normed_two, gate_weight))
    up = low_back(matmul(normed_two, up_weight))
    activated = low(jax.nn.silu(gate) * up)
    return mixed + residual_scale * low_back(matmul(activated, down_weight))

def reference(tokens, segment_ids, input_gain, query_gain, latent_gain, post_gain, query_down, query_up, latent_down, latent_up, output_weight, gate_weight, up_weight, down_weight, cotangent):
    cosine, sine = slot_tables(segment_ids)
    cosine = cosine.reshape(-1, ROPE // 2)
    sine = sine.reshape(-1, ROPE // 2)
    weights = tuple((w.astype(jnp.float32) for w in (query_down, query_up, latent_down, latent_up, output_weight, gate_weight, up_weight, down_weight)))
    gains = (input_gain, query_gain, latent_gain, post_gain)

    def forward(hidden, probe, layer_weights, layer_gains):
        first_weights = tuple((w[0] for w in layer_weights))
        second_weights = tuple((w[1] for w in layer_weights))
        first_gains = tuple((g[0] for g in layer_gains))
        second_gains = tuple((g[1] for g in layer_gains))
        middle = low_back(low(layer(hidden, first_weights, first_gains, cosine, sine, segment_ids)))
        final = layer(middle + probe, second_weights, second_gains, cosine, sine, segment_ids)
        return (middle, final)
    start = tokens.astype(jnp.float32)
    outputs, pullback = jax.vjp(forward, start, jnp.zeros_like(start), weights, gains)
    middle, final = outputs
    grad_start, grad_probe, grad_weights, grad_gains = pullback((jnp.zeros_like(middle), cotangent.astype(jnp.float32)))
    boundary = jnp.stack([middle, final]).astype(jnp.bfloat16)
    input_grads = jnp.stack([grad_start, grad_probe])
    return (boundary, input_grads, grad_gains[0], grad_gains[1], grad_gains[2], grad_gains[3], grad_weights[0], grad_weights[1], grad_weights[2], grad_weights[3], grad_weights[4], grad_weights[5], grad_weights[6], grad_weights[7])
```

```python
import functools
import math

import jax
import jax.numpy as jnp
from jax import lax
from jax.experimental import pallas as pl
from jax.experimental.pallas import tpu as pltpu
from jax.sharding import PartitionSpec as P

D = 2560
HEADS = 40
NOPE = 64
ROPE = 32
VDIM = 64
QRANK = 768
KVRANK = 256
SLOT = 96
LANES = 128

epsilon = 1e-05
residual_scale = 1.4 / math.sqrt(62.0)
masked_score = -1e30
score_scale = 1.0 / math.sqrt(NOPE + ROPE)
bf16 = jnp.bfloat16
f32 = jnp.float32


def norm_scale(value):
    return lax.rsqrt(jnp.mean(value * value, axis=-1, keepdims=True) + epsilon)


def norm_back(value, scale, gain, grad):
    weighted = grad * gain
    inner = jnp.mean(value * weighted, axis=-1, keepdims=True)
    grad_value = scale * weighted - value * (scale * scale * scale) * inner
    return (grad_value, jnp.sum(grad * value * scale, axis=0))


def rotate(value, cosine, sine):
    half = value.shape[-1] // 2
    front = value[..., :half]
    back = value[..., half:]
    return jnp.concatenate([front * cosine - back * sine, back * cosine + front * sine], axis=-1)


def slot_tables(segments):
    index = jnp.arange(SLOT, dtype=jnp.int32)
    first = jnp.ones(segments.shape[:1] + (1,), dtype=jnp.bool_)
    starts = jnp.concatenate([first, segments[:, 1:] != segments[:, :-1]], axis=1)
    first_index = lax.cummax(jnp.where(starts, index, 0), axis=1)
    position = (index - first_index).astype(f32)
    freq = jnp.exp(jnp.arange(ROPE // 2, dtype=f32) * (-2.0 * math.log(10000.0) / ROPE))
    angle = position[..., None] * freq
    return (jnp.cos(angle), jnp.sin(angle))


def head_tables(segments):
    cosine, sine = slot_tables(segments)
    slots = segments.shape[0]
    ones = jnp.ones((slots, SLOT, NOPE), f32)
    tail = jnp.zeros((slots, SLOT, LANES - NOPE - ROPE), f32)
    half = jnp.zeros_like(sine)
    keep = jnp.concatenate([ones, cosine, cosine, tail], axis=-1)
    left = jnp.concatenate([0.0 * ones, -sine, half, tail], axis=-1)
    right = jnp.concatenate([0.0 * ones, half, sine, tail], axis=-1)
    index = jnp.arange(SLOT, dtype=jnp.int32)
    allowed = (segments[:, :, None] == segments[:, None, :]) & (index[None, :] <= index[:, None])
    mask = jnp.where(allowed, 0.0, masked_score).astype(f32)
    flat = lambda table: table.reshape(slots * SLOT, LANES)
    return (flat(keep), flat(left), flat(right), mask)


def contract_rows(left, right):
    return lax.dot_general(left, right, (((0,), (0,)), ((), ())), preferred_element_type=f32)


def contract_cols(left, right):
    return lax.dot_general(left, right, (((1,), (1,)), ((), ())), preferred_element_type=f32)


def project(left, weight):
    return jnp.dot(left, weight, preferred_element_type=f32)


def low_lanes():
    return lax.broadcasted_iota(jnp.int32, (SLOT, LANES), 1) < NOPE


def attend_kernel(heads, q_ref, kv_ref, sh_ref, keep_ref, left_ref, right_ref, mask_ref,
                  att_ref, qo_ref, kvo_ref):
    low = low_lanes()
    shared = sh_ref[...].astype(f32)
    keep, left, right = keep_ref[...], left_ref[...], right_ref[...]
    mask = mask_ref[0]
    held = None
    for head in range(heads):
        lanes = slice(head * LANES, (head + 1) * LANES)
        q = q_ref[:, lanes]
        q = q * keep + pltpu.roll(q, LANES - 16, 1) * left + pltpu.roll(q, 16, 1) * right
        q = q.astype(bf16)
        qo_ref[:, lanes] = q
        kv = kv_ref[:, lanes]
        kvb = kv.astype(bf16)
        kvo_ref[:, lanes] = kvb
        k = jnp.where(low, kv, shared).astype(bf16)
        scores = contract_cols(q, k) * score_scale + mask
        top = jnp.max(scores, axis=-1, keepdims=True)
        terms = jnp.exp(scores - top)
        probs = terms / jnp.sum(terms, axis=-1, keepdims=True)
        out = project(probs.astype(bf16), kvb)
        if head % 2 == 0:
            held = pltpu.roll(out, NOPE, 1)
            if head == heads - 1:
                att_ref[:, head * VDIM:(head + 1) * VDIM] = held[:, :VDIM].astype(bf16)
        else:
            att_ref[:, (head - 1) * VDIM:(head + 1) * VDIM] = jnp.where(low, held, out).astype(bf16)


def attend(query, keyval, shared, tables):
    tokens = query.shape[0]
    heads = query.shape[1] // LANES
    wide = pl.BlockSpec((SLOT, heads * LANES), lambda s: (s, 0))
    one = pl.BlockSpec((SLOT, LANES), lambda s: (s, 0))
    return pl.pallas_call(
        functools.partial(attend_kernel, heads),
        grid=(tokens // SLOT,),
        in_specs=[wide, wide, one, one, one, one, pl.BlockSpec((1, SLOT, SLOT), lambda s: (s, 0, 0))],
        out_specs=[pl.BlockSpec((SLOT, heads * VDIM), lambda s: (s, 0)), wide, wide],
        out_shape=[
            jax.ShapeDtypeStruct((tokens, heads * VDIM), bf16),
            jax.ShapeDtypeStruct(query.shape, bf16),
            jax.ShapeDtypeStruct(keyval.shape, bf16),
        ],
        name="attend",
    )(query, keyval, shared, *tables)


def attend_back_kernel(heads, q_ref, kv_ref, sh_ref, keep_ref, left_ref, right_ref, mask_ref,
                       ga_ref, gq_ref, gkv_ref, gsh_ref):
    low = low_lanes()
    shared = sh_ref[...].astype(f32)
    keep, left, right = keep_ref[...], left_ref[...], right_ref[...]
    mask = mask_ref[0]
    total = jnp.zeros((SLOT, LANES), f32)
    for head in range(heads):
        lanes = slice(head * LANES, (head + 1) * LANES)
        q = q_ref[:, lanes]
        kvb = kv_ref[:, lanes]
        k = jnp.where(low, kvb.astype(f32), shared).astype(bf16)
        scores = contract_cols(q, k) * score_scale + mask
        top = jnp.max(scores, axis=-1, keepdims=True)
        terms = jnp.exp(scores - top)
        probs = terms / jnp.sum(terms, axis=-1, keepdims=True)
        if head % 2 == 0 and head == heads - 1:
            ga = ga_ref[:, head * VDIM:(head + 1) * VDIM].astype(f32)
            ga = jnp.concatenate([jnp.zeros_like(ga), ga], axis=1)
        else:
            start = (head // 2) * LANES
            ga = ga_ref[:, start:start + LANES].astype(f32)
            if head % 2 == 0:
                ga = pltpu.roll(ga, NOPE, 1)
            ga = jnp.where(low, 0.0, ga)
        ga = ga.astype(bf16)
        grad_values = contract_rows(probs.astype(bf16), ga)
        grad_probs = contract_cols(ga, kvb)
        inner = jnp.sum(probs * grad_probs, axis=-1, keepdims=True)
        grad_scores = (probs * (grad_probs - inner) * score_scale).astype(bf16)
        gq = project(grad_scores, k)
        gq = gq * keep - pltpu.roll(gq, LANES - 16, 1) * left - pltpu.roll(gq, 16, 1) * right
        gq_ref[:, lanes] = gq.astype(bf16)
        gk = contract_rows(grad_scores, q)
        total = total + gk
        gkv_ref[:, lanes] = jnp.where(low, gk, grad_values).astype(bf16)
    gsh_ref[...] = total


def attend_back(query, keyval, shared, tables, grad_attended):
    tokens = query.shape[0]
    heads = query.shape[1] // LANES
    wide = pl.BlockSpec((SLOT, heads * LANES), lambda s: (s, 0))
    one = pl.BlockSpec((SLOT, LANES), lambda s: (s, 0))
    return pl.pallas_call(
        functools.partial(attend_back_kernel, heads),
        grid=(tokens // SLOT,),
        in_specs=[wide, wide, one, one, one, one,
                  pl.BlockSpec((1, SLOT, SLOT), lambda s: (s, 0, 0)),
                  pl.BlockSpec((SLOT, heads * VDIM), lambda s: (s, 0))],
        out_specs=[wide, wide, one],
        out_shape=[
            jax.ShapeDtypeStruct(query.shape, bf16),
            jax.ShapeDtypeStruct(keyval.shape, bf16),
            jax.ShapeDtypeStruct((tokens, LANES), f32),
        ],
        name="attend_back",
    )(query, keyval, shared, *tables, grad_attended)


def gather(value):
    return lax.all_gather(value, "shard", axis=0, tiled=True)


def scatter(value):
    return lax.psum_scatter(value.astype(bf16), "shard", scatter_dimension=0, tiled=True).astype(f32)


def layer_forward(hidden, own_tables, tables, gains, weights):
    input_gain, query_gain, latent_gain, post_gain = gains
    down_both, query_up, latent_up, output_weight, gate_up, down_weight = weights
    scale_in = norm_scale(hidden)
    normed = (hidden * scale_in * input_gain).astype(bf16)
    latents = project(normed, down_both)
    latent_q = latents[:, :QRANK]
    latent = latents[:, QRANK:QRANK + KVRANK]
    scale_q = norm_scale(latent_q)
    scale_kv = norm_scale(latent)
    own_in = jnp.concatenate(
        [
            latent_q * scale_q * query_gain,
            latent * scale_kv * latent_gain,
            rotate(latents[:, QRANK + KVRANK:], *own_tables),
        ],
        axis=1,
    ).astype(bf16)
    all_in = gather(own_in)
    query_in = all_in[:, :QRANK]
    kv_in = all_in[:, QRANK:QRANK + KVRANK]
    shared = jnp.pad(all_in[:, QRANK + KVRANK:], ((0, 0), (NOPE, LANES - NOPE - ROPE)))
    attended, queries, keyval = attend(
        project(query_in, query_up), project(kv_in, latent_up), shared, tables
    )
    mixed = hidden + residual_scale * scatter(project(attended, output_weight))
    scale_post = norm_scale(mixed)
    own_two = (mixed * scale_post * post_gain).astype(bf16)
    normed_two = gather(own_two)
    both = project(normed_two, gate_up)
    width = both.shape[1] // 2
    gate, up = both[:, :width], both[:, width:]
    activated = (jax.nn.silu(gate) * up).astype(bf16)
    output = mixed + residual_scale * scatter(project(activated, down_weight))
    kept = (hidden, scale_in, normed, latent_q, scale_q, latent, scale_kv, query_in, kv_in,
            shared, queries, keyval, attended, mixed, scale_post, own_two, gate, up)
    return (output, kept)


def gate_backward(grad_act, gate, up):
    sigmoid = jax.nn.sigmoid(gate)
    grad_gate = (grad_act * up * sigmoid * (1.0 + gate * (1.0 - sigmoid))).astype(bf16)
    grad_up = (grad_act * gate * sigmoid).astype(bf16)
    return jnp.concatenate([grad_gate, grad_up], axis=1)


def layer_backward(grad_out, kept, own_tables, tables, gains, weights):
    (hidden, scale_in, normed, latent_q, scale_q, latent, scale_kv, query_in, kv_in,
     shared, queries, keyval, attended, mixed, scale_post, own_two, gate, up) = kept
    input_gain, query_gain, latent_gain, post_gain = gains
    down_both, query_up, latent_up, output_weight, gate_up, down_weight = weights
    cosine, sine = own_tables
    own_down = (residual_scale * grad_out).astype(bf16)
    grad_down = gather(own_down)
    grad_both = gate_backward(contract_cols(grad_down, down_weight), gate, up)
    grad_normed_two = scatter(contract_cols(grad_both, gate_up))
    grad_mixed_norm, dgain_post = norm_back(mixed, scale_post, post_gain, grad_normed_two)
    grad_mixed = grad_out + grad_mixed_norm
    grad_branch = gather((residual_scale * grad_mixed).astype(bf16))
    grad_attended = contract_cols(grad_branch, output_weight).astype(bf16)
    grad_query, grad_keyval, grad_shared = attend_back(queries, keyval, shared, tables, grad_attended)
    grad_in = scatter(
        jnp.concatenate(
            [
                contract_cols(grad_query, query_up),
                contract_cols(grad_keyval, latent_up),
                grad_shared[:, NOPE:NOPE + ROPE],
            ],
            axis=1,
        )
    )
    grad_latent_q, dgain_query = norm_back(latent_q, scale_q, query_gain, grad_in[:, :QRANK])
    grad_latent, dgain_latent = norm_back(
        latent, scale_kv, latent_gain, grad_in[:, QRANK:QRANK + KVRANK]
    )
    grad_lat = jnp.concatenate(
        [grad_latent_q, grad_latent, rotate(grad_in[:, QRANK + KVRANK:], cosine, -sine)], axis=1
    ).astype(bf16)
    grad_normed = contract_cols(grad_lat, down_both)
    grad_hidden_norm, dgain_input = norm_back(hidden, scale_in, input_gain, grad_normed)
    grad_hidden = grad_mixed + grad_hidden_norm
    found = (own_down, grad_branch, grad_query, grad_keyval, grad_lat)
    return (grad_hidden, found, (dgain_input, dgain_query, dgain_latent, dgain_post))


def spread(weight, count):
    rows, columns = weight.shape
    parts = weight.reshape(rows, count, columns // count).transpose(1, 0, 2)
    return lax.all_to_all(parts, "shard", 0, 0, tiled=True).reshape(rows * count, columns // count)


def collect(grad, count):
    rows, columns = grad.shape
    parts = lax.all_to_all(
        grad.reshape(count, rows // count, columns), "shard", 0, 0, tiled=True
    )
    return parts.transpose(1, 0, 2).reshape(rows // count, columns * count)


def pad_heads(weight):
    rows, columns = weight.shape
    heads = weight.reshape(rows, columns // (NOPE + ROPE), NOPE + ROPE)
    return jnp.pad(heads, ((0, 0), (0, 0), (0, LANES - NOPE - ROPE))).reshape(rows, -1)


def cut_heads(grad):
    rows, columns = grad.shape
    heads = grad.reshape(rows, columns // LANES, LANES)[:, :, :NOPE + ROPE]
    return heads.reshape(rows, -1)


def body(tokens, segment_ids, input_gain, query_gain, latent_gain, post_gain, query_down, query_up,
         latent_down, latent_up, output_weight, gate_weight, up_weight, down_weight, cotangent):
    at_start = lax.axis_index("section") == 0
    sections = lax.axis_size("section")
    count = lax.axis_size("shard")
    gains = (input_gain[0], query_gain[0], latent_gain[0], post_gain[0])
    down_both = gather(jnp.concatenate([query_down[0], latent_down[0]], axis=1))
    query_up_all = pad_heads(spread(query_up[0], count))
    latent_up_all = spread(latent_up[0], count)
    gate_up = jnp.concatenate([spread(gate_weight[0], count), spread(up_weight[0], count)], axis=1)
    weights = (down_both, query_up_all, latent_up_all, output_weight[0], gate_up, down_weight[0])
    own_tables = tuple(t.reshape(-1, ROPE // 2) for t in slot_tables(segment_ids))
    tables = head_tables(gather(segment_ids))

    start = tokens.astype(f32)
    onward = [(source, source + 1) for source in range(sections - 1)]
    back = [(source + 1, source) for source in range(sections - 1)]
    leaving, _ = layer_forward(start, own_tables, tables, gains, weights)
    received = lax.ppermute(leaving.astype(bf16), "section", onward)
    entering = jnp.where(at_start, start, received.astype(f32))
    leaving, kept = layer_forward(entering, own_tables, tables, gains, weights)
    boundary = leaving.astype(bf16)

    last = cotangent.astype(f32)
    grad, _, _ = layer_backward(last, kept, own_tables, tables, gains, weights)
    returned = lax.ppermute(grad.astype(bf16), "section", back)
    incoming = jnp.where(at_start, returned.astype(f32), last)
    grad, found, gain_terms = layer_backward(incoming, kept, own_tables, tables, gains, weights)

    (hidden, scale_in, normed, latent_q, scale_q, latent, scale_kv, query_in, kv_in,
     shared, queries, keyval, attended, mixed, scale_post, own_two, gate, up) = kept
    own_down, grad_branch, grad_query, grad_keyval, grad_lat = found

    two_all = lax.all_gather(own_two, ("rep", "shard"), axis=0, tiled=True)
    down_all = lax.all_gather(own_down, ("rep", "shard"), axis=0, tiled=True)
    both = project(two_all, gate_up)
    width = both.shape[1] // 2
    gate_all, up_all = both[:, :width], both[:, width:]
    activated_all = (jax.nn.silu(gate_all) * up_all).astype(bf16)
    grad_both = gate_backward(contract_cols(down_all, down_weight[0]), gate_all, up_all)
    total_gate = collect(contract_rows(two_all, grad_both[:, :width]).astype(bf16), count)
    total_up = collect(contract_rows(two_all, grad_both[:, width:]).astype(bf16), count)
    total_down = contract_rows(activated_all, down_all)

    normed_rows = lax.all_to_all(
        normed.reshape(normed.shape[0], count, -1).transpose(1, 0, 2), "shard", 0, 0, tiled=True
    ).reshape(normed.shape[0] * count, -1)
    part_down = contract_rows(normed_rows, gather(grad_lat)).astype(bf16)
    part_query = collect(cut_heads(contract_rows(query_in, grad_query).astype(bf16)), count)
    part_latent = collect(contract_rows(kv_in, grad_keyval).astype(bf16), count)
    part_output = contract_rows(attended, grad_branch).astype(bf16)
    total_down_both, total_query, total_latent, total_output = (
        part.astype(f32) for part in lax.psum((part_down, part_query, part_latent, part_output), "rep")
    )
    gain_totals = lax.psum(gain_terms, ("rep", "shard"))
    return (
        boundary[None],
        grad[None],
        gain_totals[0][None],
        gain_totals[1][None],
        gain_totals[2][None],
        gain_totals[3][None],
        total_down_both[None, :, :QRANK],
        total_query[None],
        total_down_both[None, :, QRANK:],
        total_latent[None],
        total_output[None],
        total_gate.astype(f32)[None],
        total_up.astype(f32)[None],
        total_down[None],
    )


def solution(mesh):
    tokens = P(("rep", "shard"), None)
    gain = P("section", None)
    weight = P("section", "shard", None)
    out = P("section", ("rep", "shard"), None)
    return jax.shard_map(
        body,
        mesh=mesh,
        in_specs=(tokens, tokens) + (gain,) * 4 + (weight,) * 8 + (tokens,),
        out_specs=(out, out) + (gain,) * 4 + (weight,) * 8,
        check_vma=False,
    )
```

```python
import functools
import math

import jax
import jax.numpy as jnp
from jax import lax
from jax.experimental import pallas as pl
from jax.experimental.pallas import tpu as pltpu
from jax.sharding import PartitionSpec as P

D = 2560
HEADS = 40
NOPE = 64
ROPE = 32
VDIM = 64
QRANK = 768
KVRANK = 256
FF = 6400
SLOT = 96
LANES = 128

epsilon = 1e-05
residual_scale = 1.4 / math.sqrt(62.0)
masked_score = -1e30
score_scale = 1.0 / math.sqrt(NOPE + ROPE)
bf16 = jnp.bfloat16
f32 = jnp.float32


def norm_scale(value):
    return lax.rsqrt(jnp.mean(value * value, axis=-1, keepdims=True) + epsilon)


def norm_back(value, scale, gain, grad):
    weighted = grad * gain
    inner = jnp.mean(value * weighted, axis=-1, keepdims=True)
    grad_value = scale * weighted - value * (scale * scale * scale) * inner
    return (grad_value, jnp.sum(grad * value * scale, axis=0))


def rotate(value, cosine, sine):
    half = value.shape[-1] // 2
    front = value[..., :half]
    back = value[..., half:]
    return jnp.concatenate([front * cosine - back * sine, back * cosine + front * sine], axis=-1)


def slot_tables(segments):
    index = jnp.arange(SLOT, dtype=jnp.int32)
    first_index = jnp.sum((segments[:, None, :] < segments[:, :, None]).astype(jnp.int32), axis=-1)
    position = (index - first_index).astype(f32)
    freq = jnp.exp(jnp.arange(ROPE // 2, dtype=f32) * (-2.0 * math.log(10000.0) / ROPE))
    angle = position[..., None] * freq
    return (jnp.cos(angle), jnp.sin(angle))


def head_tables(segments):
    cosine, sine = slot_tables(segments)
    slots = segments.shape[0]
    ones = jnp.ones((slots, SLOT, NOPE), f32)
    tail = jnp.zeros((slots, SLOT, LANES - NOPE - ROPE), f32)
    half = jnp.zeros_like(sine)
    keep = jnp.concatenate([ones, cosine, cosine, tail], axis=-1)
    left = jnp.concatenate([0.0 * ones, -sine, half, tail], axis=-1)
    right = jnp.concatenate([0.0 * ones, half, sine, tail], axis=-1)
    index = jnp.arange(SLOT, dtype=jnp.int32)
    allowed = (segments[:, :, None] == segments[:, None, :]) & (index[None, :] <= index[:, None])
    mask = jnp.where(allowed, 0.0, masked_score).astype(f32)
    flat = lambda table: table.reshape(slots * SLOT, LANES)
    return (flat(keep), flat(left), flat(right), mask, mask.transpose(0, 2, 1))


def contract_rows(left, right):
    return lax.dot_general(left, right, (((0,), (0,)), ((), ())), preferred_element_type=f32)


def contract_cols(left, right):
    return lax.dot_general(left, right, (((1,), (1,)), ((), ())), preferred_element_type=f32)


def project(left, weight):
    return jnp.dot(left, weight, preferred_element_type=f32)


def low_lanes():
    return lax.broadcasted_iota(jnp.int32, (SLOT, LANES), 1) < NOPE


HEAD_GROUP = 5
HEAD_ROWS = 16


def attend_kernel(heads, q_ref, kv_ref, sh_ref, keep_ref, left_ref, right_ref, mask_ref,
                  att_ref, qo_ref, kvo_ref, log_ref):
    low = low_lanes()
    lane = lax.broadcasted_iota(jnp.int32, (SLOT, LANES), 1)
    shared = sh_ref[...].astype(f32)
    keep, left, right = keep_ref[...], left_ref[...], right_ref[...]
    mask = mask_ref[0]
    tallest = jnp.zeros((SLOT, LANES), f32)
    sums = jnp.ones((SLOT, LANES), f32)
    for first in range(0, heads, HEAD_GROUP):
        group = range(first, min(first + HEAD_GROUP, heads))
        scores, values = [], []
        for head in group:
            lanes = slice(head * LANES, (head + 1) * LANES)
            q = q_ref[:, lanes]
            q = q * keep + pltpu.roll(q, LANES - 16, 1) * left + pltpu.roll(q, 16, 1) * right
            q = q.astype(bf16)
            qo_ref[:, lanes] = q
            kv = kv_ref[:, lanes]
            kvo_ref[:, lanes] = kv.astype(bf16)
            k = jnp.where(low, kv, shared).astype(bf16)
            values.append(jnp.where(low, 1.0, kv).astype(bf16))
            scores.append(contract_cols(q, k) * score_scale + mask)
        tops = [jnp.max(score, axis=-1, keepdims=True) for score in scores]
        terms = [jnp.exp(score - top).astype(bf16) for score, top in zip(scores, tops)]
        outs = [project(term, value) for term, value in zip(terms, values)]
        for head, top, out in zip(group, tops, outs):
            turned = pltpu.roll(out, NOPE, 1)
            tallest = jnp.where(lane == head, top, tallest)
            sums = jnp.where(lane == head, out, sums)
            pair = (head // 2) * LANES
            if head % 2 == 0:
                att = turned / out
                att_ref[:, pair:pair + VDIM] = att[:, :VDIM].astype(bf16)
            else:
                att = out / turned
                att_ref[:, pair + VDIM:pair + LANES] = att[:, VDIM:].astype(bf16)
    log_ref[0] = (tallest + jnp.log(sums)).T[:HEAD_ROWS, :]


def attention_cost(tokens, heads, passes):
    return pl.CostEstimate(
        flops=passes * tokens * heads * SLOT * LANES * 20, bytes_accessed=tokens * heads * LANES * 12,
        transcendentals=tokens * heads * SLOT,
    )


def attend(query, keyval, shared, tables):
    tokens = query.shape[0]
    heads = query.shape[1] // LANES
    wide = pl.BlockSpec((SLOT, heads * LANES), lambda s: (s, 0))
    one = pl.BlockSpec((SLOT, LANES), lambda s: (s, 0))
    square = pl.BlockSpec((1, SLOT, SLOT), lambda s: (s, 0, 0))
    return pl.pallas_call(
        functools.partial(attend_kernel, heads),
        grid=(tokens // SLOT,),
        in_specs=[wide, wide, one, one, one, one, square],
        out_specs=[pl.BlockSpec((SLOT, heads * VDIM), lambda s: (s, 0)), wide, wide,
                   pl.BlockSpec((1, HEAD_ROWS, SLOT), lambda s: (s, 0, 0))],
        out_shape=[
            jax.ShapeDtypeStruct((tokens, heads * VDIM), bf16),
            jax.ShapeDtypeStruct(query.shape, bf16),
            jax.ShapeDtypeStruct(keyval.shape, bf16),
            jax.ShapeDtypeStruct((tokens // SLOT, HEAD_ROWS, SLOT), f32),
        ],
        cost_estimate=attention_cost(tokens, heads, 4),
        name="attend",
    )(query, keyval, shared, *tables[:4])


def attend_back_kernel(heads, q_ref, kv_ref, sh_ref, keep_ref, left_ref, right_ref, mask_ref,
                       ga_ref, att_ref, log_ref, gq_ref, gkv_ref, gsh_ref):
    low = low_lanes()
    shared = sh_ref[...].astype(f32)
    keep, left, right = keep_ref[...], left_ref[...], right_ref[...]
    mask = mask_ref[0]
    total = jnp.zeros((SLOT, LANES), f32)
    product = ga_ref[...].astype(f32) * att_ref[...].astype(f32)
    high = product.astype(bf16)
    rest = (product - high.astype(f32)).astype(bf16)
    shape = (HEAD_ROWS, product.shape[1])
    chosen = lax.broadcasted_iota(jnp.int32, shape, 1) // VDIM == lax.broadcasted_iota(jnp.int32, shape, 0)
    chosen = jnp.where(chosen, 1.0, 0.0).astype(bf16)
    inner = contract_cols(chosen, high) + contract_cols(chosen, rest)
    for first in range(0, heads, HEAD_GROUP):
        group = range(first, min(first + HEAD_GROUP, heads))
        queries, keys, grads, scores, grad_probs = [], [], [], [], []
        for head in group:
            lanes = slice(head * LANES, (head + 1) * LANES)
            q = q_ref[:, lanes]
            kvb = kv_ref[:, lanes]
            k = jnp.where(low, kvb.astype(f32), shared).astype(bf16)
            if head % 2 == 0 and head == heads - 1:
                ga = ga_ref[:, head * VDIM:(head + 1) * VDIM].astype(f32)
                ga = jnp.concatenate([jnp.zeros_like(ga), ga], axis=1)
            else:
                start = (head // 2) * LANES
                ga = ga_ref[:, start:start + LANES].astype(f32)
                if head % 2 == 0:
                    ga = pltpu.roll(ga, NOPE, 1)
                ga = jnp.where(low, 0.0, ga)
            ga = ga.astype(bf16)
            queries.append(q)
            keys.append(k)
            grads.append(ga)
            scores.append(contract_cols(k, q) * score_scale + mask)
            grad_probs.append(contract_cols(kvb, ga))
        probs = [jnp.exp(score - log_ref[0, head:head + 1, :]) for head, score in zip(group, scores)]
        changes = [
            (prob * (grad - inner[head:head + 1, :]) * score_scale).astype(bf16)
            for head, prob, grad in zip(group, probs, grad_probs)
        ]
        grad_values = [project(prob.astype(bf16), ga) for prob, ga in zip(probs, grads)]
        grad_keys = [project(change, q) for change, q in zip(changes, queries)]
        grad_queries = [contract_rows(change, k) for change, k in zip(changes, keys)]
        for head, gv, gk, gq in zip(group, grad_values, grad_keys, grad_queries):
            lanes = slice(head * LANES, (head + 1) * LANES)
            gq = gq * keep - pltpu.roll(gq, LANES - 16, 1) * left - pltpu.roll(gq, 16, 1) * right
            gq_ref[:, lanes] = gq.astype(bf16)
            total = total + gk
            gkv_ref[:, lanes] = jnp.where(low, gk, gv).astype(bf16)
    gsh_ref[...] = total


def attend_back(query, keyval, shared, tables, grad_attended, attended, logs):
    tokens = query.shape[0]
    heads = query.shape[1] // LANES
    wide = pl.BlockSpec((SLOT, heads * LANES), lambda s: (s, 0))
    one = pl.BlockSpec((SLOT, LANES), lambda s: (s, 0))
    half = pl.BlockSpec((SLOT, heads * VDIM), lambda s: (s, 0))
    return pl.pallas_call(
        functools.partial(attend_back_kernel, heads),
        grid=(tokens // SLOT,),
        in_specs=[wide, wide, one, one, one, one, pl.BlockSpec((1, SLOT, SLOT), lambda s: (s, 0, 0)),
                  half, half, pl.BlockSpec((1, HEAD_ROWS, SLOT), lambda s: (s, 0, 0))],
        out_specs=[wide, wide, one],
        out_shape=[
            jax.ShapeDtypeStruct(query.shape, bf16),
            jax.ShapeDtypeStruct(keyval.shape, bf16),
            jax.ShapeDtypeStruct((tokens, LANES), f32),
        ],
        cost_estimate=attention_cost(tokens, heads, 10),
        name="attend_back",
    )(query, keyval, shared, *tables[:3], tables[4], grad_attended, attended, logs)


MESH = pl.DeviceIdType.MESH
VMEM_LIMIT = 60 * 1024 * 1024


def partners():
    me = lax.axis_index("shard")
    core = me % 2
    return me, core, me + 1 - 2 * core, (me + 2) % 4


def greet(devices):
    barrier = pltpu.get_barrier_semaphore()
    for device in devices:
        pl.semaphore_signal(barrier, inc=1, device_id=device, device_id_type=MESH)
    pl.semaphore_wait(barrier, len(devices))


def columns(step, width):
    return pl.ds(pl.multiple_of(step * width, LANES), width)


def rows_at(start, rows):
    return pl.ds(pl.multiple_of(start * rows, 16), rows)


def remote(source, target, sems, step, device):
    return pltpu.make_async_remote_copy(
        src_ref=source, dst_ref=target, send_sem=sems.at[0, step], recv_sem=sems.at[1, step],
        device_id={"shard": device}, device_id_type=MESH,
    )


def exchange_scratch(rows, steps, width):
    part = pltpu.VMEM((steps, rows, width), bf16)
    return [part] * 6 + [
        pltpu.VMEM((steps, rows, width), f32),
        pltpu.VMEM((2 * rows, width), f32),
        pltpu.SemaphoreType.DMA((3, 2, steps)),
    ]


def each(steps, unrolled, do):
    if unrolled:
        for step in range(steps):
            do(step)
    else:
        def again(step, carry):
            do(step)
            return carry
        lax.fori_loop(0, steps, again, 0)


def sum_scatter(rows, steps, unrolled, partial, scratch, use):
    (to_sib, from_sib, to_far, from_far, own_sib, own_from, hold, stage, sems) = scratch
    me, core, sib, far = partners()
    mine = rows_at(core, rows)
    other = rows_at(1 - core, rows)

    def first(step):
        return remote(to_sib.at[step], from_sib.at[step], sems.at[0], step, sib)

    def across(step):
        return remote(to_far.at[step], from_far.at[step], sems.at[1], step, far)

    def beside(step):
        return remote(own_sib.at[step], own_from.at[step], sems.at[2], step, sib)

    def far_part(step):
        stage[...] = partial(rows_at(far // 2, 2 * rows), step)
        to_sib[step] = stage[other, :].astype(bf16)
        first(step).start()
        hold[step] = stage[mine, :]

    def far_send(step):
        first(step).wait_recv()
        to_far[step] = (hold[step] + from_sib[step].astype(f32)).astype(bf16)
        across(step).start()

    def far_step(step):
        far_part(step)
        if unrolled:
            if step > 0:
                far_send(step - 1)
        else:
            @pl.when(step > 0)
            def _():
                far_send(step - 1)

    each(steps, unrolled, far_step)
    far_send(steps - 1)

    def near_part(step):
        stage[...] = partial(rows_at(me // 2, 2 * rows), step)
        own_sib[step] = stage[other, :].astype(bf16)
        beside(step).start()
        hold[step] = stage[mine, :]

    each(steps, unrolled, near_part)

    def finish(step):
        beside(step).wait_recv()
        across(step).wait_recv()
        use(step, hold[step] + own_from[step].astype(f32) + from_far[step].astype(f32))

    each(steps, unrolled, finish)

    def settle(step):
        first(step).wait_send()
        across(step).wait_send()
        beside(step).wait_send()

    each(steps, unrolled, settle)


def spread_rows(rows, steps, width, place, all_ref, sems):
    me, core, sib, far = partners()

    def part(owner, step):
        return all_ref.at[rows_at(owner, rows), columns(step, width)]

    def across(step):
        return remote(part(me, step), part(me, step), sems.at[0], step, far)

    def beside(step):
        return remote(part(me, step), part(me, step), sems.at[1], step, sib)

    def onward(step):
        return remote(part(far, step), part(far, step), sems.at[2], step, sib)

    def send(step):
        place(step)
        across(step).start()
        beside(step).start()

    each(steps, False, send)

    def forward(step):
        across(step).wait_recv()
        onward(step).start()

    each(steps, False, forward)

    def settle(step):
        beside(step).wait_recv()
        onward(step).wait_recv()
        across(step).wait_send()
        beside(step).wait_send()
        onward(step).wait_send()

    each(steps, False, settle)


def vmem(count):
    return [pl.BlockSpec(memory_space=pltpu.VMEM)] * count


def comm_call(kernel, name, number, inputs, out_shape, scratch, flops=0):
    nbytes = sum(v.size * v.dtype.itemsize for v in (*inputs, *out_shape))
    return pl.pallas_call(
        kernel,
        in_specs=vmem(len(inputs)),
        out_specs=vmem(len(out_shape)),
        out_shape=out_shape,
        scratch_shapes=scratch,
        compiler_params=pltpu.CompilerParams(
            collective_id=number, has_side_effects=True, vmem_limit_bytes=VMEM_LIMIT
        ),
        cost_estimate=pl.CostEstimate(flops=flops, bytes_accessed=nbytes, transcendentals=0),
        name=name,
    )(*inputs)


def shape(rows, width, dtype):
    return jax.ShapeDtypeStruct((rows, width), dtype)


def gather_kernel(steps, width, own_ref, all_ref, sems):
    rows = own_ref.shape[0]
    me, core, sib, far = partners()
    greet([{"shard": sib}, {"shard": far}])

    def place(step):
        all_ref[rows_at(me, rows), columns(step, width)] = own_ref[:, columns(step, width)]

    spread_rows(rows, steps, width, place, all_ref, sems)


def gather(value, number, width):
    if lax.axis_size("shard") != 4:
        return lax.all_gather(value, "shard", axis=0, tiled=True)
    rows, total = value.shape
    steps = total // width
    (out,) = comm_call(
        functools.partial(gather_kernel, steps, width), "gather_rows", number, [value],
        [shape(4 * rows, total, bf16)], [pltpu.SemaphoreType.DMA((3, 2, steps))],
    )
    return out


def plain_gather(value):
    return lax.all_gather(value, "shard", axis=0, tiled=True)


def plain_scatter(value):
    return lax.psum_scatter(value.astype(bf16), "shard", scatter_dimension=0, tiled=True).astype(f32)


MODEL_STEP = 512


def output_kernel(att_ref, weight_ref, hidden_ref, gain_ref, mixed_ref, two_ref, *scratch):
    *parts, sems = scratch
    rows = hidden_ref.shape[0]
    width = MODEL_STEP
    steps = D // width
    me, core, sib, far = partners()
    greet([{"shard": sib}, {"shard": far}])

    def partial(where, step):
        return project(att_ref[where, :], weight_ref[:, columns(step, width)])

    def use(step, total):
        lanes = columns(step, width)
        mixed_ref[:, lanes] = hidden_ref[:, lanes] + residual_scale * total

    sum_scatter(rows, steps, False, partial, parts, use)
    mixed = mixed_ref[...]
    scale = norm_scale(mixed)

    def place(step):
        lanes = columns(step, width)
        two_ref[rows_at(me, rows), lanes] = (mixed_ref[:, lanes] * scale * gain_ref[:, lanes]).astype(bf16)

    spread_rows(rows, steps, width, place, two_ref, sems)


def output_norm(attended, weight, hidden, gain):
    if lax.axis_size("shard") != 4:
        mixed = hidden + residual_scale * plain_scatter(project(attended, weight))
        return mixed, plain_gather((mixed * norm_scale(mixed) * gain).astype(bf16))
    rows = hidden.shape[0]
    steps = D // MODEL_STEP
    return comm_call(
        output_kernel, "output_norm", 2, [attended, weight, hidden, gain[None]],
        [shape(rows, D, f32), shape(4 * rows, D, bf16)],
        exchange_scratch(rows, steps, MODEL_STEP) + [pltpu.SemaphoreType.DMA((3, 2, steps))],
        flops=2 * attended.size * D,
    )


def down_kernel(passing, act_ref, weight_ref, mixed_ref, out_ref, low_ref, *scratch):
    rows = mixed_ref.shape[0]
    width = MODEL_STEP
    steps = D // width
    me, core, sib, far = partners()
    devices = [{"shard": sib}, {"shard": far}]
    if passing:
        got_ref, *parts, sems = scratch
        section = lax.axis_index("section")
        devices.append({"section": 1 - section})
    else:
        parts = scratch
    greet(devices)

    def onward(step):
        lanes = columns(step, width)
        return pltpu.make_async_remote_copy(
            src_ref=low_ref.at[:, lanes], dst_ref=got_ref.at[:, lanes], send_sem=sems.at[0, step],
            recv_sem=sems.at[1, step], device_id={"section": 1 - section}, device_id_type=MESH,
        )

    def partial(where, step):
        return project(act_ref[where, :], weight_ref[:, columns(step, width)])

    def use(step, total):
        lanes = columns(step, width)
        out = mixed_ref[:, lanes] + residual_scale * total
        out_ref[:, lanes] = out
        low_ref[:, lanes] = out.astype(bf16)
        if passing:
            onward(step).start()

    sum_scatter(rows, steps, False, partial, parts, use)
    if passing:
        each(steps, False, lambda step: onward(step).wait())


def down_project(activated, weight, mixed, passing):
    if lax.axis_size("shard") != 4:
        output = mixed + residual_scale * plain_scatter(project(activated, weight))
        low = output.astype(bf16)
        return (output, low) + ((lax.ppermute(low, "section", [(0, 1)]),) if passing else ())
    rows = mixed.shape[0]
    steps = D // MODEL_STEP
    scratch = exchange_scratch(rows, steps, MODEL_STEP)
    return comm_call(
        functools.partial(down_kernel, passing), "down_project", 3 if passing else 4,
        [activated, weight, mixed],
        [shape(rows, D, f32)] + [shape(rows, D, bf16)] * (2 if passing else 1),
        scratch + ([pltpu.SemaphoreType.DMA((2, steps))] if passing else []),
        flops=2 * activated.size * D,
    )


def mlp_back_kernel(both_ref, weight_ref, mixed_ref, grad_ref, gain_ref, out_ref, dgain_ref, branch_ref,
                    *scratch):
    *parts, sems = scratch
    rows = mixed_ref.shape[0]
    width = MODEL_STEP
    steps = D // width
    me, core, sib, far = partners()
    greet([{"shard": sib}, {"shard": far}])

    def partial(where, step):
        return contract_cols(both_ref[where, :], weight_ref[columns(step, width), :])

    def use(step, total):
        out_ref[:, columns(step, width)] = total

    sum_scatter(rows, steps, False, partial, parts, use)
    mixed = mixed_ref[...]
    scale = norm_scale(mixed)
    inner = jnp.mean(mixed * out_ref[...] * gain_ref[...], axis=-1, keepdims=True)
    slope = scale * scale * scale * inner

    def place(step):
        lanes = columns(step, width)
        grad, value = out_ref[:, lanes], mixed_ref[:, lanes]
        dgain_ref[:, lanes] = jnp.sum(grad * value * scale, axis=0, keepdims=True)
        total = grad_ref[:, lanes] + scale * (grad * gain_ref[:, lanes]) - value * slope
        out_ref[:, lanes] = total
        branch_ref[rows_at(me, rows), lanes] = (residual_scale * total).astype(bf16)

    spread_rows(rows, steps, width, place, branch_ref, sems)


def mlp_back(grad_both, gate_up, mixed, grad_out, gain):
    if lax.axis_size("shard") != 4:
        grad = plain_scatter(contract_cols(grad_both, gate_up))
        back, dgain = norm_back(mixed, norm_scale(mixed), gain, grad)
        grad_mixed = grad_out + back
        return grad_mixed, dgain[None], plain_gather((residual_scale * grad_mixed).astype(bf16))
    rows = mixed.shape[0]
    steps = D // MODEL_STEP
    return comm_call(
        mlp_back_kernel, "mlp_back", 5, [grad_both, gate_up, mixed, grad_out, gain[None]],
        [shape(rows, D, f32), shape(1, D, f32), shape(4 * rows, D, bf16)],
        exchange_scratch(rows, steps, MODEL_STEP) + [pltpu.SemaphoreType.DMA((3, 2, steps))],
        flops=2 * grad_both.size * D,
    )


LATENT_STEP = 256


def latent_back_kernel(gq_ref, gkv_ref, gsh_ref, qup_ref, lup_ref, out_ref, *scratch):
    rows = out_ref.shape[0]
    width = LATENT_STEP
    me, core, sib, far = partners()
    greet([{"shard": sib}, {"shard": far}])

    def partial(where, step):
        if step < QRANK // width:
            return contract_cols(gq_ref[where, :], qup_ref[step * width:(step + 1) * width, :])
        if step == QRANK // width:
            return contract_cols(gkv_ref[where, :], lup_ref[...])
        shared = gsh_ref[where, :]
        return jnp.concatenate([shared, jnp.zeros_like(shared)], axis=1)

    def use(step, total):
        out_ref[:, step * width:(step + 1) * width] = total

    sum_scatter(rows, out_ref.shape[1] // width, True, partial, scratch, use)


def latent_back(grad_query, grad_keyval, grad_shared, query_up, latent_up):
    if lax.axis_size("shard") != 4:
        return plain_scatter(
            jnp.concatenate(
                [contract_cols(grad_query, query_up), contract_cols(grad_keyval, latent_up), grad_shared],
                axis=1,
            )
        )
    rows = grad_query.shape[0] // 4
    steps = QRANK // LATENT_STEP + 2
    (out,) = comm_call(
        latent_back_kernel, "latent_back", 6, [grad_query, grad_keyval, grad_shared, query_up, latent_up],
        [shape(rows, steps * LATENT_STEP, f32)], exchange_scratch(rows, steps, LATENT_STEP),
        flops=2 * grad_query.size * QRANK + 2 * grad_keyval.size * KVRANK,
    )
    return out


def any_space(count):
    return [pl.BlockSpec(memory_space=pl.ANY)] * count


def pair(value, index):
    return value.at[0, index], value.at[1, index]


def send_to(source, target, sems, index, device):
    send, receive = pair(sems, index)
    return pltpu.make_async_remote_copy(
        src_ref=source, dst_ref=target, send_sem=send, recv_sem=receive,
        device_id={"shard": device}, device_id_type=MESH,
    )


def move_kernel(whole, split, *refs):
    amount = whole + len(split)
    inputs, outputs, (sems, local) = refs[:amount], refs[amount:2 * amount], refs[2 * amount:]
    me, core, sib, far = partners()
    diagonal = far + 1 - 2 * core
    greet([{"shard": sib}, {"shard": far}, {"shard": diagonal}])
    waits, forwards, keeps = [], [], []
    number = 0
    for i, (source, target) in enumerate(zip(inputs, outputs)):
        if i < whole:
            to_far = send_to(source, target.at[me], sems, number, far)
            to_sib = send_to(source, target.at[me], sems, number + 1, sib)
            onward = send_to(target.at[far], target.at[far], sems, number + 2, sib)
            to_far.start()
            to_sib.start()
            forwards.append((to_far, onward))
            waits.append(to_sib)
            kept = source
        else:
            part = split[i - whole]
            for j, device in enumerate((far, diagonal, sib)):
                copy = send_to(part(source, device), target.at[me], sems, number + j, device)
                copy.start()
                waits.append(copy)
            kept = part(source, me)
        number += 3
        keep = pltpu.make_async_copy(kept, target.at[me], local.at[i])
        keep.start()
        keeps.append(keep)
    for to_far, onward in forwards:
        to_far.wait_recv()
        onward.start()
    for to_far, onward in forwards:
        to_far.wait_send()
        onward.wait()
    for copy in waits:
        copy.wait()
    for keep in keeps:
        keep.wait()


def move(name, number, wholes, splits):
    inputs = list(wholes) + [array for array, _, _ in splits]
    shapes = [w.shape for w in wholes] + [part for _, part, _ in splits]
    out_shape = [jax.ShapeDtypeStruct((4,) + tuple(sh), v.dtype) for sh, v in zip(shapes, inputs)]
    return pl.pallas_call(
        functools.partial(move_kernel, len(wholes), [f for _, _, f in splits]),
        in_specs=any_space(len(inputs)),
        out_specs=any_space(len(inputs)),
        out_shape=out_shape,
        scratch_shapes=[pltpu.SemaphoreType.DMA((2, 3 * len(inputs))), pltpu.SemaphoreType.DMA((len(inputs),))],
        compiler_params=pltpu.CompilerParams(collective_id=number, has_side_effects=True),
        cost_estimate=pl.CostEstimate(
            flops=0, bytes_accessed=sum(4 * v.size * v.dtype.itemsize for v in inputs), transcendentals=0
        ),
        name=name,
    )(*inputs)


QUERY_WINDOW = 1024


def query_window(ref, owner):
    return ref.at[:, pl.ds(pl.multiple_of(owner // 2 * 1920 + owner % 2 * 896, LANES), QUERY_WINDOW)]


def latent_window(ref, owner):
    return ref.at[:, pl.ds(pl.multiple_of(owner * 1280, LANES), 1280)]


def first_move(query_down, latent_down, query_up, latent_up, segments, count):
    if count != 4:
        return (
            plain_gather(query_down), plain_gather(latent_down), pad_heads(spread(query_up, count)),
            spread(latent_up, count), plain_gather(segments),
        )
    down_q, down_kv, groups, up_q, up_kv = move(
        "first_move", 7, [query_down, latent_down, segments],
        [(query_up, (query_up.shape[0], QUERY_WINDOW), query_window),
         (latent_up, (latent_up.shape[0], 1280), latent_window)],
    )
    merge = lambda value: value.reshape((-1,) + value.shape[2:])
    up_q = lax.dynamic_slice_in_dim(merge(up_q), lax.axis_index("shard") % 2 * 64, 960, 1)
    return merge(down_q), merge(down_kv), pad_heads(up_q), merge(up_kv), merge(groups)


def row_block(rows):
    return lambda ref, owner: ref.at[pl.ds(pl.multiple_of(owner * rows, 16), rows), :]


def last_move(grad_lat, gain_terms, query_part, latent_part, count):
    if count != 4:
        return (
            plain_gather(grad_lat), plain_gather(gain_terms), collect(cut_heads(query_part), count),
            collect(latent_part, count),
        )
    rows_q, rows_kv = query_part.shape[0] // 4, latent_part.shape[0] // 4
    lat, got_gains, got_q, got_kv = move(
        "last_move", 8, [grad_lat, gain_terms],
        [(query_part, (rows_q, query_part.shape[1]), row_block(rows_q)),
         (latent_part, (rows_kv, latent_part.shape[1]), row_block(rows_kv))],
    )
    side = lambda value: value.transpose(1, 0, 2).reshape(value.shape[1], -1)
    return lat.reshape(-1, lat.shape[2]), got_gains.reshape(4, -1), cut_heads(side(got_q)), side(got_kv)


def place_kernel(width, own, beside, gf, gf2, gd, gd2, uf, uf2, ud, ud2, gate_ref, up_ref):
    me, core, sib, far = partners()
    gate_ref[...] = jnp.zeros_like(gate_ref)
    up_ref[...] = jnp.zeros_like(up_ref)

    def lanes(owner):
        return pl.ds(pl.multiple_of(owner // 2 * 3200 + owner % 2 * 1536, LANES), width)

    for owner, part in ((me, own), (sib, beside)):
        gate_ref[:, lanes(owner)] += part[:, :width].astype(f32)
        up_ref[:, lanes(owner)] += part[:, width:].astype(f32)
    diagonal = far + 1 - 2 * core
    for owner, gate, gate2, up, up2 in ((far, gf, gf2, uf, uf2), (diagonal, gd, gd2, ud, ud2)):
        gate_ref[:, lanes(owner)] += gate[...].astype(f32) + gate2[...].astype(f32)
        up_ref[:, lanes(owner)] += up[...].astype(f32) + up2[...].astype(f32)


def head_lanes(value):
    return jnp.pad(value, ((0, 0), (NOPE, LANES - NOPE - ROPE)))


def layer_forward(hidden, own_tables, tables, gains, weights, passing, hidden_weights):
    input_gain, query_gain, latent_gain, post_gain = gains
    down_both, query_up, latent_up, output_weight = weights[:4]
    scale_in = norm_scale(hidden)
    normed = (hidden * scale_in * input_gain).astype(bf16)
    down_q, down_kv = down_both
    latent_q = project(normed, down_q)
    latent_kv = project(normed, down_kv)
    latent = latent_kv[:, :KVRANK]
    scale_q = norm_scale(latent_q)
    scale_kv = norm_scale(latent)
    own_in = jnp.concatenate(
        [
            latent_q * scale_q * query_gain,
            latent * scale_kv * latent_gain,
            head_lanes(rotate(latent_kv[:, KVRANK:], *own_tables)),
        ],
        axis=1,
    ).astype(bf16)
    all_in = gather(own_in, 0, 384)
    all_in, finish = hidden_weights(all_in)
    query_in = all_in[:, :QRANK]
    kv_in = all_in[:, QRANK:QRANK + KVRANK]
    shared = all_in[:, QRANK + KVRANK:]
    attended, queries, keyval, logs = attend(
        project(query_in, query_up), project(kv_in, latent_up), shared, tables
    )
    attended, gate_up = finish(attended)
    mixed, normed_two = output_norm(attended, output_weight, hidden, post_gain)
    both = project(normed_two, gate_up)
    width = both.shape[1] // 2
    gate, up = both[:, :width], both[:, width:]
    activated = (jax.nn.silu(gate) * up).astype(bf16)
    def outputs(order=lambda value: value):
        return down_project(order(activated), weights[4], mixed, passing)

    kept = (hidden, scale_in, normed, latent_q, scale_q, latent, scale_kv, query_in, kv_in,
            shared, queries, keyval, logs, attended, mixed, normed_two, gate, up)
    return (outputs, kept, gate_up)


def gate_backward(grad_act, gate, up):
    sigmoid = jax.nn.sigmoid(gate)
    grad_gate = (grad_act * up * sigmoid * (1.0 + gate * (1.0 - sigmoid))).astype(bf16)
    grad_up = (grad_act * gate * sigmoid).astype(bf16)
    return jnp.concatenate([grad_gate, grad_up], axis=1)


def mlp_backward(grad_out, kept, gains, weights):
    mixed, gate, up = kept[14], kept[16], kept[17]
    gate_up, down_weight = weights[4:]
    own_down = (residual_scale * grad_out).astype(bf16)
    grad_down = gather(own_down, 1, 512)
    grad_both = gate_backward(contract_cols(grad_down, down_weight), gate, up)
    grad_mixed, dgain_post, grad_branch = mlp_back(grad_both, gate_up, mixed, grad_out, gains[3])
    return own_down, grad_mixed, dgain_post[0], grad_branch


def attention_backward(grad_mixed, grad_branch, kept, own_tables, tables, gains, weights):
    (hidden, scale_in, normed, latent_q, scale_q, latent, scale_kv, query_in, kv_in,
     shared, queries, keyval, logs, attended, mixed, normed_two, gate, up) = kept
    input_gain, query_gain, latent_gain, post_gain = gains
    down_both, query_up, latent_up, output_weight, gate_up, down_weight = weights
    cosine, sine = own_tables
    grad_attended = contract_cols(grad_branch, output_weight).astype(bf16)
    grad_query, grad_keyval, grad_shared = attend_back(
        queries, keyval, shared, tables, grad_attended, attended, logs
    )
    grad_in = latent_back(grad_query, grad_keyval, grad_shared, query_up, latent_up)
    grad_latent_q, dgain_query = norm_back(latent_q, scale_q, query_gain, grad_in[:, :QRANK])
    grad_latent, dgain_latent = norm_back(
        latent, scale_kv, latent_gain, grad_in[:, QRANK:QRANK + KVRANK]
    )
    start = QRANK + KVRANK + NOPE
    grad_shared = rotate(grad_in[:, start:start + ROPE], cosine, -sine)
    grad_lat = jnp.concatenate(
        [grad_latent_q, grad_latent, jnp.pad(grad_shared, ((0, 0), (0, LANES - ROPE)))], axis=1
    ).astype(bf16)
    down_q, down_kv = down_both
    grad_normed = contract_cols(grad_lat[:, :QRANK], down_q) + contract_cols(
        grad_lat[:, QRANK:QRANK + KVRANK + ROPE], down_kv
    )
    grad_hidden_norm, dgain_input = norm_back(hidden, scale_in, input_gain, grad_normed)
    grad_hidden = grad_mixed + grad_hidden_norm
    found = (grad_branch, grad_query, grad_keyval, grad_lat)
    return (grad_hidden, found, (dgain_input, dgain_query, dgain_latent))


def spread(weight, count):
    rows, columns = weight.shape
    parts = weight.reshape(rows, count, columns // count).transpose(1, 0, 2)
    return lax.all_to_all(parts, "shard", 0, 0, tiled=True).reshape(rows * count, columns // count)


def collect(grad, count):
    rows, columns = grad.shape
    parts = lax.all_to_all(
        grad.reshape(count, rows // count, columns), "shard", 0, 0, tiled=True
    )
    return parts.transpose(1, 0, 2).reshape(rows // count, columns * count)


def pad_heads(weight):
    rows, columns = weight.shape
    heads = weight.reshape(rows, columns // (NOPE + ROPE), NOPE + ROPE)
    return jnp.pad(heads, ((0, 0), (0, 0), (0, LANES - NOPE - ROPE))).reshape(rows, -1)


def cut_heads(grad):
    rows, columns = grad.shape
    heads = grad.reshape(rows, columns // LANES, LANES)[:, :, :NOPE + ROPE]
    return heads.reshape(rows, -1)


def swap(value, step):
    count = lax.axis_size("shard")
    return lax.ppermute(value, "shard", [(source, source ^ step) for source in range(count)])


def hidden_window(count):
    size = FF // count
    width = -(-size // LANES) * LANES
    starts = [owner * size // LANES * LANES for owner in range(count)]
    starts = [min(start, FF - width) for start in starts]
    return size, width, starts, [owner * size - start for owner, start in enumerate(starts)]


def take_at(table, place):
    return jnp.asarray(table, jnp.int32)[place]


def shared_links(count):
    return count == 4 and lax.axis_size("rep") % 2 == 0


def relay_pairs(count):
    reps = lax.axis_size("rep")
    places = [(rep, own) for rep in range(reps) for own in range(count)]
    number = lambda rep, own: rep * count + own
    same = [(number(r, o), number(r, o ^ 2)) for r, o in places if o % 2 == r % 2]
    other = [(number(r, o), number(r, o ^ 3)) for r, o in places if o % 2 != r % 2]
    beside = [(number(r, o), number(r ^ 1, o)) for r, o in places if o % 2 == r % 2]
    return same, other, beside


def relay(value, count):
    *across, beside = relay_pairs(count)
    direct = [lax.ppermute(value, ("rep", "shard"), way) for way in across]
    return [(part, lax.ppermute(part, ("rep", "shard"), beside)) for part in direct]


def relay_owner(me):
    return (me // 2 * 2 + 2) % 4 + lax.axis_index("rep") % 2


def spread_hidden(gate, up, count):
    me = lax.axis_index("shard")
    size, width, starts, offsets = hidden_window(count)
    rows = gate.shape[0]
    whole = jnp.zeros((rows * count, 2 * width), bf16)
    for step in range(count):
        owner = me ^ step
        begin = take_at(starts, owner)
        part = jnp.concatenate(
            [lax.dynamic_slice(gate, (0, begin), (rows, width)), lax.dynamic_slice(up, (0, begin), (rows, width))],
            axis=1,
        )
        if step:
            part = swap(part, step)
        whole = lax.dynamic_update_slice(whole, part, (owner * rows, 0))
    return whole


def relay_hidden(gate, up, count):
    me = lax.axis_index("shard")
    size, width, starts, offsets = hidden_window(count)
    rows = gate.shape[0]
    pairs = relay_pairs(count)
    windows = lambda owner: [
        lax.dynamic_slice(weight, (0, take_at(starts, owner)), (rows, width)) for weight in (gate, up)
    ]
    direct = [
        [lax.ppermute(part, ("rep", "shard"), way) for way in pairs[:2]] for part in windows(relay_owner(me))
    ]
    own = windows(me)
    beside = [swap(part, 1) for part in windows(me ^ 1)]

    def finish(value):
        value, *flat = together(value, *direct[0], *direct[1], *beside)
        whole = jnp.zeros((rows * count, 2 * width), bf16)
        for which in range(2):
            far = [part + lax.ppermute(part, ("rep", "shard"), pairs[2]) for part in flat[2 * which:2 * which + 2]]
            for step, part in enumerate((own[which], flat[4 + which], *far)):
                whole = lax.dynamic_update_slice(whole, part, ((me ^ step) * rows, which * width))
        return value, whole

    return finish


def window_rows(down, count):
    size, width, starts, offsets = hidden_window(count)
    whole = jnp.zeros((width, down.shape[1]), bf16)
    return lax.dynamic_update_slice(whole, down, (take_at(offsets, lax.axis_index("shard")), 0))


def window_gradients(two_all, grad_both, count):
    me = lax.axis_index("shard")
    width = grad_both.shape[1] // 2
    rows = D // count

    def part(owner, grad):
        left = lax.dynamic_slice(two_all, (0, owner * rows), (two_all.shape[0], rows))
        return contract_rows(left, grad).astype(bf16)

    if shared_links(count):
        owner = relay_owner(me)
        return [part(owner, grad_both[:, :width]), part(owner, grad_both[:, width:]), part(me ^ 1, grad_both), part(me, grad_both)]
    return [part(me ^ step, grad_both) for step in reversed(range(count))]


def send_windows(parts, count):
    if shared_links(count):
        gate, up, beside, own = parts
        return [own, swap(beside, 1), *(relay(gate, count)), *(relay(up, count))]
    return [parts[-1]] + [swap(parts[count - 1 - step], step) for step in range(1, count)]


def place_windows(parts, count):
    size, width, starts, offsets = hidden_window(count)
    rows = parts[0].shape[0]
    if shared_links(count):
        own, beside, gate_far, gate_diagonal, up_far, up_diagonal = parts
        inputs = [own, beside, *gate_far, *gate_diagonal, *up_far, *up_diagonal]
        tile = 64
        return pl.pallas_call(
            functools.partial(place_kernel, width),
            grid=(rows // tile,),
            in_specs=[pl.BlockSpec((tile, v.shape[1]), lambda i: (i, 0)) for v in inputs],
            out_specs=[pl.BlockSpec((tile, FF), lambda i: (i, 0))] * 2,
            out_shape=[jax.ShapeDtypeStruct((rows, FF), f32)] * 2,
            compiler_params=pltpu.CompilerParams(vmem_limit_bytes=VMEM_LIMIT),
            name="place_windows",
        )(*inputs)
    me = lax.axis_index("shard")
    gathered = jnp.zeros((count, rows, 2 * width), bf16)
    for step, part in enumerate(parts):
        gathered = lax.dynamic_update_slice(gathered, part[None], (me ^ step, 0, 0))
    totals = []
    for which in range(2):
        pieces = []
        for owner in range(count):
            offset = which * width + offsets[owner]
            pieces.append(gathered[owner, :, offset:offset + size])
        totals.append(jnp.concatenate(pieces, axis=1).astype(f32))
    return totals


def together(*values):
    return lax.optimization_barrier(values)


def body(tokens, segment_ids, input_gain, query_gain, latent_gain, post_gain, query_down, query_up,
         latent_down, latent_up, output_weight, gate_weight, up_weight, down_weight, cotangent):
    at_start = lax.axis_index("section") == 0
    count = lax.axis_size("shard")
    size, width, starts, offsets = hidden_window(count)
    gains = (input_gain[0], query_gain[0], latent_gain[0], post_gain[0])
    down_q, down_kv, query_up_all, latent_up_all, groups = first_move(
        query_down[0], latent_down[0], query_up[0], latent_up[0], segment_ids, count
    )
    down_both = (down_q, down_kv)
    down_rows = window_rows(down_weight[0], count)
    weights = (down_both, query_up_all, latent_up_all, output_weight[0], down_rows)
    own_tables = tuple(t.reshape(-1, ROPE // 2) for t in slot_tables(segment_ids))
    tables = head_tables(groups)

    def first_weights(all_in):
        all_in, gate, up = together(all_in, gate_weight[0], up_weight[0])
        if shared_links(count):
            return all_in, relay_hidden(gate, up, count)
        whole = spread_hidden(gate, up, count)
        return all_in, lambda value: (value, whole)

    start = tokens.astype(f32)
    outputs, _, gate_up = layer_forward(start, own_tables, tables, gains, weights, True, first_weights)
    leaving, low, received = outputs()
    received, last = together(received, cotangent)
    last = last.astype(f32)
    entering = jnp.where(at_start, start, received.astype(f32))
    outputs, kept, _ = layer_forward(
        entering, own_tables, tables, gains, weights, False, lambda all_in: (all_in, lambda value: (value, gate_up))
    )
    weights = weights[:4] + (gate_up, down_rows)

    (hidden, scale_in, normed, latent_q, scale_q, latent, scale_kv, query_in, kv_in,
     shared, queries, keyval, logs, attended, mixed, normed_two, gate, up) = kept
    rows = hidden.shape[0]
    _, grad_mixed, _, grad_branch = mlp_backward(last, kept, gains, weights)
    own_two = lax.dynamic_slice_in_dim(normed_two, lax.axis_index("shard") * rows, rows, 0)
    grad_branch, own_two = together(grad_branch, own_two)
    two_all = lax.all_gather(own_two, ("rep", "shard"), axis=0, tiled=True)
    grad, _, _ = attention_backward(grad_mixed, grad_branch, kept, own_tables, tables, gains, weights)
    returned = lax.ppermute(grad.astype(bf16), "section", [(1, 0)])
    incoming = jnp.where(at_start, returned.astype(f32), last)

    own_down, grad_mixed, dgain_post, grad_branch = mlp_backward(incoming, kept, gains, weights)
    grad_branch, own_down, two_all = together(grad_branch, own_down, two_all)
    down_all = lax.all_gather(own_down, ("rep", "shard"), axis=0, tiled=True)
    part_output = contract_rows(attended, grad_branch).astype(bf16)
    grad_branch, part_output = together(grad_branch, part_output)
    total_output = lax.psum(part_output, "rep")

    grad, found, (dgain_input, dgain_query, dgain_latent) = attention_backward(
        grad_mixed, grad_branch, kept, own_tables, tables, gains, weights
    )
    grad_branch, grad_query, grad_keyval, grad_lat = found
    gain_terms = jnp.concatenate([dgain_input, dgain_query, dgain_latent, dgain_post])[None]
    normed_rows = lax.all_to_all(
        normed.reshape(normed.shape[0], count, -1).transpose(1, 0, 2), "shard", 0, 0, tiled=True
    ).reshape(normed.shape[0] * count, -1)
    part_query = contract_rows(query_in, grad_query).astype(bf16)
    part_latent = contract_rows(kv_in, grad_keyval).astype(bf16)
    lat_all, gains_all, part_query, part_latent = last_move(
        grad_lat, gain_terms, part_query, part_latent, count
    )
    part_down = contract_rows(normed_rows, lat_all[:, :QRANK + KVRANK + ROPE]).astype(bf16)
    part_gains = jnp.sum(gains_all, axis=0).astype(bf16)
    part_down, part_query, part_latent, down_all = together(part_down, part_query, part_latent, down_all)
    part_down, total_output = together(part_down, total_output)
    side = part_down.shape[1]
    gain_rows = -(-part_gains.shape[0] // side)
    part_gains = jnp.pad(part_gains, (0, gain_rows * side - part_gains.shape[0])).reshape(gain_rows, side)
    part_down = jnp.concatenate([part_down, part_gains], axis=0)
    total_down_both, total_query, total_latent = (
        part.astype(f32) for part in lax.psum((part_down, part_query, part_latent), "rep")
    )
    gain_totals = total_down_both[-gain_rows:].reshape(-1)
    total_down_both = total_down_both[:-gain_rows]

    both = project(two_all, gate_up)
    gate_all, up_all = both[:, :width], both[:, width:]
    activated_all = (jax.nn.silu(gate_all) * up_all).astype(bf16)
    grad_both = gate_backward(contract_cols(down_all, down_rows), gate_all, up_all)
    payloads = window_gradients(two_all, grad_both, count)
    activated_all, *payloads = together(activated_all, *payloads)
    hidden_parts = send_windows(payloads, count)
    total_down = contract_rows(activated_all, down_all)
    offset = take_at(offsets, lax.axis_index("shard"))
    total_down = lax.dynamic_slice_in_dim(total_down, offset, size, 0)
    leaving, boundary = outputs(lambda value: together(value, total_down)[0])
    total_gate, total_up = place_windows(hidden_parts, count)
    first, second, third = D, D + QRANK, D + QRANK + KVRANK
    gain_totals = (gain_totals[:first], gain_totals[first:second], gain_totals[second:third], gain_totals[third:third + D])
    return (
        boundary[None],
        grad[None],
        gain_totals[0][None],
        gain_totals[1][None],
        gain_totals[2][None],
        gain_totals[3][None],
        total_down_both[None, :, :QRANK],
        total_query[None],
        total_down_both[None, :, QRANK:],
        total_latent[None],
        total_output.astype(f32)[None],
        total_gate[None],
        total_up[None],
        total_down[None],
    )


def solution(mesh):
    tokens = P(("rep", "shard"), None)
    gain = P("section", None)
    weight = P("section", "shard", None)
    out = P("section", ("rep", "shard"), None)
    return jax.shard_map(
        body,
        mesh=mesh,
        in_specs=(tokens, tokens) + (gain,) * 4 + (weight,) * 8 + (tokens,),
        out_specs=(out, out) + (gain,) * 4 + (weight,) * 8,
        check_vma=False,
    )
```

```python
import functools
import math

import jax
import jax.numpy as jnp
from jax import lax
from jax.experimental import pallas as pl
from jax.experimental.pallas import tpu as pltpu
from jax.sharding import PartitionSpec as P

D = 2560
HEADS = 40
NOPE = 64
ROPE = 32
VDIM = 64
QRANK = 768
KVRANK = 256
FF = 6400
SLOT = 96
LANES = 128

epsilon = 1e-05
residual_scale = 1.4 / math.sqrt(62.0)
masked_score = -1e30
score_scale = 1.0 / math.sqrt(NOPE + ROPE)
bf16 = jnp.bfloat16
f32 = jnp.float32


def norm_scale(value):
    return lax.rsqrt(jnp.mean(value * value, axis=-1, keepdims=True) + epsilon)


def norm_back(value, scale, gain, grad):
    weighted = grad * gain
    inner = jnp.mean(value * weighted, axis=-1, keepdims=True)
    grad_value = scale * weighted - value * (scale * scale * scale) * inner
    return (grad_value, jnp.sum(grad * value * scale, axis=0))


def rotate(value, cosine, sine):
    half = value.shape[-1] // 2
    front = value[..., :half]
    back = value[..., half:]
    return jnp.concatenate([front * cosine - back * sine, back * cosine + front * sine], axis=-1)


def slot_tables(segments):
    index = jnp.arange(SLOT, dtype=jnp.int32)
    first_index = jnp.sum((segments[:, None, :] < segments[:, :, None]).astype(jnp.int32), axis=-1)
    position = (index - first_index).astype(f32)
    freq = jnp.exp(jnp.arange(ROPE // 2, dtype=f32) * (-2.0 * math.log(10000.0) / ROPE))
    angle = position[..., None] * freq
    return (jnp.cos(angle), jnp.sin(angle))


def head_tables(segments):
    cosine, sine = slot_tables(segments)
    slots = segments.shape[0]
    ones = jnp.ones((slots, SLOT, NOPE), f32)
    tail = jnp.zeros((slots, SLOT, LANES - NOPE - ROPE), f32)
    half = jnp.zeros_like(sine)
    keep = jnp.concatenate([ones, cosine, cosine, tail], axis=-1)
    left = jnp.concatenate([0.0 * ones, -sine, half, tail], axis=-1)
    right = jnp.concatenate([0.0 * ones, half, sine, tail], axis=-1)
    index = jnp.arange(SLOT, dtype=jnp.int32)
    allowed = (segments[:, :, None] == segments[:, None, :]) & (index[None, :] <= index[:, None])
    mask = jnp.where(allowed, 0.0, masked_score).astype(f32)
    flat = lambda table: table.reshape(slots * SLOT, LANES)
    return (flat(keep), flat(left), flat(right), mask, mask.transpose(0, 2, 1))


def contract_rows(left, right):
    return lax.dot_general(left, right, (((0,), (0,)), ((), ())), preferred_element_type=f32)


def contract_cols(left, right):
    return lax.dot_general(left, right, (((1,), (1,)), ((), ())), preferred_element_type=f32)


def project(left, weight):
    return jnp.dot(left, weight, preferred_element_type=f32)


def low_lanes():
    return lax.broadcasted_iota(jnp.int32, (SLOT, LANES), 1) < NOPE


HEAD_GROUP = 5
HEAD_ROWS = 16


def attend_kernel(heads, q_ref, kv_ref, sh_ref, keep_ref, left_ref, right_ref, mask_ref,
                  att_ref, qo_ref, kvo_ref, log_ref):
    low = low_lanes()
    lane = lax.broadcasted_iota(jnp.int32, (SLOT, LANES), 1)
    shared = sh_ref[...].astype(f32)
    keep, left, right = keep_ref[...], left_ref[...], right_ref[...]
    mask = mask_ref[0]
    tallest = jnp.zeros((SLOT, LANES), f32)
    sums = jnp.ones((SLOT, LANES), f32)
    for first in range(0, heads, HEAD_GROUP):
        group = range(first, min(first + HEAD_GROUP, heads))
        scores, values = [], []
        for head in group:
            lanes = slice(head * LANES, (head + 1) * LANES)
            q = q_ref[:, lanes]
            q = q * keep + pltpu.roll(q, LANES - 16, 1) * left + pltpu.roll(q, 16, 1) * right
            q = q.astype(bf16)
            qo_ref[:, lanes] = q
            kv = kv_ref[:, lanes]
            kvo_ref[:, lanes] = kv.astype(bf16)
            k = jnp.where(low, kv, shared).astype(bf16)
            values.append(jnp.where(low, 1.0, kv).astype(bf16))
            scores.append(contract_cols(q, k) * score_scale + mask)
        tops = [jnp.max(score, axis=-1, keepdims=True) for score in scores]
        terms = [jnp.exp(score - top).astype(bf16) for score, top in zip(scores, tops)]
        outs = [project(term, value) for term, value in zip(terms, values)]
        for head, top, out in zip(group, tops, outs):
            turned = pltpu.roll(out, NOPE, 1)
            tallest = jnp.where(lane == head, top, tallest)
            sums = jnp.where(lane == head, out, sums)
            pair = (head // 2) * LANES
            if head % 2 == 0:
                att = turned / out
                att_ref[:, pair:pair + VDIM] = att[:, :VDIM].astype(bf16)
            else:
                att = out / turned
                att_ref[:, pair + VDIM:pair + LANES] = att[:, VDIM:].astype(bf16)
    log_ref[0] = (tallest + jnp.log(sums)).T[:HEAD_ROWS, :]


def attention_cost(tokens, heads, passes):
    return pl.CostEstimate(
        flops=passes * tokens * heads * SLOT * LANES * 20, bytes_accessed=tokens * heads * LANES * 12,
        transcendentals=tokens * heads * SLOT,
    )


def attend(query, keyval, shared, tables):
    tokens = query.shape[0]
    heads = query.shape[1] // LANES
    wide = pl.BlockSpec((SLOT, heads * LANES), lambda s: (s, 0))
    one = pl.BlockSpec((SLOT, LANES), lambda s: (s, 0))
    square = pl.BlockSpec((1, SLOT, SLOT), lambda s: (s, 0, 0))
    return pl.pallas_call(
        functools.partial(attend_kernel, heads),
        grid=(tokens // SLOT,),
        in_specs=[wide, wide, one, one, one, one, square],
        out_specs=[pl.BlockSpec((SLOT, heads * VDIM), lambda s: (s, 0)), wide, wide,
                   pl.BlockSpec((1, HEAD_ROWS, SLOT), lambda s: (s, 0, 0))],
        out_shape=[
            jax.ShapeDtypeStruct((tokens, heads * VDIM), bf16),
            jax.ShapeDtypeStruct(query.shape, bf16),
            jax.ShapeDtypeStruct(keyval.shape, bf16),
            jax.ShapeDtypeStruct((tokens // SLOT, HEAD_ROWS, SLOT), f32),
        ],
        cost_estimate=attention_cost(tokens, heads, 4),
        name="attend",
    )(query, keyval, shared, *tables[:4])


def attend_back_kernel(heads, q_ref, kv_ref, sh_ref, keep_ref, left_ref, right_ref, mask_ref,
                       ga_ref, att_ref, log_ref, gq_ref, gkv_ref, gsh_ref):
    low = low_lanes()
    shared = sh_ref[...].astype(f32)
    keep, left, right = keep_ref[...], left_ref[...], right_ref[...]
    mask = mask_ref[0]
    total = jnp.zeros((SLOT, LANES), f32)
    product = ga_ref[...].astype(f32) * att_ref[...].astype(f32)
    high = product.astype(bf16)
    rest = (product - high.astype(f32)).astype(bf16)
    shape = (HEAD_ROWS, product.shape[1])
    chosen = lax.broadcasted_iota(jnp.int32, shape, 1) // VDIM == lax.broadcasted_iota(jnp.int32, shape, 0)
    chosen = jnp.where(chosen, 1.0, 0.0).astype(bf16)
    inner = contract_cols(chosen, high) + contract_cols(chosen, rest)
    for first in range(0, heads, HEAD_GROUP):
        group = range(first, min(first + HEAD_GROUP, heads))
        queries, keys, grads, scores, grad_probs = [], [], [], [], []
        for head in group:
            lanes = slice(head * LANES, (head + 1) * LANES)
            q = q_ref[:, lanes]
            kvb = kv_ref[:, lanes]
            k = jnp.where(low, kvb.astype(f32), shared).astype(bf16)
            if head % 2 == 0 and head == heads - 1:
                ga = ga_ref[:, head * VDIM:(head + 1) * VDIM].astype(f32)
                ga = jnp.concatenate([jnp.zeros_like(ga), ga], axis=1)
            else:
                start = (head // 2) * LANES
                ga = ga_ref[:, start:start + LANES].astype(f32)
                if head % 2 == 0:
                    ga = pltpu.roll(ga, NOPE, 1)
                ga = jnp.where(low, 0.0, ga)
            ga = ga.astype(bf16)
            queries.append(q)
            keys.append(k)
            grads.append(ga)
            scores.append(contract_cols(k, q) * score_scale + mask)
            grad_probs.append(contract_cols(kvb, ga))
        probs = [jnp.exp(score - log_ref[0, head:head + 1, :]) for head, score in zip(group, scores)]
        changes = [
            (prob * (grad - inner[head:head + 1, :]) * score_scale).astype(bf16)
            for head, prob, grad in zip(group, probs, grad_probs)
        ]
        grad_values = [project(prob.astype(bf16), ga) for prob, ga in zip(probs, grads)]
        grad_keys = [project(change, q) for change, q in zip(changes, queries)]
        grad_queries = [contract_rows(change, k) for change, k in zip(changes, keys)]
        for head, gv, gk, gq in zip(group, grad_values, grad_keys, grad_queries):
            lanes = slice(head * LANES, (head + 1) * LANES)
            gq = gq * keep - pltpu.roll(gq, LANES - 16, 1) * left - pltpu.roll(gq, 16, 1) * right
            gq_ref[:, lanes] = gq.astype(bf16)
            total = total + gk
            gkv_ref[:, lanes] = jnp.where(low, gk, gv).astype(bf16)
    gsh_ref[...] = total


def attend_back(query, keyval, shared, tables, grad_attended, attended, logs):
    tokens = query.shape[0]
    heads = query.shape[1] // LANES
    wide = pl.BlockSpec((SLOT, heads * LANES), lambda s: (s, 0))
    one = pl.BlockSpec((SLOT, LANES), lambda s: (s, 0))
    half = pl.BlockSpec((SLOT, heads * VDIM), lambda s: (s, 0))
    return pl.pallas_call(
        functools.partial(attend_back_kernel, heads),
        grid=(tokens // SLOT,),
        in_specs=[wide, wide, one, one, one, one, pl.BlockSpec((1, SLOT, SLOT), lambda s: (s, 0, 0)),
                  half, half, pl.BlockSpec((1, HEAD_ROWS, SLOT), lambda s: (s, 0, 0))],
        out_specs=[wide, wide, one],
        out_shape=[
            jax.ShapeDtypeStruct(query.shape, bf16),
            jax.ShapeDtypeStruct(keyval.shape, bf16),
            jax.ShapeDtypeStruct((tokens, LANES), f32),
        ],
        cost_estimate=attention_cost(tokens, heads, 10),
        name="attend_back",
    )(query, keyval, shared, *tables[:3], tables[4], grad_attended, attended, logs)


MESH = pl.DeviceIdType.MESH
VMEM_LIMIT = 60 * 1024 * 1024


def partners():
    me = lax.axis_index("shard")
    core = me % 2
    return me, core, me + 1 - 2 * core, (me + 2) % 4


def greet(devices):
    barrier = pltpu.get_barrier_semaphore()
    for device in devices:
        pl.semaphore_signal(barrier, inc=1, device_id=device, device_id_type=MESH)
    pl.semaphore_wait(barrier, len(devices))


def columns(step, width):
    return pl.ds(pl.multiple_of(step * width, LANES), width)


def rows_at(start, rows):
    return pl.ds(pl.multiple_of(start * rows, 16), rows)


def remote(source, target, sems, step, device):
    return pltpu.make_async_remote_copy(
        src_ref=source, dst_ref=target, send_sem=sems.at[0, step], recv_sem=sems.at[1, step],
        device_id={"shard": device}, device_id_type=MESH,
    )


def exchange_scratch(rows, steps, width):
    part = pltpu.VMEM((steps, rows, width), bf16)
    return [part] * 6 + [
        pltpu.VMEM((steps, rows, width), f32),
        pltpu.VMEM((2 * rows, width), f32),
        pltpu.SemaphoreType.DMA((3, 2, steps)),
    ]


def each(steps, unrolled, do):
    if unrolled:
        for step in range(steps):
            do(step)
    else:
        def again(step, carry):
            do(step)
            return carry
        lax.fori_loop(0, steps, again, 0)


def sum_scatter(rows, steps, unrolled, partial, scratch, use):
    (to_sib, from_sib, to_far, from_far, own_sib, own_from, hold, stage, sems) = scratch
    me, core, sib, far = partners()
    mine = rows_at(core, rows)
    other = rows_at(1 - core, rows)

    def first(step):
        return remote(to_sib.at[step], from_sib.at[step], sems.at[0], step, sib)

    def across(step):
        return remote(to_far.at[step], from_far.at[step], sems.at[1], step, far)

    def beside(step):
        return remote(own_sib.at[step], own_from.at[step], sems.at[2], step, sib)

    def far_part(step):
        stage[...] = partial(rows_at(far // 2, 2 * rows), step)
        to_sib[step] = stage[other, :].astype(bf16)
        first(step).start()
        hold[step] = stage[mine, :]

    def far_send(step):
        first(step).wait_recv()
        to_far[step] = (hold[step] + from_sib[step].astype(f32)).astype(bf16)
        across(step).start()

    def far_step(step):
        far_part(step)
        if unrolled:
            if step > 0:
                far_send(step - 1)
        else:
            @pl.when(step > 0)
            def _():
                far_send(step - 1)

    each(steps, unrolled, far_step)
    far_send(steps - 1)

    def near_part(step):
        stage[...] = partial(rows_at(me // 2, 2 * rows), step)
        own_sib[step] = stage[other, :].astype(bf16)
        beside(step).start()
        hold[step] = stage[mine, :]

    each(steps, unrolled, near_part)

    def finish(step):
        beside(step).wait_recv()
        across(step).wait_recv()
        use(step, hold[step] + own_from[step].astype(f32) + from_far[step].astype(f32))

    each(steps, unrolled, finish)

    def settle(step):
        first(step).wait_send()
        across(step).wait_send()
        beside(step).wait_send()

    each(steps, unrolled, settle)


def spread_rows(rows, steps, width, place, all_ref, sems):
    me, core, sib, far = partners()

    def part(owner, step):
        return all_ref.at[rows_at(owner, rows), columns(step, width)]

    def across(step):
        return remote(part(me, step), part(me, step), sems.at[0], step, far)

    def beside(step):
        return remote(part(me, step), part(me, step), sems.at[1], step, sib)

    def onward(step):
        return remote(part(far, step), part(far, step), sems.at[2], step, sib)

    def send(step):
        place(step)
        across(step).start()
        beside(step).start()

    each(steps, False, send)

    def forward(step):
        across(step).wait_recv()
        onward(step).start()

    each(steps, False, forward)

    def settle(step):
        beside(step).wait_recv()
        onward(step).wait_recv()
        across(step).wait_send()
        beside(step).wait_send()
        onward(step).wait_send()

    each(steps, False, settle)


def vmem(count):
    return [pl.BlockSpec(memory_space=pltpu.VMEM)] * count


def comm_call(kernel, name, number, inputs, out_shape, scratch, flops=0, aliased={}):
    nbytes = sum(v.size * v.dtype.itemsize for v in (*inputs, *out_shape))
    return pl.pallas_call(
        kernel,
        in_specs=vmem(len(inputs) - len(aliased)) + any_space(len(aliased)),
        out_specs=vmem(len(out_shape) - len(aliased)) + any_space(len(aliased)),
        out_shape=out_shape,
        scratch_shapes=scratch,
        input_output_aliases=aliased,
        compiler_params=pltpu.CompilerParams(
            collective_id=number, has_side_effects=True, vmem_limit_bytes=VMEM_LIMIT
        ),
        cost_estimate=pl.CostEstimate(flops=0, bytes_accessed=0 * nbytes, transcendentals=0),
        name=name,
    )(*inputs)


def shape(rows, width, dtype):
    return jax.ShapeDtypeStruct((rows, width), dtype)


def gather_kernel(steps, width, own_ref, all_ref, sems):
    rows = own_ref.shape[0]
    me, core, sib, far = partners()
    greet([{"shard": sib}, {"shard": far}])

    def place(step):
        all_ref[rows_at(me, rows), columns(step, width)] = own_ref[:, columns(step, width)]

    spread_rows(rows, steps, width, place, all_ref, sems)


def gather(value, number, width):
    if lax.axis_size("shard") != 4:
        return lax.all_gather(value, "shard", axis=0, tiled=True)
    rows, total = value.shape
    steps = total // width
    (out,) = comm_call(
        functools.partial(gather_kernel, steps, width), "gather_rows", number, [value],
        [shape(4 * rows, total, bf16)], [pltpu.SemaphoreType.DMA((3, 2, steps))],
    )
    return out


def plain_gather(value):
    return lax.all_gather(value, "shard", axis=0, tiled=True)


def plain_scatter(value):
    return lax.psum_scatter(value.astype(bf16), "shard", scatter_dimension=0, tiled=True).astype(f32)


MODEL_STEP = 512


def output_kernel(relaying, att_ref, weight_ref, hidden_ref, gain_ref, *refs):
    if relaying:
        _, mixed_ref, two_ref, up_ref, *scratch, passed = refs
    else:
        mixed_ref, two_ref, *scratch = refs
    *parts, sems = scratch
    rows = hidden_ref.shape[0]
    width = MODEL_STEP
    steps = D // width
    me, core, sib, far = partners()
    devices = [{"shard": sib}, {"shard": far}]
    if relaying:
        partner, away = replica_pair()
        devices.append({"rep": partner})
    greet(devices)
    if relaying:
        @pl.when(away == 0)
        def _():
            for slot, owner in enumerate((far, far + 1 - 2 * core)):
                pass_on(up_ref, passed, slot, owner).start()

    def partial(where, step):
        return project(att_ref[where, :], weight_ref[:, columns(step, width)])

    def use(step, total):
        lanes = columns(step, width)
        mixed_ref[:, lanes] = hidden_ref[:, lanes] + residual_scale * total

    sum_scatter(rows, steps, False, partial, parts, use)
    mixed = mixed_ref[...]
    scale = norm_scale(mixed)

    def place(step):
        lanes = columns(step, width)
        two_ref[rows_at(me, rows), lanes] = (mixed_ref[:, lanes] * scale * gain_ref[:, lanes]).astype(bf16)

    spread_rows(rows, steps, width, place, two_ref, sems)
    if relaying:
        @pl.when(away == 0)
        def _():
            for slot, owner in enumerate((far, far + 1 - 2 * core)):
                pass_on(up_ref, passed, slot, owner).wait_send()

        @pl.when(away == 1)
        def _():
            for slot, owner in enumerate((far, far + 1 - 2 * core)):
                pass_on(up_ref, passed, slot, owner).wait_recv()


def output_norm(attended, weight, hidden, gain, up=None):
    if lax.axis_size("shard") != 4:
        mixed = hidden + residual_scale * plain_scatter(project(attended, weight))
        return mixed, plain_gather((mixed * norm_scale(mixed) * gain).astype(bf16))
    rows = hidden.shape[0]
    steps = D // MODEL_STEP
    scratch = exchange_scratch(rows, steps, MODEL_STEP) + [pltpu.SemaphoreType.DMA((3, 2, steps))]
    inputs = [attended, weight, hidden, gain[None]]
    outputs = [shape(rows, D, f32), shape(4 * rows, D, bf16)]
    flops = 2 * attended.size * D
    if up is None:
        return comm_call(functools.partial(output_kernel, False), "output_norm", 2, inputs, outputs, scratch, flops)
    return comm_call(
        functools.partial(output_kernel, True), "output_norm", 9, inputs + [up],
        outputs + [jax.ShapeDtypeStruct(up.shape, bf16)], scratch + [pltpu.SemaphoreType.DMA((2, 2))], flops,
        aliased={4: 2},
    )


def down_kernel(passing, act_ref, given_ref, mixed_ref, out_ref, low_ref, *scratch):
    rows = mixed_ref.shape[0]
    width = MODEL_STEP
    steps = D // width
    me, core, sib, far = partners()
    devices = [{"shard": sib}, {"shard": far}]
    weight_ref = given_ref
    if passing:
        got_ref, weight_ref, *parts, sems = scratch
        size, more = given_ref.shape[0], weight_ref.shape[0] - given_ref.shape[0]
        weight_ref[pl.ds(pl.multiple_of((1 - core) * size, 16), more), :] = jnp.zeros((more, D), bf16)
        piece = 64

        def fill(step):
            source = pl.ds(pl.multiple_of(step * piece, 16), piece)
            target = pl.ds(pl.multiple_of(step * piece + core * more, 16), piece)
            weight_ref[target, :] = given_ref[source, :]

        each(size // piece, False, fill)
        section = lax.axis_index("section")
        devices.append({"section": 1 - section})
    else:
        parts = scratch
    greet(devices)

    def onward(step):
        lanes = columns(step, width)
        return pltpu.make_async_remote_copy(
            src_ref=low_ref.at[:, lanes], dst_ref=got_ref.at[:, lanes], send_sem=sems.at[0, step],
            recv_sem=sems.at[1, step], device_id={"section": 1 - section}, device_id_type=MESH,
        )

    def partial(where, step):
        return project(act_ref[where, :], weight_ref[:, columns(step, width)])

    def use(step, total):
        lanes = columns(step, width)
        out = mixed_ref[:, lanes] + residual_scale * total
        out_ref[:, lanes] = out
        low_ref[:, lanes] = out.astype(bf16)
        if passing:
            onward(step).start()

    sum_scatter(rows, steps, False, partial, parts, use)
    if passing:
        each(steps, False, lambda step: onward(step).wait())


def down_project(activated, weight, mixed, passing):
    count = lax.axis_size("shard")
    if count != 4:
        if passing:
            weight = window_rows(weight, count)
        output = mixed + residual_scale * plain_scatter(project(activated, weight))
        low = output.astype(bf16)
        return (output, low) + ((lax.ppermute(low, "section", [(0, 1)]), weight) if passing else ())
    rows = mixed.shape[0]
    steps = D // MODEL_STEP
    scratch = exchange_scratch(rows, steps, MODEL_STEP)
    return comm_call(
        functools.partial(down_kernel, passing), "down_project", 3 if passing else 4,
        [activated, weight, mixed],
        [shape(rows, D, f32)] + [shape(rows, D, bf16)] * (2 if passing else 1)
        + [shape(HIDDEN_WINDOW, D, bf16)] * passing,
        scratch + ([pltpu.SemaphoreType.DMA((2, steps))] if passing else []),
        flops=2 * activated.size * D,
    )


def mlp_back_kernel(gate_ref, up_ref, gate_weight_ref, up_weight_ref, mixed_ref, grad_ref, gain_ref, out_ref, dgain_ref, branch_ref,
                    *scratch):
    *parts, sems = scratch
    rows = mixed_ref.shape[0]
    width = MODEL_STEP
    steps = D // width
    me, core, sib, far = partners()
    greet([{"shard": sib}, {"shard": far}])

    def partial(where, step):
        rows_of = columns(step, width)
        return contract_cols(gate_ref[where, :], gate_weight_ref[rows_of, :]) + contract_cols(
            up_ref[where, :], up_weight_ref[rows_of, :]
        )

    def use(step, total):
        out_ref[:, columns(step, width)] = total

    sum_scatter(rows, steps, False, partial, parts, use)
    mixed = mixed_ref[...]
    scale = norm_scale(mixed)
    inner = jnp.mean(mixed * out_ref[...] * gain_ref[...], axis=-1, keepdims=True)
    slope = scale * scale * scale * inner

    def place(step):
        lanes = columns(step, width)
        grad, value = out_ref[:, lanes], mixed_ref[:, lanes]
        dgain_ref[:, lanes] = jnp.sum(grad * value * scale, axis=0, keepdims=True)
        total = grad_ref[:, lanes] + scale * (grad * gain_ref[:, lanes]) - value * slope
        out_ref[:, lanes] = total
        branch_ref[rows_at(me, rows), lanes] = (residual_scale * total).astype(bf16)

    spread_rows(rows, steps, width, place, branch_ref, sems)


def mlp_back(grad_gate, grad_up, gate_weight, up_weight, mixed, grad_out, gain):
    if lax.axis_size("shard") != 4:
        grad = plain_scatter(contract_cols(grad_gate, gate_weight) + contract_cols(grad_up, up_weight))
        back, dgain = norm_back(mixed, norm_scale(mixed), gain, grad)
        grad_mixed = grad_out + back
        return grad_mixed, dgain[None], plain_gather((residual_scale * grad_mixed).astype(bf16))
    rows = mixed.shape[0]
    steps = D // MODEL_STEP
    return comm_call(
        mlp_back_kernel, "mlp_back", 5,
        [grad_gate, grad_up, gate_weight, up_weight, mixed, grad_out, gain[None]],
        [shape(rows, D, f32), shape(1, D, f32), shape(4 * rows, D, bf16)],
        exchange_scratch(rows, steps, MODEL_STEP) + [pltpu.SemaphoreType.DMA((3, 2, steps))],
        flops=4 * grad_gate.size * D,
    )


LATENT_STEP = 256


def latent_back_kernel(gq_ref, gkv_ref, gsh_ref, qup_ref, lup_ref, out_ref, *scratch):
    rows = out_ref.shape[0]
    width = LATENT_STEP
    me, core, sib, far = partners()
    greet([{"shard": sib}, {"shard": far}])

    def partial(where, step):
        if step < QRANK // width:
            return contract_cols(gq_ref[where, :], qup_ref[step * width:(step + 1) * width, :])
        if step == QRANK // width:
            return contract_cols(gkv_ref[where, :], lup_ref[...])
        shared = gsh_ref[where, :]
        return jnp.concatenate([shared, jnp.zeros_like(shared)], axis=1)

    def use(step, total):
        out_ref[:, step * width:(step + 1) * width] = total

    sum_scatter(rows, out_ref.shape[1] // width, True, partial, scratch, use)


def latent_back(grad_query, grad_keyval, grad_shared, query_up, latent_up):
    if lax.axis_size("shard") != 4:
        return plain_scatter(
            jnp.concatenate(
                [contract_cols(grad_query, query_up), contract_cols(grad_keyval, latent_up), grad_shared],
                axis=1,
            )
        )
    rows = grad_query.shape[0] // 4
    steps = QRANK // LATENT_STEP + 2
    (out,) = comm_call(
        latent_back_kernel, "latent_back", 6, [grad_query, grad_keyval, grad_shared, query_up, latent_up],
        [shape(rows, steps * LATENT_STEP, f32)], exchange_scratch(rows, steps, LATENT_STEP),
        flops=2 * grad_query.size * QRANK + 2 * grad_keyval.size * KVRANK,
    )
    return out


def any_space(count):
    return [pl.BlockSpec(memory_space=pl.ANY)] * count


def pair(value, index):
    return value.at[0, index], value.at[1, index]


def send_to(source, target, sems, index, device):
    send, receive = pair(sems, index)
    return pltpu.make_async_remote_copy(
        src_ref=source, dst_ref=target, send_sem=send, recv_sem=receive,
        device_id={"shard": device}, device_id_type=MESH,
    )


def replica_pair():
    replica = lax.axis_index("rep")
    return replica + 1 - 2 * (replica % 2), (lax.axis_index("shard") + replica) % 2


def pass_on(target, sems, step, owner):
    partner, _ = replica_pair()
    return pltpu.make_async_remote_copy(
        src_ref=target.at[owner], dst_ref=target.at[owner], send_sem=sems.at[0, step], recv_sem=sems.at[1, step],
        device_id={"rep": partner}, device_id_type=MESH,
    )


def move_kernel(whole, split, relayed, *refs):
    amount = whole + len(split) + len(relayed)
    inputs, outputs, held = refs[:amount], refs[amount:2 * amount], refs[2 * amount:3 * amount]
    sems, local, *relays = refs[3 * amount:]
    me, core, sib, far = partners()
    diagonal = far + 1 - 2 * core
    devices = [{"shard": sib}, {"shard": far}, {"shard": diagonal}]
    if relayed:
        partner, away = replica_pair()
        devices.append({"rep": partner})
    greet(devices)
    waits, forwards, keeps, bulk = [], [], [], []
    number = 0
    for i, (source, target) in enumerate(zip(inputs, outputs)):
        if i < whole:
            to_far = send_to(source, target.at[me], sems, number, far)
            to_sib = send_to(source, target.at[me], sems, number + 1, sib)
            onward = send_to(target.at[far], target.at[far], sems, number + 2, sib)
            to_far.start()
            to_sib.start()
            forwards.append((to_far, onward))
            waits.append(to_sib)
            kept = source
        elif i < whole + len(split):
            part = split[i - whole]
            for j, device in enumerate((far, diagonal, sib)):
                copy = send_to(part(source, device), target.at[me], sems, number + j, device)
                copy.start()
                waits.append(copy)
            kept = part(source, me)
        else:
            begin, arrive, passed = relays
            place = i - whole - len(split)
            taker = far // 2 * 2 + lax.axis_index("rep") % 2

            def across(owner, slot):
                return pltpu.make_async_remote_copy(
                    src_ref=hidden_columns(source, taker), dst_ref=target.at[owner], send_sem=begin.at[place],
                    recv_sem=arrive.at[place, slot], device_id={"shard": taker}, device_id_type=MESH,
                )

            across(me, away).start()
            beside = send_to(hidden_columns(source, sib), target.at[me], sems, number, sib)
            beside.start()
            waits.append(beside)
            bulk.append((place, target, across))
            kept = hidden_columns(source, me)
        number += 3
        keep = pltpu.make_async_copy(kept, held[i], local.at[0, i])
        keep.start()
        keeps.append((keep, pltpu.make_async_copy(held[i], target.at[me], local.at[1, i])))
    for keep, store in keeps:
        keep.wait()
        store.start()
    for to_far, onward in forwards:
        to_far.wait_recv()
        onward.start()
    for to_far, onward in forwards:
        to_far.wait_send()
        onward.wait()
    for copy in waits:
        copy.wait()
    for keep, store in keeps:
        store.wait()
    for place, target, across in bulk:
        passing = relayed[place]
        passed = relays[2]

        @pl.when(away == 0)
        def _():
            for slot, owner in enumerate((far, diagonal)):
                across(owner, slot).wait_recv()
                if passing:
                    pass_on(target, passed, 2 * place + slot, owner).start()

    for place, target, across in bulk:
        passing = relayed[place]
        passed = relays[2]
        across(me, away).wait_send()
        if passing:
            @pl.when(away == 0)
            def _():
                for slot, owner in enumerate((far, diagonal)):
                    pass_on(target, passed, 2 * place + slot, owner).wait_send()

            @pl.when(away == 1)
            def _():
                for slot, owner in enumerate((far, diagonal)):
                    pass_on(target, passed, 2 * place + slot, owner).wait_recv()


def move(name, number, wholes, splits, relayed=()):
    inputs = list(wholes) + [array for array, _, _ in (*splits, *relayed)]
    shapes = [w.shape for w in wholes] + [part for _, part, _ in (*splits, *relayed)]
    out_shape = [jax.ShapeDtypeStruct((4,) + tuple(sh), v.dtype) for sh, v in zip(shapes, inputs)]
    scratch = [pltpu.VMEM(sh, v.dtype) for sh, v in zip(shapes, inputs)]
    scratch += [pltpu.SemaphoreType.DMA((2, 3 * len(inputs))), pltpu.SemaphoreType.DMA((2, len(inputs)))]
    if relayed:
        amount = len(relayed)
        scratch += [
            pltpu.SemaphoreType.DMA((amount,)), pltpu.SemaphoreType.DMA((amount, 2)),
            pltpu.SemaphoreType.DMA((2, 2 * amount)),
        ]
    return pl.pallas_call(
        functools.partial(move_kernel, len(wholes), [f for _, _, f in splits], [p for _, _, p in relayed]),
        in_specs=any_space(len(inputs)),
        out_specs=any_space(len(inputs)),
        out_shape=out_shape,
        scratch_shapes=scratch,
        compiler_params=pltpu.CompilerParams(
            collective_id=number, has_side_effects=True, vmem_limit_bytes=VMEM_LIMIT
        ),
        cost_estimate=pl.CostEstimate(
            flops=0, bytes_accessed=sum(4 * v.size * v.dtype.itemsize for v in inputs), transcendentals=0
        ),
        name=name,
    )(*inputs)


HIDDEN_WINDOW = 1664


def hidden_columns(ref, owner):
    return ref.at[:, pl.ds(pl.multiple_of(owner // 2 * 3200 + owner % 2 * 1536, LANES), HIDDEN_WINDOW)]


QUERY_WINDOW = 1024


def query_window(ref, owner):
    return ref.at[:, pl.ds(pl.multiple_of(owner // 2 * 1920 + owner % 2 * 896, LANES), QUERY_WINDOW)]


def latent_window(ref, owner):
    return ref.at[:, pl.ds(pl.multiple_of(owner * 1280, LANES), 1280)]


def first_move(query_down, latent_down, query_up, latent_up, segments, gate, up, count):
    if count != 4:
        gate, up = spread_hidden(gate, up, count)
        return (
            plain_gather(query_down), plain_gather(latent_down), pad_heads(spread(query_up, count)),
            spread(latent_up, count), plain_gather(segments), gate, up,
        )
    part = (gate.shape[0], HIDDEN_WINDOW)
    relayed = [(gate, part, True), (up, part, False)] if shared_links(count) else []
    down_q, down_kv, groups, up_q, up_kv, *hidden = move(
        "first_move", 7, [query_down, latent_down, segments],
        [(query_up, (query_up.shape[0], QUERY_WINDOW), query_window),
         (latent_up, (latent_up.shape[0], 1280), latent_window)],
        relayed,
    )
    merge = lambda value: value.reshape((-1,) + value.shape[2:])
    up_q = lax.dynamic_slice_in_dim(merge(up_q), lax.axis_index("shard") % 2 * 64, 960, 1)
    gate, up = hidden if relayed else spread_hidden(gate, up, count)
    return merge(down_q), merge(down_kv), pad_heads(up_q), merge(up_kv), merge(groups), gate, up


EXCHANGE_WIDTH = 1280


def last_move(grad_lat, gain_terms, query_part, latent_part, count):
    if count != 4:
        parts = (
            plain_gather(grad_lat), plain_gather(gain_terms), collect(cut_heads(query_part), count),
            collect(latent_part, count),
        )
        return parts, lambda parts: parts
    side = lambda value: value.transpose(1, 0, 2).reshape(value.shape[1], -1)
    same = lambda value: jnp.broadcast_to(value[None], (count,) + value.shape)
    wide = lambda value: jnp.pad(value, ((0, 0), (0, EXCHANGE_WIDTH - value.shape[1])))
    amount = gain_terms.shape[1]
    gain_rows = -(-amount // EXCHANGE_WIDTH)
    gain_rows += -gain_rows % 16
    gains = jnp.pad(gain_terms[0].astype(bf16), (0, gain_rows * EXCHANGE_WIDTH - amount)).reshape(gain_rows, -1)
    pieces = [
        query_part.reshape(count, -1, EXCHANGE_WIDTH), latent_part.reshape(count, -1, EXCHANGE_WIDTH),
        same(wide(grad_lat)), same(gains),
    ]
    got = lax.all_to_all(jnp.concatenate(pieces, axis=1), "shard", 0, 0, tiled=True)
    ends = [0]
    for piece in pieces:
        ends.append(ends[-1] + piece.shape[1])
    def finish(got):
        got_q, got_kv, lat, gains = (got[:, start:end] for start, end in zip(ends, ends[1:]))
        return (
            lat.reshape(-1, EXCHANGE_WIDTH)[:, :grad_lat.shape[1]],
            gains.reshape(count, -1)[:, :amount].astype(f32), cut_heads(side(got_q)), side(got_kv),
        )

    return got, finish


def place_kernel(*refs):
    me, core, sib, far = partners()
    *parts, out_ref = refs
    out_ref[...] = jnp.zeros_like(out_ref)
    for owner, part in zip((me, sib, far, far + 1 - 2 * core), parts):
        lanes = pl.ds(pl.multiple_of(owner // 2 * 3200 + owner % 2 * 1536, LANES), HIDDEN_WINDOW)
        out_ref[:, lanes] += part[...].astype(f32)


def head_lanes(value):
    return jnp.pad(value, ((0, 0), (NOPE, LANES - NOPE - ROPE)))


def layer_forward(hidden, own_tables, tables, gains, weights, passing, lacking, early):
    input_gain, query_gain, latent_gain, post_gain = gains
    down_both, query_up, latent_up, output_weight, gate_weight, up_weight, down_weight = weights
    scale_in = norm_scale(hidden)
    normed = (hidden * scale_in * input_gain).astype(bf16)
    down_q, down_kv = down_both
    latent_q = project(normed, down_q)
    latent_kv = project(normed, down_kv)
    latent = latent_kv[:, :KVRANK]
    scale_q = norm_scale(latent_q)
    scale_kv = norm_scale(latent)
    own_in = jnp.concatenate(
        [
            latent_q * scale_q * query_gain,
            latent * scale_kv * latent_gain,
            head_lanes(rotate(latent_kv[:, KVRANK:], *own_tables)),
        ],
        axis=1,
    ).astype(bf16)
    all_in = gather(own_in, 0, 384)
    all_in, early = together(all_in, early)
    if lacking is not None:
        early = plain_gather(early)
    query_in = all_in[:, :QRANK]
    kv_in = all_in[:, QRANK:QRANK + KVRANK]
    shared = all_in[:, QRANK + KVRANK:]
    attended, queries, keyval, logs = attend(
        project(query_in, query_up), project(kv_in, latent_up), shared, tables
    )
    attended, early = together(attended, early)
    if lacking:
        mixed, normed_two, up_weight = output_norm(attended, output_weight, hidden, post_gain, up_weight)
    else:
        mixed, normed_two = output_norm(attended, output_weight, hidden, post_gain)
    merge = lambda value: value.reshape(D, -1)
    gate = project(normed_two, merge(gate_weight))
    up = project(normed_two, merge(up_weight))
    activated = (jax.nn.silu(gate) * up).astype(bf16)
    def outputs(value):
        return down_project(value, down_weight, mixed, passing)

    kept = (hidden, scale_in, normed, latent_q, scale_q, latent, scale_kv, query_in, kv_in,
            shared, queries, keyval, logs, attended, mixed, normed_two, gate, up)
    return (outputs, activated, kept, merge(gate_weight), merge(up_weight), early)


def gate_backward(grad_act, gate, up):
    sigmoid = jax.nn.sigmoid(gate)
    grad_gate = (grad_act * up * sigmoid * (1.0 + gate * (1.0 - sigmoid))).astype(bf16)
    grad_up = (grad_act * gate * sigmoid).astype(bf16)
    return grad_gate, grad_up


def mlp_backward(grad_out, kept, gains, weights, gather_down, wanted):
    mixed, gate, up = kept[14], kept[16], kept[17]
    gate_weight, up_weight, down_weight = weights[4:]
    own_down = (residual_scale * grad_out).astype(bf16)
    grad_down, own_down, wanted = together(gather_down(own_down), own_down, wanted)
    grad_gate, grad_up = gate_backward(contract_cols(grad_down, down_weight), gate, up)
    grad_mixed, dgain_post, grad_branch = mlp_back(
        grad_gate, grad_up, gate_weight, up_weight, mixed, grad_out, gains[3]
    )
    return (grad_gate, grad_up), wanted, own_down, grad_mixed, dgain_post[0], grad_branch


def attention_backward(grad_mixed, grad_branch, kept, own_tables, tables, gains, weights, wanted):
    (hidden, scale_in, normed, latent_q, scale_q, latent, scale_kv, query_in, kv_in,
     shared, queries, keyval, logs, attended, mixed, normed_two, gate, up) = kept
    input_gain, query_gain, latent_gain, post_gain = gains
    down_both, query_up, latent_up, output_weight = weights[:4]
    cosine, sine = own_tables
    grad_attended = contract_cols(grad_branch, output_weight).astype(bf16)
    grad_query, grad_keyval, grad_shared = attend_back(
        queries, keyval, shared, tables, grad_attended, attended, logs
    )
    grad_in = latent_back(grad_query, grad_keyval, grad_shared, query_up, latent_up)
    grad_in, wanted = together(grad_in, wanted)
    grad_latent_q, dgain_query = norm_back(latent_q, scale_q, query_gain, grad_in[:, :QRANK])
    grad_latent, dgain_latent = norm_back(
        latent, scale_kv, latent_gain, grad_in[:, QRANK:QRANK + KVRANK]
    )
    start = QRANK + KVRANK + NOPE
    grad_shared = rotate(grad_in[:, start:start + ROPE], cosine, -sine)
    grad_lat = jnp.concatenate(
        [grad_latent_q, grad_latent, jnp.pad(grad_shared, ((0, 0), (0, LANES - ROPE)))], axis=1
    ).astype(bf16)
    down_q, down_kv = down_both
    grad_normed = contract_cols(grad_lat[:, :QRANK], down_q) + contract_cols(
        grad_lat[:, QRANK:QRANK + KVRANK + ROPE], down_kv
    )
    grad_hidden_norm, dgain_input = norm_back(hidden, scale_in, input_gain, grad_normed)
    grad_hidden = grad_mixed + grad_hidden_norm
    found = (grad_branch, grad_query, grad_keyval, grad_lat)
    return (grad_hidden, found, (dgain_input, dgain_query, dgain_latent), wanted)


def spread(weight, count):
    rows, columns = weight.shape
    parts = weight.reshape(rows, count, columns // count).transpose(1, 0, 2)
    return lax.all_to_all(parts, "shard", 0, 0, tiled=True).reshape(rows * count, columns // count)


def collect(grad, count):
    rows, columns = grad.shape
    parts = lax.all_to_all(
        grad.reshape(count, rows // count, columns), "shard", 0, 0, tiled=True
    )
    return parts.transpose(1, 0, 2).reshape(rows // count, columns * count)


def pad_heads(weight):
    rows, columns = weight.shape
    heads = weight.reshape(rows, columns // (NOPE + ROPE), NOPE + ROPE)
    return jnp.pad(heads, ((0, 0), (0, 0), (0, LANES - NOPE - ROPE))).reshape(rows, -1)


def cut_heads(grad):
    rows, columns = grad.shape
    heads = grad.reshape(rows, columns // LANES, LANES)[:, :, :NOPE + ROPE]
    return heads.reshape(rows, -1)


def swap(value, step):
    count = lax.axis_size("shard")
    return lax.ppermute(value, "shard", [(source, source ^ step) for source in range(count)])


def hidden_window(count):
    size = FF // count
    width = -(-size // LANES) * LANES
    starts = [owner * size // LANES * LANES for owner in range(count)]
    starts = [min(start, FF - width) for start in starts]
    return size, width, starts, [owner * size - start for owner, start in enumerate(starts)]


def take_at(table, place):
    return jnp.asarray(table, jnp.int32)[place]


def shared_links(count):
    return count == 4 and lax.axis_size("rep") % 2 == 0


def spread_hidden(gate, up, count):
    me = lax.axis_index("shard")
    size, width, starts, offsets = hidden_window(count)
    rows = gate.shape[0]
    results = []
    for weight in (gate, up):
        whole = jnp.zeros((rows * count, width), bf16)
        for step in range(count):
            owner = me ^ step
            part = lax.dynamic_slice(weight, (0, take_at(starts, owner)), (rows, width))
            if step:
                part = swap(part, step)
            whole = lax.dynamic_update_slice(whole, part, (owner * rows, 0))
        results.append(whole)
    return results


def window_rows(down, count):
    size, width, starts, offsets = hidden_window(count)
    whole = jnp.zeros((width, down.shape[1]), bf16)
    return lax.dynamic_update_slice(whole, down, (take_at(offsets, lax.axis_index("shard")), 0))


def chip_gradients_kernel(order_ref, two_ref, gate_ref, up_ref, gate_out, up_out, turned):
    tokens, rows = two_ref.shape
    piece = 512
    for start in range(0, tokens, piece):
        size = min(piece, tokens - start)
        turned[:, start:start + size] = two_ref[start:start + size, :].T
    width = gate_ref.shape[1]
    whole = width // piece
    for grad, out in ((gate_ref, gate_out), (up_ref, up_out)):
        def tile(step):
            lanes = columns(step, piece)
            out[0, :, lanes] = project(turned[...], grad[:, lanes]).astype(bf16)

        each(whole, False, tile)
        if whole * piece < width:
            out[0, :, whole * piece:] = project(turned[...], grad[:, whole * piece:]).astype(bf16)


def chip_gradients(two_all, grad_gate, grad_up):
    me, core, sib, far = partners()
    tokens, width = grad_gate.shape
    rows = D // 4
    held = pl.BlockSpec((tokens, width), lambda i, order: (0, 0), pipeline_mode=pl.Buffered(1))
    part = pl.BlockSpec((1, rows, width), lambda i, order: (i, 0, 0))
    gate, up = pl.pallas_call(
        chip_gradients_kernel,
        grid_spec=pltpu.PrefetchScalarGridSpec(
            num_scalar_prefetch=1,
            grid=(2,),
            in_specs=[pl.BlockSpec((tokens, rows), lambda i, order: (0, order[i])), held, held],
            out_specs=[part, part],
            scratch_shapes=[pltpu.VMEM((rows, tokens), bf16)],
        ),
        out_shape=[jax.ShapeDtypeStruct((2, rows, width), bf16)] * 2,
        compiler_params=pltpu.CompilerParams(vmem_limit_bytes=VMEM_LIMIT),
        name="chip_gradients",
    )(jnp.stack([sib, me]).astype(jnp.int32), two_all, grad_gate, grad_up)
    return [gate[0], up[0], gate[1], up[1]]


RECOMPUTE_ROWS = 384


def recompute_kernel(from_ref, own_ref, two_ref, down_ref, gate_ref, up_ref, rows_ref, act_own, gate_own, up_own,
                     act_out, gate_out, up_out):
    place = pl.program_id(0)
    width = gate_ref.shape[1]
    piece = 512

    @pl.when(own_ref[place] == 1)
    def _():
        act_out[...] = act_own[...]
        gate_out[...] = gate_own[...]
        up_out[...] = up_own[...]

    @pl.when(own_ref[place] == 0)
    def _():
        def tile(lanes, some_rows):
            gate = project(two_ref[...], gate_ref[:, lanes])
            up = project(two_ref[...], up_ref[:, lanes])
            grad = contract_cols(down_ref[...], rows_ref[some_rows, :])
            sigmoid = jax.nn.sigmoid(gate)
            silu = gate * sigmoid
            act_out[:, lanes] = (silu * up).astype(bf16)
            gate_out[:, lanes] = (grad * up * sigmoid * (1.0 + gate * (1.0 - sigmoid))).astype(bf16)
            up_out[:, lanes] = (grad * silu).astype(bf16)

        each(width // piece, False, lambda step: tile(columns(step, piece), columns(step, piece)))
        if width % piece:
            rest = slice(width // piece * piece, width)
            tile(rest, rest)


def recompute(two_all, down_all, gate_columns, up_columns, down_rows, own):
    tokens, width = two_all.shape[0], gate_columns.shape[1]
    group = own[0].shape[0]
    tile = RECOMPUTE_ROWS
    each_group = group // tile
    places = jnp.arange(tokens // tile, dtype=jnp.int32)
    is_own = places // each_group == lax.axis_index("rep")
    source = jnp.where(is_own, places % each_group, 0).astype(jnp.int32)
    whole = lambda value: pl.BlockSpec(value.shape, lambda i, a, b: (0, 0), pipeline_mode=pl.Buffered(1))
    wide = pl.BlockSpec((tile, D), lambda i, a, b: (i, 0))
    mine = pl.BlockSpec((tile, width), lambda i, a, b: (a[i], 0))
    part = pl.BlockSpec((tile, width), lambda i, a, b: (i, 0))
    return pl.pallas_call(
        recompute_kernel,
        grid_spec=pltpu.PrefetchScalarGridSpec(
            num_scalar_prefetch=2,
            grid=(tokens // tile,),
            in_specs=[wide, wide, whole(gate_columns), whole(up_columns), whole(down_rows), mine, mine, mine],
            out_specs=[part] * 3,
        ),
        out_shape=[jax.ShapeDtypeStruct((tokens, width), bf16)] * 3,
        compiler_params=pltpu.CompilerParams(vmem_limit_bytes=VMEM_LIMIT),
        name="recompute",
    )(source, is_own.astype(jnp.int32), two_all, down_all, gate_columns, up_columns, down_rows, *own)


def down_gradient_kernel(act_ref, down_ref, out_ref, turned):
    tokens, width = act_ref.shape
    size = out_ref.shape[0]
    piece = 512

    @pl.when(pl.program_id(0) == 0)
    def _():
        for start in range(0, tokens, piece):
            turned[:, start:start + piece] = act_ref[start:start + piece, :].T

    offset = lax.axis_index("shard") % 2 * (width - size)
    half = size // 2

    def tile(step):
        rows = pl.ds(pl.multiple_of(step * half, 16), half)
        out_ref[rows, :] = project(turned[pl.ds(pl.multiple_of(step * half + offset, 16), half), :], down_ref[...])

    each(2, False, tile)


def down_gradient(activated_all, down_all):
    tokens, width = activated_all.shape
    size, piece = FF // 4, 512
    return pl.pallas_call(
        down_gradient_kernel,
        grid=(D // piece,),
        in_specs=[pl.BlockSpec((tokens, width), lambda i: (0, 0), pipeline_mode=pl.Buffered(1)),
                  pl.BlockSpec((tokens, piece), lambda i: (0, i))],
        out_specs=pl.BlockSpec((size, piece), lambda i: (0, i)),
        out_shape=jax.ShapeDtypeStruct((size, D), f32),
        scratch_shapes=[pltpu.VMEM((width, tokens), bf16)],
        compiler_params=pltpu.CompilerParams(vmem_limit_bytes=VMEM_LIMIT),
        name="down_gradient",
    )(activated_all, down_all)


def owner_gradients(two_all, grad_gate, grad_up, owner, count):
    rows = D // count
    left = lax.dynamic_slice(two_all, (0, owner * rows), (two_all.shape[0], rows))
    return [contract_rows(left, grad).astype(bf16) for grad in (grad_gate, grad_up)]


def place_windows(both, count):
    size, width, starts, offsets = hidden_window(count)
    rows = both[0][0].shape[0]
    if count == 4:
        tile = 64
        return [
            pl.pallas_call(
                place_kernel,
                grid=(rows // tile,),
                in_specs=[pl.BlockSpec((tile, width), lambda i: (i, 0))] * 4,
                out_specs=pl.BlockSpec((tile, FF), lambda i: (i, 0)),
                out_shape=jax.ShapeDtypeStruct((rows, FF), f32),
                compiler_params=pltpu.CompilerParams(vmem_limit_bytes=VMEM_LIMIT),
                cost_estimate=pl.CostEstimate(flops=0, bytes_accessed=rows * FF * 8, transcendentals=0),
                name="place_windows",
            )(*some)
            for some in both
        ]
    me = lax.axis_index("shard")
    totals = []
    for parts in both:
        gathered = jnp.zeros((count, rows, width), bf16)
        for step, part in enumerate(parts):
            gathered = lax.dynamic_update_slice(gathered, part[None], (me ^ step, 0, 0))
        pieces = [gathered[owner, :, offset:offset + size] for owner, offset in enumerate(offsets)]
        totals.append(jnp.concatenate(pieces, axis=1).astype(f32))
    return totals


def together(*values):
    return lax.optimization_barrier(values)


def body(tokens, segment_ids, input_gain, query_gain, latent_gain, post_gain, query_down, query_up,
         latent_down, latent_up, output_weight, gate_weight, up_weight, down_weight, cotangent):
    at_start = lax.axis_index("section") == 0
    count = lax.axis_size("shard")
    size, width, starts, offsets = hidden_window(count)
    gains = (input_gain[0], query_gain[0], latent_gain[0], post_gain[0])
    down_q, down_kv, query_up_all, latent_up_all, groups, gate_columns, up_columns = first_move(
        query_down[0], latent_down[0], query_up[0], latent_up[0], segment_ids, gate_weight[0], up_weight[0], count
    )
    down_both = (down_q, down_kv)
    own_tables = tuple(t.reshape(-1, ROPE // 2) for t in slot_tables(segment_ids))
    tables = head_tables(groups)

    weights = (down_both, query_up_all, latent_up_all, output_weight[0], gate_columns, up_columns, down_weight[0])
    start = tokens.astype(f32)
    last = cotangent.astype(f32)
    last_down = (residual_scale * last).astype(bf16)
    outputs, activated, _, gate_columns, up_columns, all_last = layer_forward(
        start, own_tables, tables, gains, weights, True, shared_links(count), last_down
    )
    leaving, low, received, down_rows = outputs(activated)
    weights = weights[:4] + (gate_columns, up_columns, down_rows)
    entering = jnp.where(at_start, start, received.astype(f32))
    _, kept_activated, kept, _, _, _ = layer_forward(
        entering, own_tables, tables, gains, weights, False, None, all_last
    )

    (hidden, scale_in, normed, latent_q, scale_q, latent, scale_kv, query_in, kv_in,
     shared, queries, keyval, logs, attended, mixed, normed_two, gate, up) = kept
    rows = hidden.shape[0]
    own_two = lax.dynamic_slice_in_dim(normed_two, lax.axis_index("shard") * rows, rows, 0)
    _, _, _, grad_mixed, _, grad_branch = mlp_backward(last, kept, gains, weights, lambda own: all_last, at_start)
    grad_branch, own_two = together(grad_branch, own_two)
    two_all = lax.all_gather(own_two, ("rep", "shard"), axis=0, tiled=True)
    grad, _, _, _ = attention_backward(
        grad_mixed, grad_branch, kept, own_tables, tables, gains, weights, at_start
    )
    grad_low, kept_activated = together(grad.astype(bf16), kept_activated)
    returned = lax.ppermute(grad_low, "section", [(1, 0)])
    leaving, boundary = down_project(kept_activated, down_rows, mixed, False)
    incoming = jnp.where(at_start, returned.astype(f32), last)
    incoming, boundary = together(incoming, boundary)

    own_grads, two_all, own_down, grad_mixed, dgain_post, grad_branch = mlp_backward(
        incoming, kept, gains, weights, lambda own: gather(own, 1, 512), two_all
    )
    down_all = lax.all_gather(own_down, ("rep", "shard"), axis=0, tiled=True)
    part_output = contract_rows(attended, grad_branch).astype(bf16)
    grad_branch, part_output = together(grad_branch, part_output)

    grad, found, (dgain_input, dgain_query, dgain_latent), down_all = attention_backward(
        grad_mixed, grad_branch, kept, own_tables, tables, gains, weights, down_all
    )
    grad_branch, grad_query, grad_keyval, grad_lat = found
    gain_terms = jnp.concatenate([dgain_input, dgain_query, dgain_latent, dgain_post])[None]
    normed_rows = lax.all_to_all(
        normed.reshape(normed.shape[0], count, -1).transpose(1, 0, 2), "shard", 0, 0, tiled=True
    ).reshape(normed.shape[0] * count, -1)
    part_query = contract_rows(query_in, grad_query).astype(bf16)
    part_latent = contract_rows(kv_in, grad_keyval).astype(bf16)
    exchanged, exchange_end = last_move(grad_lat, gain_terms, part_query, part_latent, count)
    part_output, down_all, two_all, own_grads, normed_rows = together(
        part_output, down_all, two_all, own_grads, normed_rows
    )
    total_output = lax.psum(part_output, "rep")
    if count == 4:
        activated_all, grad_gate, grad_up = recompute(
            two_all, down_all, gate_columns, up_columns, down_rows, (kept_activated, *own_grads)
        )
    else:
        gate_all = project(two_all, gate_columns)
        up_all = project(two_all, up_columns)
        activated_all = (jax.nn.silu(gate_all) * up_all).astype(bf16)
        grad_gate, grad_up = gate_backward(contract_cols(down_all, down_rows), gate_all, up_all)
    def attention_shares(exchanged):
        lat_all, gains_all, part_query, part_latent = exchange_end(exchanged)
        part_down = contract_rows(normed_rows, lat_all[:, :QRANK + KVRANK + ROPE]).astype(bf16)
        part_gains = jnp.sum(gains_all, axis=0).astype(bf16)
        side = part_down.shape[1]
        gain_rows = -(-part_gains.shape[0] // side)
        part_gains = jnp.pad(part_gains, (0, gain_rows * side - part_gains.shape[0])).reshape(gain_rows, side)
        part_down = jnp.concatenate([part_down, part_gains], axis=0)
        return part_down, part_latent, part_query

    me = lax.axis_index("shard")
    if count == 4:
        away = [owner_gradients(two_all, grad_gate, grad_up, me ^ 2, count)]
        two_all, _, exchanged, total_output = together(two_all, away[0], exchanged, total_output)
        away.append(owner_gradients(two_all, grad_gate, grad_up, me ^ 3, count))
        brought = [[swap(away[step][i], 2 + step) for step in range(2)] for i in range(2)]
        shares = attention_shares(exchanged)
        two_all, _, *shares = together(two_all, away[1], *shares)
        total_down_both, total_latent, total_query = lax.psum(tuple(shares), "rep")
        near = chip_gradients(two_all, grad_gate, grad_up)
        activated_all, near[0], *brought[0] = together(activated_all, near[0], *brought[0])
        total_down = down_gradient(activated_all, down_all)
        hidden_parts = [[near[2 + i], swap(near[i], 1), *brought[i]] for i in range(2)]
    else:
        parts = [owner_gradients(two_all, grad_gate, grad_up, me ^ step, count) for step in range(count)]
        hidden_parts = [
            [swap(parts[step][i], step) if step else parts[step][i] for step in range(count)] for i in range(2)
        ]
        total_down_both, total_latent, total_query = lax.psum(attention_shares(exchanged), "rep")
        total_down = contract_rows(activated_all, down_all)
        total_down = lax.dynamic_slice_in_dim(total_down, take_at(offsets, me), size, 0)
    total_down, total_query, total_latent, hidden_parts[0][0] = together(
        total_down, total_query, total_latent, hidden_parts[0][0]
    )
    gain_rows = total_down_both.shape[0] - D // count
    gain_totals = total_down_both[-gain_rows:].reshape(-1).astype(f32)
    total_down_both = total_down_both[:-gain_rows].astype(f32)
    total_query, total_latent = total_query.astype(f32), total_latent.astype(f32)
    total_gate, total_up = place_windows(hidden_parts, count)
    first, second, third = D, D + QRANK, D + QRANK + KVRANK
    gain_totals = (gain_totals[:first], gain_totals[first:second], gain_totals[second:third], gain_totals[third:third + D])
    return (
        boundary[None],
        grad[None],
        gain_totals[0][None],
        gain_totals[1][None],
        gain_totals[2][None],
        gain_totals[3][None],
        total_down_both[None, :, :QRANK],
        total_query[None],
        total_down_both[None, :, QRANK:],
        total_latent[None],
        total_output.astype(f32)[None],
        total_gate[None],
        total_up[None],
        total_down[None],
    )


def solution(mesh):
    tokens = P(("rep", "shard"), None)
    gain = P("section", None)
    weight = P("section", "shard", None)
    out = P("section", ("rep", "shard"), None)
    return jax.shard_map(
        body,
        mesh=mesh,
        in_specs=(tokens, tokens) + (gain,) * 4 + (weight,) * 8 + (tokens,),
        out_specs=(out, out) + (gain,) * 4 + (weight,) * 8,
        check_vma=False,
    )
```

```python
import functools
import math

import jax
import jax.numpy as jnp
from jax import lax
from jax.experimental import pallas as pl
from jax.experimental.pallas import tpu as pltpu
from jax.sharding import PartitionSpec as P

D = 2560
HEADS = 40
NOPE = 64
ROPE = 32
VDIM = 64
QRANK = 768
KVRANK = 256
FF = 6400
SLOT = 96
LANES = 128

epsilon = 1e-05
residual_scale = 1.4 / math.sqrt(62.0)
masked_score = -1e30
score_scale = 1.0 / math.sqrt(NOPE + ROPE)
bf16 = jnp.bfloat16
f32 = jnp.float32


def norm_scale(value):
    return lax.rsqrt(jnp.mean(value * value, axis=-1, keepdims=True) + epsilon)


def norm_back(value, scale, gain, grad):
    weighted = grad * gain
    inner = jnp.mean(value * weighted, axis=-1, keepdims=True)
    grad_value = scale * weighted - value * (scale * scale * scale) * inner
    return (grad_value, jnp.sum(grad * value * scale, axis=0))


def rotate(value, cosine, sine):
    half = value.shape[-1] // 2
    front = value[..., :half]
    back = value[..., half:]
    return jnp.concatenate([front * cosine - back * sine, back * cosine + front * sine], axis=-1)


def slot_tables(segments):
    index = jnp.arange(SLOT, dtype=jnp.int32)
    first_index = jnp.sum((segments[:, None, :] < segments[:, :, None]).astype(jnp.int32), axis=-1)
    position = (index - first_index).astype(f32)
    freq = jnp.exp(jnp.arange(ROPE // 2, dtype=f32) * (-2.0 * math.log(10000.0) / ROPE))
    angle = position[..., None] * freq
    return (jnp.cos(angle), jnp.sin(angle))


def head_tables(segments):
    cosine, sine = slot_tables(segments)
    slots = segments.shape[0]
    ones = jnp.ones((slots, SLOT, NOPE), f32)
    tail = jnp.zeros((slots, SLOT, LANES - NOPE - ROPE), f32)
    half = jnp.zeros_like(sine)
    keep = jnp.concatenate([ones, cosine, cosine, tail], axis=-1)
    left = jnp.concatenate([0.0 * ones, -sine, half, tail], axis=-1)
    right = jnp.concatenate([0.0 * ones, half, sine, tail], axis=-1)
    index = jnp.arange(SLOT, dtype=jnp.int32)
    allowed = (segments[:, :, None] == segments[:, None, :]) & (index[None, :] <= index[:, None])
    mask = jnp.where(allowed, 0.0, masked_score).astype(f32)
    flat = lambda table: table.reshape(slots * SLOT, LANES)
    return (flat(keep), flat(left), flat(right), mask, mask.transpose(0, 2, 1))


def contract_rows(left, right):
    return lax.dot_general(left, right, (((0,), (0,)), ((), ())), preferred_element_type=f32)


def contract_cols(left, right):
    return lax.dot_general(left, right, (((1,), (1,)), ((), ())), preferred_element_type=f32)


def project(left, weight):
    return jnp.dot(left, weight, preferred_element_type=f32)


def low_lanes():
    return lax.broadcasted_iota(jnp.int32, (SLOT, LANES), 1) < NOPE


HEAD_GROUP = 5
HEAD_ROWS = 16


def attend_kernel(heads, q_ref, kv_ref, sh_ref, keep_ref, left_ref, right_ref, mask_ref,
                  att_ref, qo_ref, kvo_ref, log_ref):
    low = low_lanes()
    lane = lax.broadcasted_iota(jnp.int32, (SLOT, LANES), 1)
    shared = sh_ref[...].astype(f32)
    keep, left, right = keep_ref[...], left_ref[...], right_ref[...]
    mask = mask_ref[0]
    tallest = jnp.zeros((SLOT, LANES), f32)
    sums = jnp.ones((SLOT, LANES), f32)
    for first in range(0, heads, HEAD_GROUP):
        group = range(first, min(first + HEAD_GROUP, heads))
        scores, values = [], []
        for head in group:
            lanes = slice(head * LANES, (head + 1) * LANES)
            q = q_ref[:, lanes]
            q = q * keep + pltpu.roll(q, LANES - 16, 1) * left + pltpu.roll(q, 16, 1) * right
            q = q.astype(bf16)
            qo_ref[:, lanes] = q
            kv = kv_ref[:, lanes]
            kvo_ref[:, lanes] = kv.astype(bf16)
            k = jnp.where(low, kv, shared).astype(bf16)
            values.append(jnp.where(low, 1.0, kv).astype(bf16))
            scores.append(contract_cols(q, k) * score_scale + mask)
        tops = [jnp.max(score, axis=-1, keepdims=True) for score in scores]
        terms = [jnp.exp(score - top).astype(bf16) for score, top in zip(scores, tops)]
        outs = [project(term, value) for term, value in zip(terms, values)]
        for head, top, out in zip(group, tops, outs):
            turned = pltpu.roll(out, NOPE, 1)
            tallest = jnp.where(lane == head, top, tallest)
            sums = jnp.where(lane == head, out, sums)
            pair = (head // 2) * LANES
            if head % 2 == 0:
                att = turned / out
                att_ref[:, pair:pair + VDIM] = att[:, :VDIM].astype(bf16)
            else:
                att = out / turned
                att_ref[:, pair + VDIM:pair + LANES] = att[:, VDIM:].astype(bf16)
    log_ref[0] = (tallest + jnp.log(sums)).T[:HEAD_ROWS, :]


def attention_cost(tokens, heads, passes):
    return pl.CostEstimate(
        flops=passes * tokens * heads * SLOT * LANES * 20, bytes_accessed=tokens * heads * LANES * 12,
        transcendentals=tokens * heads * SLOT,
    )


def attend(query, keyval, shared, tables):
    tokens = query.shape[0]
    heads = query.shape[1] // LANES
    wide = pl.BlockSpec((SLOT, heads * LANES), lambda s: (s, 0))
    one = pl.BlockSpec((SLOT, LANES), lambda s: (s, 0))
    square = pl.BlockSpec((1, SLOT, SLOT), lambda s: (s, 0, 0))
    return pl.pallas_call(
        functools.partial(attend_kernel, heads),
        grid=(tokens // SLOT,),
        in_specs=[wide, wide, one, one, one, one, square],
        out_specs=[pl.BlockSpec((SLOT, heads * VDIM), lambda s: (s, 0)), wide, wide,
                   pl.BlockSpec((1, HEAD_ROWS, SLOT), lambda s: (s, 0, 0))],
        out_shape=[
            jax.ShapeDtypeStruct((tokens, heads * VDIM), bf16),
            jax.ShapeDtypeStruct(query.shape, bf16),
            jax.ShapeDtypeStruct(keyval.shape, bf16),
            jax.ShapeDtypeStruct((tokens // SLOT, HEAD_ROWS, SLOT), f32),
        ],
        cost_estimate=attention_cost(tokens, heads, 4),
        name="attend",
    )(query, keyval, shared, *tables[:4])


def attend_back_kernel(heads, q_ref, kv_ref, sh_ref, keep_ref, left_ref, right_ref, mask_ref,
                       ga_ref, att_ref, log_ref, gq_ref, gkv_ref, gsh_ref):
    low = low_lanes()
    shared = sh_ref[...].astype(f32)
    keep, left, right = keep_ref[...], left_ref[...], right_ref[...]
    mask = mask_ref[0]
    total = jnp.zeros((SLOT, LANES), f32)
    product = ga_ref[...].astype(f32) * att_ref[...].astype(f32)
    high = product.astype(bf16)
    rest = (product - high.astype(f32)).astype(bf16)
    shape = (HEAD_ROWS, product.shape[1])
    chosen = lax.broadcasted_iota(jnp.int32, shape, 1) // VDIM == lax.broadcasted_iota(jnp.int32, shape, 0)
    chosen = jnp.where(chosen, 1.0, 0.0).astype(bf16)
    inner = contract_cols(chosen, high) + contract_cols(chosen, rest)
    for first in range(0, heads, HEAD_GROUP):
        group = range(first, min(first + HEAD_GROUP, heads))
        queries, keys, grads, scores, grad_probs = [], [], [], [], []
        for head in group:
            lanes = slice(head * LANES, (head + 1) * LANES)
            q = q_ref[:, lanes]
            kvb = kv_ref[:, lanes]
            k = jnp.where(low, kvb.astype(f32), shared).astype(bf16)
            if head % 2 == 0 and head == heads - 1:
                ga = ga_ref[:, head * VDIM:(head + 1) * VDIM].astype(f32)
                ga = jnp.concatenate([jnp.zeros_like(ga), ga], axis=1)
            else:
                start = (head // 2) * LANES
                ga = ga_ref[:, start:start + LANES].astype(f32)
                if head % 2 == 0:
                    ga = pltpu.roll(ga, NOPE, 1)
                ga = jnp.where(low, 0.0, ga)
            ga = ga.astype(bf16)
            queries.append(q)
            keys.append(k)
            grads.append(ga)
            scores.append(contract_cols(k, q) * score_scale + mask)
            grad_probs.append(contract_cols(kvb, ga))
        probs = [jnp.exp(score - log_ref[0, head:head + 1, :]) for head, score in zip(group, scores)]
        changes = [
            (prob * (grad - inner[head:head + 1, :]) * score_scale).astype(bf16)
            for head, prob, grad in zip(group, probs, grad_probs)
        ]
        grad_values = [project(prob.astype(bf16), ga) for prob, ga in zip(probs, grads)]
        grad_keys = [project(change, q) for change, q in zip(changes, queries)]
        grad_queries = [contract_rows(change, k) for change, k in zip(changes, keys)]
        for head, gv, gk, gq in zip(group, grad_values, grad_keys, grad_queries):
            lanes = slice(head * LANES, (head + 1) * LANES)
            gq = gq * keep - pltpu.roll(gq, LANES - 16, 1) * left - pltpu.roll(gq, 16, 1) * right
            gq_ref[:, lanes] = gq.astype(bf16)
            total = total + gk
            gkv_ref[:, lanes] = jnp.where(low, gk, gv).astype(bf16)
    gsh_ref[...] = total


def attend_back(query, keyval, shared, tables, grad_attended, attended, logs):
    tokens = query.shape[0]
    heads = query.shape[1] // LANES
    wide = pl.BlockSpec((SLOT, heads * LANES), lambda s: (s, 0))
    one = pl.BlockSpec((SLOT, LANES), lambda s: (s, 0))
    half = pl.BlockSpec((SLOT, heads * VDIM), lambda s: (s, 0))
    return pl.pallas_call(
        functools.partial(attend_back_kernel, heads),
        grid=(tokens // SLOT,),
        in_specs=[wide, wide, one, one, one, one, pl.BlockSpec((1, SLOT, SLOT), lambda s: (s, 0, 0)),
                  half, half, pl.BlockSpec((1, HEAD_ROWS, SLOT), lambda s: (s, 0, 0))],
        out_specs=[wide, wide, one],
        out_shape=[
            jax.ShapeDtypeStruct(query.shape, bf16),
            jax.ShapeDtypeStruct(keyval.shape, bf16),
            jax.ShapeDtypeStruct((tokens, LANES), f32),
        ],
        cost_estimate=attention_cost(tokens, heads, 10),
        name="attend_back",
    )(query, keyval, shared, *tables[:3], tables[4], grad_attended, attended, logs)


MESH = pl.DeviceIdType.MESH
VMEM_LIMIT = 60 * 1024 * 1024


def partners():
    me = lax.axis_index("shard")
    core = me % 2
    return me, core, me + 1 - 2 * core, (me + 2) % 4


def greet(devices):
    barrier = pltpu.get_barrier_semaphore()
    for device in devices:
        pl.semaphore_signal(barrier, inc=1, device_id=device, device_id_type=MESH)
    pl.semaphore_wait(barrier, len(devices))


def columns(step, width):
    return pl.ds(pl.multiple_of(step * width, LANES), width)


def rows_at(start, rows):
    return pl.ds(pl.multiple_of(start * rows, 16), rows)


def remote(source, target, sems, step, device):
    return pltpu.make_async_remote_copy(
        src_ref=source, dst_ref=target, send_sem=sems.at[0, step], recv_sem=sems.at[1, step],
        device_id={"shard": device}, device_id_type=MESH,
    )


def exchange_scratch(rows, steps, width):
    part = pltpu.VMEM((steps, rows, width), bf16)
    return [part] * 6 + [
        pltpu.VMEM((steps, rows, width), f32),
        pltpu.VMEM((2 * rows, width), f32),
        pltpu.SemaphoreType.DMA((3, 2, steps)),
    ]


def each(steps, unrolled, do):
    if unrolled:
        for step in range(steps):
            do(step)
    else:
        def again(step, carry):
            do(step)
            return carry
        lax.fori_loop(0, steps, again, 0)


def sum_scatter(rows, steps, unrolled, partial, scratch, use):
    (to_sib, from_sib, to_far, from_far, own_sib, own_from, hold, stage, sems) = scratch
    me, core, sib, far = partners()
    mine = rows_at(core, rows)
    other = rows_at(1 - core, rows)

    def first(step):
        return remote(to_sib.at[step], from_sib.at[step], sems.at[0], step, sib)

    def across(step):
        return remote(to_far.at[step], from_far.at[step], sems.at[1], step, far)

    def beside(step):
        return remote(own_sib.at[step], own_from.at[step], sems.at[2], step, sib)

    def far_part(step):
        stage[...] = partial(rows_at(far // 2, 2 * rows), step)
        to_sib[step] = stage[other, :].astype(bf16)
        first(step).start()
        hold[step] = stage[mine, :]

    def far_send(step):
        first(step).wait_recv()
        to_far[step] = (hold[step] + from_sib[step].astype(f32)).astype(bf16)
        across(step).start()

    def far_step(step):
        far_part(step)
        if unrolled:
            if step > 0:
                far_send(step - 1)
        else:
            @pl.when(step > 0)
            def _():
                far_send(step - 1)

    each(steps, unrolled, far_step)
    far_send(steps - 1)

    def near_part(step):
        stage[...] = partial(rows_at(me // 2, 2 * rows), step)
        own_sib[step] = stage[other, :].astype(bf16)
        beside(step).start()
        hold[step] = stage[mine, :]

    each(steps, unrolled, near_part)

    def finish(step):
        beside(step).wait_recv()
        across(step).wait_recv()
        use(step, hold[step] + own_from[step].astype(f32) + from_far[step].astype(f32))

    each(steps, unrolled, finish)

    def settle(step):
        first(step).wait_send()
        across(step).wait_send()
        beside(step).wait_send()

    each(steps, unrolled, settle)


def spread_rows(rows, steps, width, place, all_ref, sems):
    me, core, sib, far = partners()

    def part(owner, step):
        return all_ref.at[rows_at(owner, rows), columns(step, width)]

    def across(step):
        return remote(part(me, step), part(me, step), sems.at[0], step, far)

    def beside(step):
        return remote(part(me, step), part(me, step), sems.at[1], step, sib)

    def onward(step):
        return remote(part(far, step), part(far, step), sems.at[2], step, sib)

    def send(step):
        place(step)
        across(step).start()
        beside(step).start()

    each(steps, False, send)

    def forward(step):
        across(step).wait_recv()
        onward(step).start()

    each(steps, False, forward)

    def settle(step):
        beside(step).wait_recv()
        onward(step).wait_recv()
        across(step).wait_send()
        beside(step).wait_send()
        onward(step).wait_send()

    each(steps, False, settle)


def vmem(count):
    return [pl.BlockSpec(memory_space=pltpu.VMEM)] * count


def comm_call(kernel, name, number, inputs, out_shape, scratch, flops=0, aliased={}):
    nbytes = sum(v.size * v.dtype.itemsize for v in (*inputs, *out_shape))
    return pl.pallas_call(
        kernel,
        in_specs=vmem(len(inputs) - len(aliased)) + any_space(len(aliased)),
        out_specs=vmem(len(out_shape) - len(aliased)) + any_space(len(aliased)),
        out_shape=out_shape,
        scratch_shapes=scratch,
        input_output_aliases=aliased,
        compiler_params=pltpu.CompilerParams(
            collective_id=number, has_side_effects=True, vmem_limit_bytes=VMEM_LIMIT
        ),
        cost_estimate=pl.CostEstimate(flops=0, bytes_accessed=0 * nbytes, transcendentals=0),
        name=name,
    )(*inputs)


def shape(rows, width, dtype):
    return jax.ShapeDtypeStruct((rows, width), dtype)


def gather_kernel(steps, width, own_ref, all_ref, sems):
    rows = own_ref.shape[0]
    me, core, sib, far = partners()
    greet([{"shard": sib}, {"shard": far}])

    def place(step):
        all_ref[rows_at(me, rows), columns(step, width)] = own_ref[:, columns(step, width)]

    spread_rows(rows, steps, width, place, all_ref, sems)


def gather(value, number, width):
    if lax.axis_size("shard") != 4:
        return lax.all_gather(value, "shard", axis=0, tiled=True)
    rows, total = value.shape
    steps = total // width
    (out,) = comm_call(
        functools.partial(gather_kernel, steps, width), "gather_rows", number, [value],
        [shape(4 * rows, total, bf16)], [pltpu.SemaphoreType.DMA((3, 2, steps))],
    )
    return out


def plain_gather(value):
    return lax.all_gather(value, "shard", axis=0, tiled=True)


def plain_scatter(value):
    return lax.psum_scatter(value.astype(bf16), "shard", scatter_dimension=0, tiled=True).astype(f32)


MODEL_STEP = 512


def output_kernel(relaying, att_ref, weight_ref, hidden_ref, gain_ref, *refs):
    if relaying:
        _, mixed_ref, two_ref, up_ref, *scratch, passed = refs
    else:
        mixed_ref, two_ref, *scratch = refs
    *parts, sems = scratch
    rows = hidden_ref.shape[0]
    width = MODEL_STEP
    steps = D // width
    me, core, sib, far = partners()
    devices = [{"shard": sib}, {"shard": far}]
    if relaying:
        partner, away = replica_pair()
        devices.append({"rep": partner})
    greet(devices)
    if relaying:
        @pl.when(away == 0)
        def _():
            for slot, owner in enumerate((far, far + 1 - 2 * core)):
                pass_on(up_ref, passed, slot, owner).start()

    def partial(where, step):
        return project(att_ref[where, :], weight_ref[:, columns(step, width)])

    def use(step, total):
        lanes = columns(step, width)
        mixed_ref[:, lanes] = hidden_ref[:, lanes] + residual_scale * total

    sum_scatter(rows, steps, False, partial, parts, use)
    mixed = mixed_ref[...]
    scale = norm_scale(mixed)

    def place(step):
        lanes = columns(step, width)
        two_ref[rows_at(me, rows), lanes] = (mixed_ref[:, lanes] * scale * gain_ref[:, lanes]).astype(bf16)

    spread_rows(rows, steps, width, place, two_ref, sems)
    if relaying:
        @pl.when(away == 0)
        def _():
            for slot, owner in enumerate((far, far + 1 - 2 * core)):
                pass_on(up_ref, passed, slot, owner).wait_send()

        @pl.when(away == 1)
        def _():
            for slot, owner in enumerate((far, far + 1 - 2 * core)):
                pass_on(up_ref, passed, slot, owner).wait_recv()


def output_norm(attended, weight, hidden, gain, up=None):
    if lax.axis_size("shard") != 4:
        mixed = hidden + residual_scale * plain_scatter(project(attended, weight))
        return mixed, plain_gather((mixed * norm_scale(mixed) * gain).astype(bf16))
    rows = hidden.shape[0]
    steps = D // MODEL_STEP
    scratch = exchange_scratch(rows, steps, MODEL_STEP) + [pltpu.SemaphoreType.DMA((3, 2, steps))]
    inputs = [attended, weight, hidden, gain[None]]
    outputs = [shape(rows, D, f32), shape(4 * rows, D, bf16)]
    flops = 2 * attended.size * D
    if up is None:
        return comm_call(functools.partial(output_kernel, False), "output_norm", 2, inputs, outputs, scratch, flops)
    return comm_call(
        functools.partial(output_kernel, True), "output_norm", 9, inputs + [up],
        outputs + [jax.ShapeDtypeStruct(up.shape, bf16)], scratch + [pltpu.SemaphoreType.DMA((2, 2))], flops,
        aliased={4: 2},
    )


def down_kernel(passing, act_ref, given_ref, mixed_ref, out_ref, low_ref, *scratch):
    rows = mixed_ref.shape[0]
    width = MODEL_STEP
    steps = D // width
    me, core, sib, far = partners()
    devices = [{"shard": sib}, {"shard": far}]
    weight_ref = given_ref
    if passing:
        got_ref, weight_ref, *parts, sems = scratch
        size, more = given_ref.shape[0], weight_ref.shape[0] - given_ref.shape[0]
        weight_ref[pl.ds(pl.multiple_of((1 - core) * size, 16), more), :] = jnp.zeros((more, D), bf16)
        piece = 64

        def fill(step):
            source = pl.ds(pl.multiple_of(step * piece, 16), piece)
            target = pl.ds(pl.multiple_of(step * piece + core * more, 16), piece)
            weight_ref[target, :] = given_ref[source, :]

        each(size // piece, False, fill)
        section = lax.axis_index("section")
        devices.append({"section": 1 - section})
    else:
        parts = scratch
    greet(devices)

    def onward(step):
        lanes = columns(step, width)
        return pltpu.make_async_remote_copy(
            src_ref=low_ref.at[:, lanes], dst_ref=got_ref.at[:, lanes], send_sem=sems.at[0, step],
            recv_sem=sems.at[1, step], device_id={"section": 1 - section}, device_id_type=MESH,
        )

    def partial(where, step):
        return project(act_ref[where, :], weight_ref[:, columns(step, width)])

    def use(step, total):
        lanes = columns(step, width)
        out = mixed_ref[:, lanes] + residual_scale * total
        out_ref[:, lanes] = out
        low_ref[:, lanes] = out.astype(bf16)
        if passing:
            onward(step).start()

    sum_scatter(rows, steps, False, partial, parts, use)
    if passing:
        each(steps, False, lambda step: onward(step).wait())


def down_project(activated, weight, mixed, passing):
    count = lax.axis_size("shard")
    if count != 4:
        if passing:
            weight = window_rows(weight, count)
        output = mixed + residual_scale * plain_scatter(project(activated, weight))
        low = output.astype(bf16)
        return (output, low) + ((lax.ppermute(low, "section", [(0, 1)]), weight) if passing else ())
    rows = mixed.shape[0]
    steps = D // MODEL_STEP
    scratch = exchange_scratch(rows, steps, MODEL_STEP)
    return comm_call(
        functools.partial(down_kernel, passing), "down_project", 3 if passing else 4,
        [activated, weight, mixed],
        [shape(rows, D, f32)] + [shape(rows, D, bf16)] * (2 if passing else 1)
        + [shape(HIDDEN_WINDOW, D, bf16)] * passing,
        scratch + ([pltpu.SemaphoreType.DMA((2, steps))] if passing else []),
        flops=2 * activated.size * D,
    )


def mlp_back_kernel(gate_ref, up_ref, gate_weight_ref, up_weight_ref, mixed_ref, grad_ref, gain_ref, out_ref, dgain_ref, branch_ref,
                    *scratch):
    *parts, sems = scratch
    rows = mixed_ref.shape[0]
    width = MODEL_STEP
    steps = D // width
    me, core, sib, far = partners()
    greet([{"shard": sib}, {"shard": far}])

    def partial(where, step):
        rows_of = columns(step, width)
        return contract_cols(gate_ref[where, :], gate_weight_ref[rows_of, :]) + contract_cols(
            up_ref[where, :], up_weight_ref[rows_of, :]
        )

    def use(step, total):
        out_ref[:, columns(step, width)] = total

    sum_scatter(rows, steps, False, partial, parts, use)
    mixed = mixed_ref[...]
    scale = norm_scale(mixed)
    inner = jnp.mean(mixed * out_ref[...] * gain_ref[...], axis=-1, keepdims=True)
    slope = scale * scale * scale * inner

    def place(step):
        lanes = columns(step, width)
        grad, value = out_ref[:, lanes], mixed_ref[:, lanes]
        dgain_ref[:, lanes] = jnp.sum(grad * value * scale, axis=0, keepdims=True)
        total = grad_ref[:, lanes] + scale * (grad * gain_ref[:, lanes]) - value * slope
        out_ref[:, lanes] = total
        branch_ref[rows_at(me, rows), lanes] = (residual_scale * total).astype(bf16)

    spread_rows(rows, steps, width, place, branch_ref, sems)


def mlp_back(grad_gate, grad_up, gate_weight, up_weight, mixed, grad_out, gain):
    if lax.axis_size("shard") != 4:
        grad = plain_scatter(contract_cols(grad_gate, gate_weight) + contract_cols(grad_up, up_weight))
        back, dgain = norm_back(mixed, norm_scale(mixed), gain, grad)
        grad_mixed = grad_out + back
        return grad_mixed, dgain[None], plain_gather((residual_scale * grad_mixed).astype(bf16))
    rows = mixed.shape[0]
    steps = D // MODEL_STEP
    return comm_call(
        mlp_back_kernel, "mlp_back", 5,
        [grad_gate, grad_up, gate_weight, up_weight, mixed, grad_out, gain[None]],
        [shape(rows, D, f32), shape(1, D, f32), shape(4 * rows, D, bf16)],
        exchange_scratch(rows, steps, MODEL_STEP) + [pltpu.SemaphoreType.DMA((3, 2, steps))],
        flops=4 * grad_gate.size * D,
    )


LATENT_STEP = 256


def latent_back_kernel(gq_ref, gkv_ref, gsh_ref, qup_ref, lup_ref, out_ref, *scratch):
    rows = out_ref.shape[0]
    width = LATENT_STEP
    me, core, sib, far = partners()
    greet([{"shard": sib}, {"shard": far}])

    def partial(where, step):
        if step < QRANK // width:
            return contract_cols(gq_ref[where, :], qup_ref[step * width:(step + 1) * width, :])
        if step == QRANK // width:
            return contract_cols(gkv_ref[where, :], lup_ref[...])
        shared = gsh_ref[where, :]
        return jnp.concatenate([shared, jnp.zeros_like(shared)], axis=1)

    def use(step, total):
        out_ref[:, step * width:(step + 1) * width] = total

    sum_scatter(rows, out_ref.shape[1] // width, True, partial, scratch, use)


def latent_back(grad_query, grad_keyval, grad_shared, query_up, latent_up):
    if lax.axis_size("shard") != 4:
        return plain_scatter(
            jnp.concatenate(
                [contract_cols(grad_query, query_up), contract_cols(grad_keyval, latent_up), grad_shared],
                axis=1,
            )
        )
    rows = grad_query.shape[0] // 4
    steps = QRANK // LATENT_STEP + 2
    (out,) = comm_call(
        latent_back_kernel, "latent_back", 6, [grad_query, grad_keyval, grad_shared, query_up, latent_up],
        [shape(rows, steps * LATENT_STEP, f32)], exchange_scratch(rows, steps, LATENT_STEP),
        flops=2 * grad_query.size * QRANK + 2 * grad_keyval.size * KVRANK,
    )
    return out


def any_space(count):
    return [pl.BlockSpec(memory_space=pl.ANY)] * count


def pair(value, index):
    return value.at[0, index], value.at[1, index]


def send_to(source, target, sems, index, device):
    send, receive = pair(sems, index)
    return pltpu.make_async_remote_copy(
        src_ref=source, dst_ref=target, send_sem=send, recv_sem=receive,
        device_id={"shard": device}, device_id_type=MESH,
    )


def replica_pair():
    replica = lax.axis_index("rep")
    return replica + 1 - 2 * (replica % 2), (lax.axis_index("shard") + replica) % 2


def pass_on(target, sems, step, owner):
    partner, _ = replica_pair()
    return pltpu.make_async_remote_copy(
        src_ref=target.at[owner], dst_ref=target.at[owner], send_sem=sems.at[0, step], recv_sem=sems.at[1, step],
        device_id={"rep": partner}, device_id_type=MESH,
    )


def move_kernel(whole, split, relayed, *refs):
    amount = whole + len(split) + len(relayed)
    inputs, outputs, held = refs[:amount], refs[amount:2 * amount], refs[2 * amount:3 * amount]
    sems, local, *relays = refs[3 * amount:]
    me, core, sib, far = partners()
    diagonal = far + 1 - 2 * core
    devices = [{"shard": sib}, {"shard": far}, {"shard": diagonal}]
    if relayed:
        partner, away = replica_pair()
        devices.append({"rep": partner})
    greet(devices)
    waits, forwards, keeps, bulk = [], [], [], []
    number = 0
    for i, (source, target) in enumerate(zip(inputs, outputs)):
        if i < whole:
            to_far = send_to(source, target.at[me], sems, number, far)
            to_sib = send_to(source, target.at[me], sems, number + 1, sib)
            onward = send_to(target.at[far], target.at[far], sems, number + 2, sib)
            to_far.start()
            to_sib.start()
            forwards.append((to_far, onward))
            waits.append(to_sib)
            kept = source
        elif i < whole + len(split):
            part = split[i - whole]
            for j, device in enumerate((far, diagonal, sib)):
                copy = send_to(part(source, device), target.at[me], sems, number + j, device)
                copy.start()
                waits.append(copy)
            kept = part(source, me)
        else:
            begin, arrive, passed = relays
            place = i - whole - len(split)
            taker = far // 2 * 2 + lax.axis_index("rep") % 2

            def across(owner, slot):
                return pltpu.make_async_remote_copy(
                    src_ref=hidden_columns(source, taker), dst_ref=target.at[owner], send_sem=begin.at[place],
                    recv_sem=arrive.at[place, slot], device_id={"shard": taker}, device_id_type=MESH,
                )

            across(me, away).start()
            beside = send_to(hidden_columns(source, sib), target.at[me], sems, number, sib)
            beside.start()
            waits.append(beside)
            bulk.append((place, target, across))
            kept = hidden_columns(source, me)
        number += 3
        keep = pltpu.make_async_copy(kept, held[i], local.at[0, i])
        keep.start()
        keeps.append((keep, pltpu.make_async_copy(held[i], target.at[me], local.at[1, i])))
    for keep, store in keeps:
        keep.wait()
        store.start()
    for to_far, onward in forwards:
        to_far.wait_recv()
        onward.start()
    for to_far, onward in forwards:
        to_far.wait_send()
        onward.wait()
    for copy in waits:
        copy.wait()
    for keep, store in keeps:
        store.wait()
    for place, target, across in bulk:
        passing = relayed[place]
        passed = relays[2]

        @pl.when(away == 0)
        def _():
            for slot, owner in enumerate((far, diagonal)):
                across(owner, slot).wait_recv()
                if passing:
                    pass_on(target, passed, 2 * place + slot, owner).start()

    for place, target, across in bulk:
        passing = relayed[place]
        passed = relays[2]
        across(me, away).wait_send()
        if passing:
            @pl.when(away == 0)
            def _():
                for slot, owner in enumerate((far, diagonal)):
                    pass_on(target, passed, 2 * place + slot, owner).wait_send()

            @pl.when(away == 1)
            def _():
                for slot, owner in enumerate((far, diagonal)):
                    pass_on(target, passed, 2 * place + slot, owner).wait_recv()


def move(name, number, wholes, splits, relayed=()):
    inputs = list(wholes) + [array for array, _, _ in (*splits, *relayed)]
    shapes = [w.shape for w in wholes] + [part for _, part, _ in (*splits, *relayed)]
    out_shape = [jax.ShapeDtypeStruct((4,) + tuple(sh), v.dtype) for sh, v in zip(shapes, inputs)]
    scratch = [pltpu.VMEM(sh, v.dtype) for sh, v in zip(shapes, inputs)]
    scratch += [pltpu.SemaphoreType.DMA((2, 3 * len(inputs))), pltpu.SemaphoreType.DMA((2, len(inputs)))]
    if relayed:
        amount = len(relayed)
        scratch += [
            pltpu.SemaphoreType.DMA((amount,)), pltpu.SemaphoreType.DMA((amount, 2)),
            pltpu.SemaphoreType.DMA((2, 2 * amount)),
        ]
    return pl.pallas_call(
        functools.partial(move_kernel, len(wholes), [f for _, _, f in splits], [p for _, _, p in relayed]),
        in_specs=any_space(len(inputs)),
        out_specs=any_space(len(inputs)),
        out_shape=out_shape,
        scratch_shapes=scratch,
        compiler_params=pltpu.CompilerParams(
            collective_id=number, has_side_effects=True, vmem_limit_bytes=VMEM_LIMIT
        ),
        cost_estimate=pl.CostEstimate(
            flops=0, bytes_accessed=sum(4 * v.size * v.dtype.itemsize for v in inputs), transcendentals=0
        ),
        name=name,
    )(*inputs)


HIDDEN_WINDOW = 1664


def hidden_columns(ref, owner):
    return ref.at[:, pl.ds(pl.multiple_of(owner // 2 * 3200 + owner % 2 * 1536, LANES), HIDDEN_WINDOW)]


QUERY_WINDOW = 1024


def query_window(ref, owner):
    return ref.at[:, pl.ds(pl.multiple_of(owner // 2 * 1920 + owner % 2 * 896, LANES), QUERY_WINDOW)]


def latent_window(ref, owner):
    return ref.at[:, pl.ds(pl.multiple_of(owner * 1280, LANES), 1280)]


def first_move(query_down, latent_down, query_up, latent_up, segments, gate, up, count):
    if count != 4:
        gate, up = spread_hidden(gate, up, count)
        return (
            plain_gather(query_down), plain_gather(latent_down), pad_heads(spread(query_up, count)),
            spread(latent_up, count), plain_gather(segments), gate, up,
        )
    part = (gate.shape[0], HIDDEN_WINDOW)
    relayed = [(gate, part, True), (up, part, False)] if shared_links(count) else []
    down_q, down_kv, groups, up_q, up_kv, *hidden = move(
        "first_move", 7, [query_down, latent_down, segments],
        [(query_up, (query_up.shape[0], QUERY_WINDOW), query_window),
         (latent_up, (latent_up.shape[0], 1280), latent_window)],
        relayed,
    )
    merge = lambda value: value.reshape((-1,) + value.shape[2:])
    up_q = lax.dynamic_slice_in_dim(merge(up_q), lax.axis_index("shard") % 2 * 64, 960, 1)
    gate, up = hidden if relayed else spread_hidden(gate, up, count)
    return merge(down_q), merge(down_kv), pad_heads(up_q), merge(up_kv), merge(groups), gate, up


EXCHANGE_WIDTH = 1280


def last_move(grad_lat, gain_terms, query_part, latent_part, count):
    if count != 4:
        parts = (
            plain_gather(grad_lat), plain_gather(gain_terms), collect(cut_heads(query_part), count),
            collect(latent_part, count),
        )
        return parts, lambda parts: parts
    side = lambda value: value.transpose(1, 0, 2).reshape(value.shape[1], -1)
    same = lambda value: jnp.broadcast_to(value[None], (count,) + value.shape)
    wide = lambda value: jnp.pad(value, ((0, 0), (0, EXCHANGE_WIDTH - value.shape[1])))
    amount = gain_terms.shape[1]
    gain_rows = -(-amount // EXCHANGE_WIDTH)
    gain_rows += -gain_rows % 16
    gains = jnp.pad(gain_terms[0].astype(bf16), (0, gain_rows * EXCHANGE_WIDTH - amount)).reshape(gain_rows, -1)
    pieces = [
        query_part.reshape(count, -1, EXCHANGE_WIDTH), latent_part.reshape(count, -1, EXCHANGE_WIDTH),
        same(wide(grad_lat)), same(gains),
    ]
    got = lax.all_to_all(jnp.concatenate(pieces, axis=1), "shard", 0, 0, tiled=True)
    ends = [0]
    for piece in pieces:
        ends.append(ends[-1] + piece.shape[1])
    def finish(got):
        got_q, got_kv, lat, gains = (got[:, start:end] for start, end in zip(ends, ends[1:]))
        return (
            lat.reshape(-1, EXCHANGE_WIDTH)[:, :grad_lat.shape[1]],
            gains.reshape(count, -1)[:, :amount].astype(f32), cut_heads(side(got_q)), side(got_kv),
        )

    return got, finish


def place_kernel(*refs):
    me, core, sib, far = partners()
    *parts, out_ref = refs
    out_ref[...] = jnp.zeros_like(out_ref)
    for owner, part in zip((me, sib, far, far + 1 - 2 * core), parts):
        lanes = pl.ds(pl.multiple_of(owner // 2 * 3200 + owner % 2 * 1536, LANES), HIDDEN_WINDOW)
        out_ref[:, lanes] += part[...].astype(f32)


def head_lanes(value):
    return jnp.pad(value, ((0, 0), (NOPE, LANES - NOPE - ROPE)))


def layer_forward(hidden, own_tables, tables, gains, weights, passing, lacking, early):
    input_gain, query_gain, latent_gain, post_gain = gains
    down_both, query_up, latent_up, output_weight, gate_weight, up_weight, down_weight = weights
    scale_in = norm_scale(hidden)
    normed = (hidden * scale_in * input_gain).astype(bf16)
    down_q, down_kv = down_both
    latent_q = project(normed, down_q)
    latent_kv = project(normed, down_kv)
    latent = latent_kv[:, :KVRANK]
    scale_q = norm_scale(latent_q)
    scale_kv = norm_scale(latent)
    own_in = jnp.concatenate(
        [
            latent_q * scale_q * query_gain,
            latent * scale_kv * latent_gain,
            head_lanes(rotate(latent_kv[:, KVRANK:], *own_tables)),
        ],
        axis=1,
    ).astype(bf16)
    all_in = gather(own_in, 0, 384)
    all_in, early = together(all_in, early)
    if lacking is not None:
        early = plain_gather(early)
    query_in = all_in[:, :QRANK]
    kv_in = all_in[:, QRANK:QRANK + KVRANK]
    shared = all_in[:, QRANK + KVRANK:]
    attended, queries, keyval, logs = attend(
        project(query_in, query_up), project(kv_in, latent_up), shared, tables
    )
    if lacking:
        mixed, normed_two, up_weight = output_norm(attended, output_weight, hidden, post_gain, up_weight)
    else:
        mixed, normed_two = output_norm(attended, output_weight, hidden, post_gain)
    normed_two, early = together(normed_two, early)
    merge = lambda value: value.reshape(D, -1)
    gate = project(normed_two, merge(gate_weight)).astype(bf16)
    up = project(normed_two, merge(up_weight)).astype(bf16)
    activated = (jax.nn.silu(gate.astype(f32)) * up.astype(f32)).astype(bf16)
    def outputs(value):
        return down_project(value, down_weight, mixed, passing)

    kept = (hidden, scale_in, normed, latent_q, scale_q, latent, scale_kv, query_in, kv_in,
            shared, queries, keyval, logs, attended, mixed, normed_two, gate, up)
    return (outputs, activated, kept, merge(gate_weight), merge(up_weight), early)


def gate_backward(grad_act, gate, up):
    sigmoid = jax.nn.sigmoid(gate)
    grad_gate = (grad_act * up * sigmoid * (1.0 + gate * (1.0 - sigmoid))).astype(bf16)
    grad_up = (grad_act * gate * sigmoid).astype(bf16)
    return grad_gate, grad_up


def mlp_backward(grad_out, kept, gains, weights, gather_down, wanted):
    mixed, gate, up = kept[14], kept[16], kept[17]
    gate_weight, up_weight, down_weight = weights[4:]
    own_down = (residual_scale * grad_out).astype(bf16)
    grad_down, wanted = together(gather_down(own_down), wanted)
    grad_gate, grad_up = gate_backward(contract_cols(grad_down, down_weight), gate.astype(f32), up.astype(f32))
    grad_mixed, dgain_post, grad_branch = mlp_back(
        grad_gate, grad_up, gate_weight, up_weight, mixed, grad_out, gains[3]
    )
    return (grad_gate, grad_up), wanted, grad_down, grad_mixed, dgain_post[0], grad_branch


def attention_backward(grad_mixed, grad_branch, kept, own_tables, tables, gains, weights, wanted):
    (hidden, scale_in, normed, latent_q, scale_q, latent, scale_kv, query_in, kv_in,
     shared, queries, keyval, logs, attended, mixed, normed_two, gate, up) = kept
    input_gain, query_gain, latent_gain, post_gain = gains
    down_both, query_up, latent_up, output_weight = weights[:4]
    cosine, sine = own_tables
    grad_attended = contract_cols(grad_branch, output_weight).astype(bf16)
    grad_query, grad_keyval, grad_shared = attend_back(
        queries, keyval, shared, tables, grad_attended, attended, logs
    )
    grad_in = latent_back(grad_query, grad_keyval, grad_shared, query_up, latent_up)
    grad_in, wanted = together(grad_in, wanted)
    grad_latent_q, dgain_query = norm_back(latent_q, scale_q, query_gain, grad_in[:, :QRANK])
    grad_latent, dgain_latent = norm_back(
        latent, scale_kv, latent_gain, grad_in[:, QRANK:QRANK + KVRANK]
    )
    start = QRANK + KVRANK + NOPE
    grad_shared = rotate(grad_in[:, start:start + ROPE], cosine, -sine)
    grad_lat = jnp.concatenate(
        [grad_latent_q, grad_latent, jnp.pad(grad_shared, ((0, 0), (0, LANES - ROPE)))], axis=1
    ).astype(bf16)
    down_q, down_kv = down_both
    grad_normed = contract_cols(grad_lat[:, :QRANK], down_q) + contract_cols(
        grad_lat[:, QRANK:QRANK + KVRANK + ROPE], down_kv
    )
    grad_hidden_norm, dgain_input = norm_back(hidden, scale_in, input_gain, grad_normed)
    grad_hidden = grad_mixed + grad_hidden_norm
    found = (grad_branch, grad_query, grad_keyval, grad_lat)
    return (grad_hidden, found, (dgain_input, dgain_query, dgain_latent), wanted)


def spread(weight, count):
    rows, columns = weight.shape
    parts = weight.reshape(rows, count, columns // count).transpose(1, 0, 2)
    return lax.all_to_all(parts, "shard", 0, 0, tiled=True).reshape(rows * count, columns // count)


def collect(grad, count):
    rows, columns = grad.shape
    parts = lax.all_to_all(
        grad.reshape(count, rows // count, columns), "shard", 0, 0, tiled=True
    )
    return parts.transpose(1, 0, 2).reshape(rows // count, columns * count)


def pad_heads(weight):
    rows, columns = weight.shape
    heads = weight.reshape(rows, columns // (NOPE + ROPE), NOPE + ROPE)
    return jnp.pad(heads, ((0, 0), (0, 0), (0, LANES - NOPE - ROPE))).reshape(rows, -1)


def cut_heads(grad):
    rows, columns = grad.shape
    heads = grad.reshape(rows, columns // LANES, LANES)[:, :, :NOPE + ROPE]
    return heads.reshape(rows, -1)


def swap(value, step):
    count = lax.axis_size("shard")
    return lax.ppermute(value, "shard", [(source, source ^ step) for source in range(count)])


def hidden_window(count):
    size = FF // count
    width = -(-size // LANES) * LANES
    starts = [owner * size // LANES * LANES for owner in range(count)]
    starts = [min(start, FF - width) for start in starts]
    return size, width, starts, [owner * size - start for owner, start in enumerate(starts)]


def take_at(table, place):
    return jnp.asarray(table, jnp.int32)[place]


def shared_links(count):
    return count == 4 and lax.axis_size("rep") % 2 == 0


def spread_hidden(gate, up, count):
    me = lax.axis_index("shard")
    size, width, starts, offsets = hidden_window(count)
    rows = gate.shape[0]
    results = []
    for weight in (gate, up):
        whole = jnp.zeros((rows * count, width), bf16)
        for step in range(count):
            owner = me ^ step
            part = lax.dynamic_slice(weight, (0, take_at(starts, owner)), (rows, width))
            if step:
                part = swap(part, step)
            whole = lax.dynamic_update_slice(whole, part, (owner * rows, 0))
        results.append(whole)
    return results


def window_rows(down, count):
    size, width, starts, offsets = hidden_window(count)
    whole = jnp.zeros((width, down.shape[1]), bf16)
    return lax.dynamic_update_slice(whole, down, (take_at(offsets, lax.axis_index("shard")), 0))


def chip_gradients_kernel(order_ref, two_ref, gate_ref, up_ref, gate_out, up_out, turned):
    tokens, rows = two_ref.shape
    piece = 512
    for start in range(0, tokens, piece):
        size = min(piece, tokens - start)
        turned[:, start:start + size] = two_ref[start:start + size, :].T
    width = gate_ref.shape[1]
    whole = width // piece
    for grad, out in ((gate_ref, gate_out), (up_ref, up_out)):
        def tile(step):
            lanes = columns(step, piece)
            out[0, :, lanes] = project(turned[...], grad[:, lanes]).astype(bf16)

        each(whole, False, tile)
        if whole * piece < width:
            out[0, :, whole * piece:] = project(turned[...], grad[:, whole * piece:]).astype(bf16)


def chip_gradients(two_all, grad_gate, grad_up):
    me, core, sib, far = partners()
    tokens, width = grad_gate.shape
    rows = D // 4
    held = pl.BlockSpec((tokens, width), lambda i, order: (0, 0), pipeline_mode=pl.Buffered(1))
    part = pl.BlockSpec((1, rows, width), lambda i, order: (i, 0, 0))
    gate, up = pl.pallas_call(
        chip_gradients_kernel,
        grid_spec=pltpu.PrefetchScalarGridSpec(
            num_scalar_prefetch=1,
            grid=(2,),
            in_specs=[pl.BlockSpec((tokens, rows), lambda i, order: (0, order[i])), held, held],
            out_specs=[part, part],
            scratch_shapes=[pltpu.VMEM((rows, tokens), bf16)],
        ),
        out_shape=[jax.ShapeDtypeStruct((2, rows, width), bf16)] * 2,
        compiler_params=pltpu.CompilerParams(vmem_limit_bytes=VMEM_LIMIT),
        name="chip_gradients",
    )(jnp.stack([sib, me]).astype(jnp.int32), two_all, grad_gate, grad_up)
    return [gate[0], up[0], gate[1], up[1]]


def recompute_kernel(from_ref, own_ref, here_ref, two_ref, near_ref, beside_ref, gate_ref, up_ref, rows_ref,
                     act_own, gate_own, up_own, act_out, gate_out, up_out, down_ref):
    place = pl.program_id(0)
    width = gate_ref.shape[1]
    piece = 512

    @pl.when(own_ref[place] == 1)
    def _():
        act_out[...] = act_own[...]
        gate_out[...] = gate_own[...]
        up_out[...] = up_own[...]

    @pl.when((own_ref[place] == 0) & (here_ref[place] == 1))
    def _():
        down_ref[...] = near_ref[...]

    @pl.when((own_ref[place] == 0) & (here_ref[place] == 0))
    def _():
        down_ref[...] = beside_ref[...]

    @pl.when(own_ref[place] == 0)
    def _():
        def tile(lanes, some_rows):
            gate = project(two_ref[...], gate_ref[:, lanes])
            up = project(two_ref[...], up_ref[:, lanes])
            grad = contract_cols(down_ref[...], rows_ref[some_rows, :])
            sigmoid = jax.nn.sigmoid(gate)
            silu = gate * sigmoid
            act_out[:, lanes] = (silu * up).astype(bf16)
            gate_out[:, lanes] = (grad * up * sigmoid * (1.0 + gate * (1.0 - sigmoid))).astype(bf16)
            up_out[:, lanes] = (grad * silu).astype(bf16)

        each(width // piece, False, lambda step: tile(columns(step, piece), columns(step, piece)))
        if width % piece:
            rest = slice(width // piece * piece, width)
            tile(rest, rest)


def recompute(two_all, down_halves, gate_columns, up_columns, down_rows, own):
    reps = lax.axis_size("rep")
    tokens, width = two_all.shape[0], gate_columns.shape[1]
    tile = own[0].shape[0] // 2
    places = jnp.arange(tokens // tile, dtype=jnp.int32)
    half = places // reps
    is_own = places % reps == lax.axis_index("rep")
    is_here = half == lax.axis_index("shard") % 2
    whole = lambda value: pl.BlockSpec(value.shape, lambda i, a, b, c: (0, 0), pipeline_mode=pl.Buffered(1))
    wide = pl.BlockSpec((tile, D), lambda i, a, b, c: (i, 0))
    again = pl.BlockSpec((tile, D), lambda i, a, b, c: (i % reps, 0))
    mine = pl.BlockSpec((tile, width), lambda i, a, b, c: (a[i], 0), pipeline_mode=pl.Buffered(1))
    part = pl.BlockSpec((tile, width), lambda i, a, b, c: (i, 0))
    return pl.pallas_call(
        recompute_kernel,
        grid_spec=pltpu.PrefetchScalarGridSpec(
            num_scalar_prefetch=3,
            grid=(tokens // tile,),
            in_specs=[wide, again, again, whole(gate_columns), whole(up_columns), whole(down_rows), mine, mine, mine],
            out_specs=[part] * 3,
            scratch_shapes=[pltpu.VMEM((tile, D), bf16)],
        ),
        out_shape=[jax.ShapeDtypeStruct((tokens, width), bf16)] * 3,
        compiler_params=pltpu.CompilerParams(vmem_limit_bytes=VMEM_LIMIT),
        name="recompute",
    )(half, is_own.astype(jnp.int32), is_here.astype(jnp.int32), two_all, *down_halves,
      gate_columns, up_columns, down_rows, *own)


def down_gradient_kernel(act_ref, near_ref, beside_ref, out_ref, turned):
    tokens, width = act_ref.shape
    size = out_ref.shape[0]
    piece = 512

    @pl.when(pl.program_id(0) == 0)
    def _():
        for start in range(0, tokens, piece):
            turned[:, start:start + piece] = act_ref[start:start + piece, :].T

    core = lax.axis_index("shard") % 2
    offset = core * (width - size)
    half = size // 2
    some = tokens // 2
    near = pl.ds(pl.multiple_of(core * some, LANES), some)
    beside = pl.ds(pl.multiple_of((1 - core) * some, LANES), some)

    def tile(step):
        rows = pl.ds(pl.multiple_of(step * half, 16), half)
        source = pl.ds(pl.multiple_of(step * half + offset, 16), half)
        out_ref[rows, :] = project(turned[source, near], near_ref[...]) + project(turned[source, beside], beside_ref[...])

    each(2, False, tile)


def down_gradient(activated_all, down_halves):
    tokens, width = activated_all.shape
    size, piece = FF // 4, 512
    return pl.pallas_call(
        down_gradient_kernel,
        grid=(D // piece,),
        in_specs=[pl.BlockSpec((tokens, width), lambda i: (0, 0), pipeline_mode=pl.Buffered(1)),
                  pl.BlockSpec((tokens // 2, piece), lambda i: (0, i)), pl.BlockSpec((tokens // 2, piece), lambda i: (0, i))],
        out_specs=pl.BlockSpec((size, piece), lambda i: (0, i)),
        out_shape=jax.ShapeDtypeStruct((size, D), f32),
        scratch_shapes=[pltpu.VMEM((width, tokens), bf16)],
        compiler_params=pltpu.CompilerParams(vmem_limit_bytes=VMEM_LIMIT),
        name="down_gradient",
    )(activated_all, *down_halves)


def half_everywhere(group, count):
    if count != 4:
        return group
    rows = group.shape[0] // 2
    half = lax.dynamic_slice_in_dim(group, lax.axis_index("shard") % 2 * rows, rows, 0)
    return lax.all_gather(half, "rep", axis=0, tiled=True)


def everyone(half, count):
    if count != 4:
        return lax.all_gather(half, "rep", axis=0, tiled=True)
    return lax.all_gather(half, "shard", axis=0, tiled=True, axis_index_groups=[[0, 1], [2, 3]])


def owner_gradient(two_all, grad, owner, count):
    rows = D // count
    left = lax.dynamic_slice(two_all, (0, owner * rows), (two_all.shape[0], rows))
    return contract_rows(left, grad).astype(bf16)


def place_windows(parts, count):
    size, width, starts, offsets = hidden_window(count)
    rows = parts[0].shape[0]
    if count == 4:
        tile = 64
        return pl.pallas_call(
            place_kernel,
            grid=(rows // tile,),
            in_specs=[pl.BlockSpec((tile, width), lambda i: (i, 0))] * 4,
            out_specs=pl.BlockSpec((tile, FF), lambda i: (i, 0)),
            out_shape=jax.ShapeDtypeStruct((rows, FF), f32),
            compiler_params=pltpu.CompilerParams(vmem_limit_bytes=VMEM_LIMIT),
            cost_estimate=pl.CostEstimate(flops=0, bytes_accessed=rows * FF * 8, transcendentals=0),
            name="place_windows",
        )(*parts)
    me = lax.axis_index("shard")
    gathered = jnp.zeros((count, rows, width), bf16)
    for step, part in enumerate(parts):
        gathered = lax.dynamic_update_slice(gathered, part[None], (me ^ step, 0, 0))
    pieces = [gathered[owner, :, offset:offset + size] for owner, offset in enumerate(offsets)]
    return jnp.concatenate(pieces, axis=1).astype(f32)


def together(*values):
    return lax.optimization_barrier(values)


def body(tokens, segment_ids, input_gain, query_gain, latent_gain, post_gain, query_down, query_up,
         latent_down, latent_up, output_weight, gate_weight, up_weight, down_weight, cotangent):
    at_start = lax.axis_index("section") == 0
    count = lax.axis_size("shard")
    size, width, starts, offsets = hidden_window(count)
    gains = (input_gain[0], query_gain[0], latent_gain[0], post_gain[0])
    down_q, down_kv, query_up_all, latent_up_all, groups, gate_columns, up_columns = first_move(
        query_down[0], latent_down[0], query_up[0], latent_up[0], segment_ids, gate_weight[0], up_weight[0], count
    )
    down_both = (down_q, down_kv)
    own_tables = tuple(t.reshape(-1, ROPE // 2) for t in slot_tables(segment_ids))
    tables = head_tables(groups)

    weights = (down_both, query_up_all, latent_up_all, output_weight[0], gate_columns, up_columns, down_weight[0])
    start = tokens.astype(f32)
    last = cotangent.astype(f32)
    last_down = (residual_scale * last).astype(bf16)
    outputs, activated, _, gate_columns, up_columns, all_last = layer_forward(
        start, own_tables, tables, gains, weights, True, shared_links(count), last_down
    )
    leaving, low, received, down_rows = outputs(activated)
    weights = weights[:4] + (gate_columns, up_columns, down_rows)
    entering = jnp.where(at_start, start, received.astype(f32))
    _, kept_activated, kept, _, _, _ = layer_forward(
        entering, own_tables, tables, gains, weights, False, None, all_last
    )

    (hidden, scale_in, normed, latent_q, scale_q, latent, scale_kv, query_in, kv_in,
     shared, queries, keyval, logs, attended, mixed, normed_two, gate, up) = kept
    half_two = half_everywhere(normed_two, count)
    _, _, _, grad_mixed, _, grad_branch = mlp_backward(last, kept, gains, weights, lambda own: all_last, at_start)
    grad, _, _, half_two = attention_backward(
        grad_mixed, grad_branch, kept, own_tables, tables, gains, weights, half_two
    )
    two_all = everyone(half_two, count)
    grad_low, kept_activated = together(grad.astype(bf16), kept_activated)
    returned = lax.ppermute(grad_low, "section", [(1, 0)])
    leaving, boundary = down_project(kept_activated, down_rows, mixed, False)
    incoming = jnp.where(at_start, returned.astype(f32), last)
    incoming, boundary = together(incoming, boundary)

    own_grads, two_all, grad_down, grad_mixed, dgain_post, grad_branch = mlp_backward(
        incoming, kept, gains, weights, lambda own: gather(own, 1, 512), two_all
    )
    half_down = half_everywhere(grad_down, count)
    part_output = contract_rows(attended, grad_branch).astype(bf16)
    grad_branch, part_output = together(grad_branch, part_output)

    grad, found, (dgain_input, dgain_query, dgain_latent), _ = attention_backward(
        grad_mixed, grad_branch, kept, own_tables, tables, gains, weights, at_start
    )
    grad_branch, grad_query, grad_keyval, grad_lat = found
    gain_terms = jnp.concatenate([dgain_input, dgain_query, dgain_latent, dgain_post])[None]
    normed_rows = lax.all_to_all(
        normed.reshape(normed.shape[0], count, -1).transpose(1, 0, 2), "shard", 0, 0, tiled=True
    ).reshape(normed.shape[0] * count, -1)
    part_query = contract_rows(query_in, grad_query).astype(bf16)
    part_latent = contract_rows(kv_in, grad_keyval).astype(bf16)
    gain_terms, half_down = together(gain_terms, half_down)
    exchanged, exchange_end = last_move(grad_lat, gain_terms, part_query, part_latent, count)
    part_output, half_down = together(part_output, half_down)
    down_all = [half_down, swap(half_down, 1)] if count == 4 else everyone(half_down, count)
    total_output = lax.psum(part_output, "rep")
    down_all, two_all, own_grads, normed_rows = together(down_all, two_all, own_grads, normed_rows)
    if count == 4:
        activated_all, grad_gate, grad_up = recompute(
            two_all, down_all, gate_columns, up_columns, down_rows, (kept_activated, *own_grads)
        )
    else:
        gate_all = project(two_all, gate_columns)
        up_all = project(two_all, up_columns)
        activated_all = (jax.nn.silu(gate_all) * up_all).astype(bf16)
        grad_gate, grad_up = gate_backward(contract_cols(down_all, down_rows), gate_all, up_all)
    def attention_shares(exchanged):
        lat_all, gains_all, part_query, part_latent = exchange_end(exchanged)
        part_down = contract_rows(normed_rows, lat_all[:, :QRANK + KVRANK + ROPE]).astype(bf16)
        part_gains = jnp.sum(gains_all, axis=0).astype(bf16)
        side = part_down.shape[1]
        gain_rows = -(-part_gains.shape[0] // side)
        part_gains = jnp.pad(part_gains, (0, gain_rows * side - part_gains.shape[0])).reshape(gain_rows, side)
        part_down = jnp.concatenate([part_down, part_gains], axis=0)
        return part_down, part_latent, part_query

    me = lax.axis_index("shard")
    if count == 4:
        grad_gate, grad_up, total_output = together(grad_gate, grad_up, total_output)
        away = [owner_gradient(two_all, grad_gate, me ^ step, count) for step in (2, 3)]
        brought = [[swap(part, 2 + i) for i, part in enumerate(away)]]
        two_all, _, exchanged, total_output = together(two_all, away, exchanged, total_output)
        shares = attention_shares(exchanged)
        two_all, *shares = together(two_all, *shares)
        total_down_both, total_latent, total_query = lax.psum(tuple(shares), "rep")
        away = [owner_gradient(two_all, grad_up, me ^ step, count) for step in (2, 3)]
        brought.append([swap(part, 2 + i) for i, part in enumerate(away)])
        two_all, _ = together(two_all, away)
        near = chip_gradients(two_all, grad_gate, grad_up)
        activated_all, near[0], brought[0] = together(activated_all, near[0], brought[0])
        total_down = down_gradient(activated_all, down_all)
        hidden_parts = [[near[2 + i], swap(near[i], 1), *brought[i]] for i in range(2)]
        total_down, hidden_parts[0] = together(total_down, hidden_parts[0])
    else:
        parts = [
            [owner_gradient(two_all, grad, me ^ step, count) for grad in (grad_gate, grad_up)] for step in range(count)
        ]
        hidden_parts = [
            [swap(parts[step][i], step) if step else parts[step][i] for step in range(count)] for i in range(2)
        ]
        total_down_both, total_latent, total_query = lax.psum(attention_shares(exchanged), "rep")
        total_down = contract_rows(activated_all, down_all)
        total_down = lax.dynamic_slice_in_dim(total_down, take_at(offsets, me), size, 0)
    total_gate = place_windows(hidden_parts[0], count)
    total_gate, hidden_parts[1][0] = together(total_gate, hidden_parts[1][0])
    total_up = place_windows(hidden_parts[1], count)
    gain_rows = total_down_both.shape[0] - D // count
    gain_totals = total_down_both[-gain_rows:].reshape(-1).astype(f32)
    total_down_both = total_down_both[:-gain_rows].astype(f32)
    total_query, total_latent = total_query.astype(f32), total_latent.astype(f32)
    first, second, third = D, D + QRANK, D + QRANK + KVRANK
    gain_totals = (gain_totals[:first], gain_totals[first:second], gain_totals[second:third], gain_totals[third:third + D])
    return (
        boundary[None],
        grad[None],
        gain_totals[0][None],
        gain_totals[1][None],
        gain_totals[2][None],
        gain_totals[3][None],
        total_down_both[None, :, :QRANK],
        total_query[None],
        total_down_both[None, :, QRANK:],
        total_latent[None],
        total_output.astype(f32)[None],
        total_gate[None],
        total_up[None],
        total_down[None],
    )


def solution(mesh):
    tokens = P(("rep", "shard"), None)
    gain = P("section", None)
    weight = P("section", "shard", None)
    out = P("section", ("rep", "shard"), None)
    return jax.shard_map(
        body,
        mesh=mesh,
        in_specs=(tokens, tokens) + (gain,) * 4 + (weight,) * 8 + (tokens,),
        out_specs=(out, out) + (gain,) * 4 + (weight,) * 8,
        check_vma=False,
    )
```

```python
import functools
import math

import jax
import jax.numpy as jnp
from jax import lax
from jax.experimental import pallas as pl
from jax.experimental.pallas import tpu as pltpu
from jax.sharding import PartitionSpec as P

D = 2560
HEADS = 40
NOPE = 64
ROPE = 32
VDIM = 64
QRANK = 768
KVRANK = 256
FF = 6400
SLOT = 96
LANES = 128

epsilon = 1e-05
residual_scale = 1.4 / math.sqrt(62.0)
masked_score = -1e30
score_scale = 1.0 / math.sqrt(NOPE + ROPE)
bf16 = jnp.bfloat16
f32 = jnp.float32


def norm_scale(value):
    return lax.rsqrt(jnp.mean(value * value, axis=-1, keepdims=True) + epsilon)


def norm_back(value, scale, gain, grad):
    weighted = grad * gain
    inner = jnp.mean(value * weighted, axis=-1, keepdims=True)
    grad_value = scale * weighted - value * (scale * scale * scale) * inner
    return (grad_value, jnp.sum(grad * value * scale, axis=0))


def rotate(value, cosine, sine):
    half = value.shape[-1] // 2
    front = value[..., :half]
    back = value[..., half:]
    return jnp.concatenate([front * cosine - back * sine, back * cosine + front * sine], axis=-1)


def slot_tables(segments):
    index = jnp.arange(SLOT, dtype=jnp.int32)
    first_index = jnp.sum((segments[:, None, :] < segments[:, :, None]).astype(jnp.int32), axis=-1)
    position = (index - first_index).astype(f32)
    freq = jnp.exp(jnp.arange(ROPE // 2, dtype=f32) * (-2.0 * math.log(10000.0) / ROPE))
    angle = position[..., None] * freq
    return (jnp.cos(angle), jnp.sin(angle))


def head_tables(segments):
    cosine, sine = slot_tables(segments)
    slots = segments.shape[0]
    ones = jnp.ones((slots, SLOT, NOPE), f32)
    tail = jnp.zeros((slots, SLOT, LANES - NOPE - ROPE), f32)
    half = jnp.zeros_like(sine)
    keep = jnp.concatenate([ones, cosine, cosine, tail], axis=-1)
    left = jnp.concatenate([0.0 * ones, -sine, half, tail], axis=-1)
    right = jnp.concatenate([0.0 * ones, half, sine, tail], axis=-1)
    index = jnp.arange(SLOT, dtype=jnp.int32)
    allowed = (segments[:, :, None] == segments[:, None, :]) & (index[None, :] <= index[:, None])
    mask = jnp.where(allowed, 0.0, masked_score).astype(f32)
    flat = lambda table: table.reshape(slots * SLOT, LANES)
    return (flat(keep), flat(left), flat(right), mask, mask.transpose(0, 2, 1))


def contract_rows(left, right):
    return lax.dot_general(left, right, (((0,), (0,)), ((), ())), preferred_element_type=f32)


def contract_cols(left, right):
    return lax.dot_general(left, right, (((1,), (1,)), ((), ())), preferred_element_type=f32)


def project(left, weight):
    return jnp.dot(left, weight, preferred_element_type=f32)


def low_lanes():
    return lax.broadcasted_iota(jnp.int32, (SLOT, LANES), 1) < NOPE


HEAD_GROUP = 5
HEAD_ROWS = 16


def attend_kernel(heads, q_ref, kv_ref, sh_ref, keep_ref, left_ref, right_ref, mask_ref,
                  att_ref, qo_ref, kvo_ref, log_ref):
    low = low_lanes()
    lane = lax.broadcasted_iota(jnp.int32, (SLOT, LANES), 1)
    shared = sh_ref[...].astype(f32)
    keep, left, right = keep_ref[...], left_ref[...], right_ref[...]
    mask = mask_ref[0]
    tallest = jnp.zeros((SLOT, LANES), f32)
    sums = jnp.ones((SLOT, LANES), f32)
    for first in range(0, heads, HEAD_GROUP):
        group = range(first, min(first + HEAD_GROUP, heads))
        scores, values = [], []
        for head in group:
            lanes = slice(head * LANES, (head + 1) * LANES)
            q = q_ref[:, lanes]
            q = q * keep + pltpu.roll(q, LANES - 16, 1) * left + pltpu.roll(q, 16, 1) * right
            q = q.astype(bf16)
            qo_ref[:, lanes] = q
            kv = kv_ref[:, lanes]
            kvo_ref[:, lanes] = kv.astype(bf16)
            k = jnp.where(low, kv, shared).astype(bf16)
            values.append(jnp.where(low, 1.0, kv).astype(bf16))
            scores.append(contract_cols(q, k) * score_scale + mask)
        tops = [jnp.max(score, axis=-1, keepdims=True) for score in scores]
        terms = [jnp.exp(score - top).astype(bf16) for score, top in zip(scores, tops)]
        outs = [project(term, value) for term, value in zip(terms, values)]
        for head, top, out in zip(group, tops, outs):
            turned = pltpu.roll(out, NOPE, 1)
            tallest = jnp.where(lane == head, top, tallest)
            sums = jnp.where(lane == head, out, sums)
            pair = (head // 2) * LANES
            if head % 2 == 0:
                att = turned / out
                att_ref[:, pair:pair + VDIM] = att[:, :VDIM].astype(bf16)
            else:
                att = out / turned
                att_ref[:, pair + VDIM:pair + LANES] = att[:, VDIM:].astype(bf16)
    log_ref[0] = (tallest + jnp.log(sums)).T[:HEAD_ROWS, :]


def attention_cost(tokens, heads, passes):
    return pl.CostEstimate(
        flops=passes * tokens * heads * SLOT * LANES * 20, bytes_accessed=tokens * heads * LANES * 12,
        transcendentals=tokens * heads * SLOT,
    )


def attend(query, keyval, shared, tables):
    tokens = query.shape[0]
    heads = query.shape[1] // LANES
    wide = pl.BlockSpec((SLOT, heads * LANES), lambda s: (s, 0))
    one = pl.BlockSpec((SLOT, LANES), lambda s: (s, 0))
    square = pl.BlockSpec((1, SLOT, SLOT), lambda s: (s, 0, 0))
    return pl.pallas_call(
        functools.partial(attend_kernel, heads),
        grid=(tokens // SLOT,),
        in_specs=[wide, wide, one, one, one, one, square],
        out_specs=[pl.BlockSpec((SLOT, heads * VDIM), lambda s: (s, 0)), wide, wide,
                   pl.BlockSpec((1, HEAD_ROWS, SLOT), lambda s: (s, 0, 0))],
        out_shape=[
            jax.ShapeDtypeStruct((tokens, heads * VDIM), bf16),
            jax.ShapeDtypeStruct(query.shape, bf16),
            jax.ShapeDtypeStruct(keyval.shape, bf16),
            jax.ShapeDtypeStruct((tokens // SLOT, HEAD_ROWS, SLOT), f32),
        ],
        cost_estimate=attention_cost(tokens, heads, 4),
        name="attend",
    )(query, keyval, shared, *tables[:4])


def attend_back_kernel(heads, q_ref, kv_ref, sh_ref, keep_ref, left_ref, right_ref, mask_ref,
                       ga_ref, att_ref, log_ref, gq_ref, gkv_ref, gsh_ref):
    low = low_lanes()
    shared = sh_ref[...].astype(f32)
    keep, left, right = keep_ref[...], left_ref[...], right_ref[...]
    mask = mask_ref[0]
    total = jnp.zeros((SLOT, LANES), f32)
    product = ga_ref[...].astype(f32) * att_ref[...].astype(f32)
    high = product.astype(bf16)
    rest = (product - high.astype(f32)).astype(bf16)
    shape = (HEAD_ROWS, product.shape[1])
    chosen = lax.broadcasted_iota(jnp.int32, shape, 1) // VDIM == lax.broadcasted_iota(jnp.int32, shape, 0)
    chosen = jnp.where(chosen, 1.0, 0.0).astype(bf16)
    inner = contract_cols(chosen, high) + contract_cols(chosen, rest)
    for first in range(0, heads, HEAD_GROUP):
        group = range(first, min(first + HEAD_GROUP, heads))
        queries, keys, grads, scores, grad_probs = [], [], [], [], []
        for head in group:
            lanes = slice(head * LANES, (head + 1) * LANES)
            q = q_ref[:, lanes]
            kvb = kv_ref[:, lanes]
            k = jnp.where(low, kvb.astype(f32), shared).astype(bf16)
            if head % 2 == 0 and head == heads - 1:
                ga = ga_ref[:, head * VDIM:(head + 1) * VDIM].astype(f32)
                ga = jnp.concatenate([jnp.zeros_like(ga), ga], axis=1)
            else:
                start = (head // 2) * LANES
                ga = ga_ref[:, start:start + LANES].astype(f32)
                if head % 2 == 0:
                    ga = pltpu.roll(ga, NOPE, 1)
                ga = jnp.where(low, 0.0, ga)
            ga = ga.astype(bf16)
            queries.append(q)
            keys.append(k)
            grads.append(ga)
            scores.append(contract_cols(k, q) * score_scale + mask)
            grad_probs.append(contract_cols(kvb, ga))
        probs = [jnp.exp(score - log_ref[0, head:head + 1, :]) for head, score in zip(group, scores)]
        changes = [
            (prob * (grad - inner[head:head + 1, :]) * score_scale).astype(bf16)
            for head, prob, grad in zip(group, probs, grad_probs)
        ]
        grad_values = [project(prob.astype(bf16), ga) for prob, ga in zip(probs, grads)]
        grad_keys = [project(change, q) for change, q in zip(changes, queries)]
        grad_queries = [contract_rows(change, k) for change, k in zip(changes, keys)]
        for head, gv, gk, gq in zip(group, grad_values, grad_keys, grad_queries):
            lanes = slice(head * LANES, (head + 1) * LANES)
            gq = gq * keep - pltpu.roll(gq, LANES - 16, 1) * left - pltpu.roll(gq, 16, 1) * right
            gq_ref[:, lanes] = gq.astype(bf16)
            total = total + gk
            gkv_ref[:, lanes] = jnp.where(low, gk, gv).astype(bf16)
    gsh_ref[...] = total


def attend_back(query, keyval, shared, tables, grad_attended, attended, logs):
    tokens = query.shape[0]
    heads = query.shape[1] // LANES
    wide = pl.BlockSpec((SLOT, heads * LANES), lambda s: (s, 0))
    one = pl.BlockSpec((SLOT, LANES), lambda s: (s, 0))
    half = pl.BlockSpec((SLOT, heads * VDIM), lambda s: (s, 0))
    return pl.pallas_call(
        functools.partial(attend_back_kernel, heads),
        grid=(tokens // SLOT,),
        in_specs=[wide, wide, one, one, one, one, pl.BlockSpec((1, SLOT, SLOT), lambda s: (s, 0, 0)),
                  half, half, pl.BlockSpec((1, HEAD_ROWS, SLOT), lambda s: (s, 0, 0))],
        out_specs=[wide, wide, one],
        out_shape=[
            jax.ShapeDtypeStruct(query.shape, bf16),
            jax.ShapeDtypeStruct(keyval.shape, bf16),
            jax.ShapeDtypeStruct((tokens, LANES), f32),
        ],
        cost_estimate=attention_cost(tokens, heads, 10),
        name="attend_back",
    )(query, keyval, shared, *tables[:3], tables[4], grad_attended, attended, logs)


MESH = pl.DeviceIdType.MESH
VMEM_LIMIT = 60 * 1024 * 1024


def partners():
    me = lax.axis_index("shard")
    core = me % 2
    return me, core, me + 1 - 2 * core, (me + 2) % 4


def greet(devices):
    barrier = pltpu.get_barrier_semaphore()
    for device in devices:
        pl.semaphore_signal(barrier, inc=1, device_id=device, device_id_type=MESH)
    pl.semaphore_wait(barrier, len(devices))


def columns(step, width):
    return pl.ds(pl.multiple_of(step * width, LANES), width)


def rows_at(start, rows):
    return pl.ds(pl.multiple_of(start * rows, 16), rows)


def remote(source, target, sems, step, device):
    return pltpu.make_async_remote_copy(
        src_ref=source, dst_ref=target, send_sem=sems.at[0, step], recv_sem=sems.at[1, step],
        device_id={"shard": device}, device_id_type=MESH,
    )


def exchange_scratch(rows, steps, width):
    part = pltpu.VMEM((steps, rows, width), bf16)
    return [part] * 6 + [
        pltpu.VMEM((steps, rows, width), f32),
        pltpu.VMEM((2 * rows, width), f32),
        pltpu.SemaphoreType.DMA((3, 2, steps)),
    ]


def each(steps, unrolled, do):
    if unrolled:
        for step in range(steps):
            do(step)
    else:
        def again(step, carry):
            do(step)
            return carry
        lax.fori_loop(0, steps, again, 0)


def sum_scatter(rows, steps, unrolled, partial, scratch, use):
    (to_sib, from_sib, to_far, from_far, own_sib, own_from, hold, stage, sems) = scratch
    me, core, sib, far = partners()
    mine = rows_at(core, rows)
    other = rows_at(1 - core, rows)

    def first(step):
        return remote(to_sib.at[step], from_sib.at[step], sems.at[0], step, sib)

    def across(step):
        return remote(to_far.at[step], from_far.at[step], sems.at[1], step, far)

    def beside(step):
        return remote(own_sib.at[step], own_from.at[step], sems.at[2], step, sib)

    def far_part(step):
        stage[...] = partial(rows_at(far // 2, 2 * rows), step)
        to_sib[step] = stage[other, :].astype(bf16)
        first(step).start()
        hold[step] = stage[mine, :]

    def far_send(step):
        first(step).wait_recv()
        to_far[step] = (hold[step] + from_sib[step].astype(f32)).astype(bf16)
        across(step).start()

    def far_step(step):
        far_part(step)
        if unrolled:
            if step > 0:
                far_send(step - 1)
        else:
            @pl.when(step > 0)
            def _():
                far_send(step - 1)

    each(steps, unrolled, far_step)
    far_send(steps - 1)

    def near_part(step):
        stage[...] = partial(rows_at(me // 2, 2 * rows), step)
        own_sib[step] = stage[other, :].astype(bf16)
        beside(step).start()
        hold[step] = stage[mine, :]

    each(steps, unrolled, near_part)

    def finish(step):
        beside(step).wait_recv()
        across(step).wait_recv()
        use(step, hold[step] + own_from[step].astype(f32) + from_far[step].astype(f32))

    each(steps, unrolled, finish)

    def settle(step):
        first(step).wait_send()
        across(step).wait_send()
        beside(step).wait_send()

    each(steps, unrolled, settle)


def spread_rows(rows, steps, width, place, all_ref, sems):
    me, core, sib, far = partners()

    def part(owner, step):
        return all_ref.at[rows_at(owner, rows), columns(step, width)]

    def across(step):
        return remote(part(me, step), part(me, step), sems.at[0], step, far)

    def beside(step):
        return remote(part(me, step), part(me, step), sems.at[1], step, sib)

    def onward(step):
        return remote(part(far, step), part(far, step), sems.at[2], step, sib)

    def send(step):
        place(step)
        across(step).start()
        beside(step).start()

    each(steps, False, send)

    def forward(step):
        across(step).wait_recv()
        onward(step).start()

    each(steps, False, forward)

    def settle(step):
        beside(step).wait_recv()
        onward(step).wait_recv()
        across(step).wait_send()
        beside(step).wait_send()
        onward(step).wait_send()

    each(steps, False, settle)


def vmem(count):
    return [pl.BlockSpec(memory_space=pltpu.VMEM)] * count


def comm_call(kernel, name, number, inputs, out_shape, scratch, flops=0, aliased={}):
    nbytes = sum(v.size * v.dtype.itemsize for v in (*inputs, *out_shape))
    return pl.pallas_call(
        kernel,
        in_specs=vmem(len(inputs) - len(aliased)) + any_space(len(aliased)),
        out_specs=vmem(len(out_shape) - len(aliased)) + any_space(len(aliased)),
        out_shape=out_shape,
        scratch_shapes=scratch,
        input_output_aliases=aliased,
        compiler_params=pltpu.CompilerParams(
            collective_id=number, has_side_effects=True, vmem_limit_bytes=VMEM_LIMIT
        ),
        cost_estimate=pl.CostEstimate(flops=0, bytes_accessed=0 * nbytes, transcendentals=0),
        name=name,
    )(*inputs)


def shape(rows, width, dtype):
    return jax.ShapeDtypeStruct((rows, width), dtype)


def gather_kernel(steps, width, own_ref, all_ref, sems):
    rows = own_ref.shape[0]
    me, core, sib, far = partners()
    greet([{"shard": sib}, {"shard": far}])

    def place(step):
        all_ref[rows_at(me, rows), columns(step, width)] = own_ref[:, columns(step, width)]

    spread_rows(rows, steps, width, place, all_ref, sems)


def gather(value, number, width):
    if lax.axis_size("shard") != 4:
        return lax.all_gather(value, "shard", axis=0, tiled=True)
    rows, total = value.shape
    steps = total // width
    (out,) = comm_call(
        functools.partial(gather_kernel, steps, width), "gather_rows", number, [value],
        [shape(4 * rows, total, bf16)], [pltpu.SemaphoreType.DMA((3, 2, steps))],
    )
    return out


def plain_gather(value):
    return lax.all_gather(value, "shard", axis=0, tiled=True)


def plain_scatter(value):
    return lax.psum_scatter(value.astype(bf16), "shard", scatter_dimension=0, tiled=True).astype(f32)


MODEL_STEP = 512


def output_kernel(relaying, att_ref, weight_ref, hidden_ref, gain_ref, *refs):
    if relaying:
        _, mixed_ref, two_ref, up_ref, *scratch, passed = refs
    else:
        mixed_ref, two_ref, *scratch = refs
    *parts, sems = scratch
    rows = hidden_ref.shape[0]
    width = MODEL_STEP
    steps = D // width
    me, core, sib, far = partners()
    devices = [{"shard": sib}, {"shard": far}]
    if relaying:
        partner, away = replica_pair()
        devices.append({"rep": partner})
    greet(devices)
    if relaying:
        @pl.when(away == 0)
        def _():
            for slot, owner in enumerate((far, far + 1 - 2 * core)):
                pass_on(up_ref, passed, slot, owner).start()

    def partial(where, step):
        return project(att_ref[where, :], weight_ref[:, columns(step, width)])

    def use(step, total):
        lanes = columns(step, width)
        mixed_ref[:, lanes] = hidden_ref[:, lanes] + residual_scale * total

    sum_scatter(rows, steps, False, partial, parts, use)
    mixed = mixed_ref[...]
    scale = norm_scale(mixed)

    def place(step):
        lanes = columns(step, width)
        two_ref[rows_at(me, rows), lanes] = (mixed_ref[:, lanes] * scale * gain_ref[:, lanes]).astype(bf16)

    spread_rows(rows, steps, width, place, two_ref, sems)
    if relaying:
        @pl.when(away == 0)
        def _():
            for slot, owner in enumerate((far, far + 1 - 2 * core)):
                pass_on(up_ref, passed, slot, owner).wait_send()

        @pl.when(away == 1)
        def _():
            for slot, owner in enumerate((far, far + 1 - 2 * core)):
                pass_on(up_ref, passed, slot, owner).wait_recv()


def output_norm(attended, weight, hidden, gain, up=None):
    if lax.axis_size("shard") != 4:
        mixed = hidden + residual_scale * plain_scatter(project(attended, weight))
        return mixed, plain_gather((mixed * norm_scale(mixed) * gain).astype(bf16))
    rows = hidden.shape[0]
    steps = D // MODEL_STEP
    scratch = exchange_scratch(rows, steps, MODEL_STEP) + [pltpu.SemaphoreType.DMA((3, 2, steps))]
    inputs = [attended, weight, hidden, gain[None]]
    outputs = [shape(rows, D, f32), shape(4 * rows, D, bf16)]
    flops = 2 * attended.size * D
    if up is None:
        return comm_call(functools.partial(output_kernel, False), "output_norm", 2, inputs, outputs, scratch, flops)
    return comm_call(
        functools.partial(output_kernel, True), "output_norm", 9, inputs + [up],
        outputs + [jax.ShapeDtypeStruct(up.shape, bf16)], scratch + [pltpu.SemaphoreType.DMA((2, 2))], flops,
        aliased={4: 2},
    )


def down_kernel(passing, act_ref, given_ref, mixed_ref, out_ref, low_ref, *scratch):
    rows = mixed_ref.shape[0]
    width = MODEL_STEP
    steps = D // width
    me, core, sib, far = partners()
    devices = [{"shard": sib}, {"shard": far}]
    weight_ref = given_ref
    if passing:
        got_ref, weight_ref, *parts, sems = scratch
        size, more = given_ref.shape[0], weight_ref.shape[0] - given_ref.shape[0]
        weight_ref[pl.ds(pl.multiple_of((1 - core) * size, 16), more), :] = jnp.zeros((more, D), bf16)
        piece = 64

        def fill(step):
            source = pl.ds(pl.multiple_of(step * piece, 16), piece)
            target = pl.ds(pl.multiple_of(step * piece + core * more, 16), piece)
            weight_ref[target, :] = given_ref[source, :]

        each(size // piece, False, fill)
        section = lax.axis_index("section")
        devices.append({"section": 1 - section})
    else:
        parts = scratch
    greet(devices)

    def onward(step):
        lanes = columns(step, width)
        return pltpu.make_async_remote_copy(
            src_ref=low_ref.at[:, lanes], dst_ref=got_ref.at[:, lanes], send_sem=sems.at[0, step],
            recv_sem=sems.at[1, step], device_id={"section": 1 - section}, device_id_type=MESH,
        )

    def partial(where, step):
        return project(act_ref[where, :], weight_ref[:, columns(step, width)])

    def use(step, total):
        lanes = columns(step, width)
        out = mixed_ref[:, lanes] + residual_scale * total
        out_ref[:, lanes] = out
        low_ref[:, lanes] = out.astype(bf16)
        if passing:
            onward(step).start()

    sum_scatter(rows, steps, False, partial, parts, use)
    if passing:
        each(steps, False, lambda step: onward(step).wait())


def down_project(activated, weight, mixed, passing):
    count = lax.axis_size("shard")
    if count != 4:
        if passing:
            weight = window_rows(weight, count)
        output = mixed + residual_scale * plain_scatter(project(activated, weight))
        low = output.astype(bf16)
        return (output, low) + ((lax.ppermute(low, "section", [(0, 1)]), weight) if passing else ())
    rows = mixed.shape[0]
    steps = D // MODEL_STEP
    scratch = exchange_scratch(rows, steps, MODEL_STEP)
    return comm_call(
        functools.partial(down_kernel, passing), "down_project", 3 if passing else 4,
        [activated, weight, mixed],
        [shape(rows, D, f32)] + [shape(rows, D, bf16)] * (2 if passing else 1)
        + [shape(HIDDEN_WINDOW, D, bf16)] * passing,
        scratch + ([pltpu.SemaphoreType.DMA((2, steps))] if passing else []),
        flops=2 * activated.size * D,
    )


def mlp_back_kernel(gate_ref, up_ref, gate_weight_ref, up_weight_ref, mixed_ref, grad_ref, gain_ref, out_ref, dgain_ref, branch_ref,
                    *scratch):
    *parts, sems = scratch
    rows = mixed_ref.shape[0]
    width = MODEL_STEP
    steps = D // width
    me, core, sib, far = partners()
    greet([{"shard": sib}, {"shard": far}])

    def partial(where, step):
        rows_of = columns(step, width)
        return contract_cols(gate_ref[where, :], gate_weight_ref[rows_of, :]) + contract_cols(
            up_ref[where, :], up_weight_ref[rows_of, :]
        )

    def use(step, total):
        out_ref[:, columns(step, width)] = total

    sum_scatter(rows, steps, False, partial, parts, use)
    mixed = mixed_ref[...]
    scale = norm_scale(mixed)
    inner = jnp.mean(mixed * out_ref[...] * gain_ref[...], axis=-1, keepdims=True)
    slope = scale * scale * scale * inner

    def place(step):
        lanes = columns(step, width)
        grad, value = out_ref[:, lanes], mixed_ref[:, lanes]
        dgain_ref[:, lanes] = jnp.sum(grad * value * scale, axis=0, keepdims=True)
        total = grad_ref[:, lanes] + scale * (grad * gain_ref[:, lanes]) - value * slope
        out_ref[:, lanes] = total
        branch_ref[rows_at(me, rows), lanes] = (residual_scale * total).astype(bf16)

    spread_rows(rows, steps, width, place, branch_ref, sems)


def mlp_back(grad_gate, grad_up, gate_weight, up_weight, mixed, grad_out, gain):
    if lax.axis_size("shard") != 4:
        grad = plain_scatter(contract_cols(grad_gate, gate_weight) + contract_cols(grad_up, up_weight))
        back, dgain = norm_back(mixed, norm_scale(mixed), gain, grad)
        grad_mixed = grad_out + back
        return grad_mixed, dgain[None], plain_gather((residual_scale * grad_mixed).astype(bf16))
    rows = mixed.shape[0]
    steps = D // MODEL_STEP
    return comm_call(
        mlp_back_kernel, "mlp_back", 5,
        [grad_gate, grad_up, gate_weight, up_weight, mixed, grad_out, gain[None]],
        [shape(rows, D, f32), shape(1, D, f32), shape(4 * rows, D, bf16)],
        exchange_scratch(rows, steps, MODEL_STEP) + [pltpu.SemaphoreType.DMA((3, 2, steps))],
        flops=4 * grad_gate.size * D,
    )


LATENT_STEP = 256


def latent_back_kernel(gq_ref, gkv_ref, gsh_ref, qup_ref, lup_ref, out_ref, *scratch):
    rows = out_ref.shape[0]
    width = LATENT_STEP
    me, core, sib, far = partners()
    greet([{"shard": sib}, {"shard": far}])

    def partial(where, step):
        if step < QRANK // width:
            return contract_cols(gq_ref[where, :], qup_ref[step * width:(step + 1) * width, :])
        if step == QRANK // width:
            return contract_cols(gkv_ref[where, :], lup_ref[...])
        shared = gsh_ref[where, :]
        return jnp.concatenate([shared, jnp.zeros_like(shared)], axis=1)

    def use(step, total):
        out_ref[:, step * width:(step + 1) * width] = total

    sum_scatter(rows, out_ref.shape[1] // width, True, partial, scratch, use)


def latent_back(grad_query, grad_keyval, grad_shared, query_up, latent_up):
    if lax.axis_size("shard") != 4:
        return plain_scatter(
            jnp.concatenate(
                [contract_cols(grad_query, query_up), contract_cols(grad_keyval, latent_up), grad_shared],
                axis=1,
            )
        )
    rows = grad_query.shape[0] // 4
    steps = QRANK // LATENT_STEP + 2
    (out,) = comm_call(
        latent_back_kernel, "latent_back", 6, [grad_query, grad_keyval, grad_shared, query_up, latent_up],
        [shape(rows, steps * LATENT_STEP, f32)], exchange_scratch(rows, steps, LATENT_STEP),
        flops=2 * grad_query.size * QRANK + 2 * grad_keyval.size * KVRANK,
    )
    return out


def any_space(count):
    return [pl.BlockSpec(memory_space=pl.ANY)] * count


def pair(value, index):
    return value.at[0, index], value.at[1, index]


def send_to(source, target, sems, index, device):
    send, receive = pair(sems, index)
    return pltpu.make_async_remote_copy(
        src_ref=source, dst_ref=target, send_sem=send, recv_sem=receive,
        device_id={"shard": device}, device_id_type=MESH,
    )


def replica_pair():
    replica = lax.axis_index("rep")
    return replica + 1 - 2 * (replica % 2), (lax.axis_index("shard") + replica) % 2


def pass_on(target, sems, step, owner):
    partner, _ = replica_pair()
    return pltpu.make_async_remote_copy(
        src_ref=target.at[owner], dst_ref=target.at[owner], send_sem=sems.at[0, step], recv_sem=sems.at[1, step],
        device_id={"rep": partner}, device_id_type=MESH,
    )


def move_kernel(whole, alike, split, relayed, *refs):
    amount = whole + len(split) + len(relayed)
    inputs, outputs, held = refs[:amount], refs[amount:2 * amount], refs[2 * amount:3 * amount]
    sems, local, *relays = refs[3 * amount:]
    me, core, sib, far = partners()
    diagonal = far + 1 - 2 * core
    devices = [{"shard": sib}, {"shard": far}, {"shard": diagonal}]
    if relayed:
        partner, away = replica_pair()
        devices.append({"rep": partner})
    greet(devices)
    waits, forwards, keeps, bulk = [], [], [], []
    number = 0
    for i, (source, target) in enumerate(zip(inputs, outputs)):
        if i < whole:
            to_far = send_to(source, target.at[me], sems, number, far)
            to_sib = send_to(source, target.at[me], sems, number + 1, sib)
            onward = send_to(target.at[far], target.at[far], sems, number + 2, sib)
            if i < alike:
                @pl.when(away == 0)
                def _():
                    to_far.start()
            else:
                to_far.start()
            to_sib.start()
            forwards.append((target, to_far, onward))
            waits.append(to_sib)
            kept = source
        elif i < whole + len(split):
            part = split[i - whole]
            for j, device in enumerate((far, diagonal, sib)):
                copy = send_to(part(source, device), target.at[me], sems, number + j, device)
                copy.start()
                waits.append(copy)
            kept = part(source, me)
        else:
            begin, arrive, passed = relays
            place = i - whole - len(split)
            part = relayed[place][0]
            taker = far // 2 * 2 + lax.axis_index("rep") % 2

            def across(owner, slot, source=source, target=target, part=part, place=place):
                return pltpu.make_async_remote_copy(
                    src_ref=part(source, taker), dst_ref=target.at[owner], send_sem=begin.at[place],
                    recv_sem=arrive.at[place, slot], device_id={"shard": taker}, device_id_type=MESH,
                )

            across(me, away).start()
            beside = send_to(part(source, sib), target.at[me], sems, number, sib)
            beside.start()
            waits.append(beside)
            bulk.append((place, target, across))
            kept = part(source, me)
        number += 3
        keep = pltpu.make_async_copy(kept, held[i], local.at[0, i])
        keep.start()
        keeps.append((keep, pltpu.make_async_copy(held[i], target.at[me], local.at[1, i])))
    for keep, store in keeps:
        keep.wait()
        store.start()
    for step, (target, to_far, onward) in enumerate(forwards):
        if step < alike:
            hop = pass_on(target, relays[2], 2 * len(relayed) + step, far)

            @pl.when(away == 0)
            def _():
                to_far.wait_recv()
                hop.start()

            @pl.when(away == 1)
            def _():
                hop.wait_recv()
        else:
            to_far.wait_recv()
        onward.start()
    for step, (target, to_far, onward) in enumerate(forwards):
        if step < alike:
            hop = pass_on(target, relays[2], 2 * len(relayed) + step, far)

            @pl.when(away == 0)
            def _():
                to_far.wait_send()
                hop.wait_send()
        else:
            to_far.wait_send()
        onward.wait()
    for copy in waits:
        copy.wait()
    for keep, store in keeps:
        store.wait()
    for place, target, across in bulk:
        passing = relayed[place][1]
        passed = relays[2]

        @pl.when(away == 0)
        def _():
            for slot, owner in enumerate((far, diagonal)):
                across(owner, slot).wait_recv()
                if passing:
                    pass_on(target, passed, 2 * place + slot, owner).start()

    for place, target, across in bulk:
        passing = relayed[place][1]
        passed = relays[2]
        across(me, away).wait_send()
        if passing:
            @pl.when(away == 0)
            def _():
                for slot, owner in enumerate((far, diagonal)):
                    pass_on(target, passed, 2 * place + slot, owner).wait_send()

            @pl.when(away == 1)
            def _():
                for slot, owner in enumerate((far, diagonal)):
                    pass_on(target, passed, 2 * place + slot, owner).wait_recv()


def move(name, number, wholes, splits, relayed=(), alike=0):
    inputs = list(wholes) + [entry[0] for entry in (*splits, *relayed)]
    shapes = [w.shape for w in wholes] + [entry[1] for entry in (*splits, *relayed)]
    out_shape = [jax.ShapeDtypeStruct((4,) + tuple(sh), v.dtype) for sh, v in zip(shapes, inputs)]
    scratch = [pltpu.VMEM(sh, v.dtype) for sh, v in zip(shapes, inputs)]
    scratch += [pltpu.SemaphoreType.DMA((2, 3 * len(inputs))), pltpu.SemaphoreType.DMA((2, len(inputs)))]
    if relayed:
        amount = len(relayed)
        scratch += [
            pltpu.SemaphoreType.DMA((amount,)), pltpu.SemaphoreType.DMA((amount, 2)),
            pltpu.SemaphoreType.DMA((2, 2 * amount + len(wholes))),
        ]
    return pl.pallas_call(
        functools.partial(move_kernel, len(wholes), alike, [f for _, _, f in splits], [entry[2:] for entry in relayed]),
        in_specs=any_space(len(inputs)),
        out_specs=any_space(len(inputs)),
        out_shape=out_shape,
        scratch_shapes=scratch,
        compiler_params=pltpu.CompilerParams(
            collective_id=number, has_side_effects=True, vmem_limit_bytes=VMEM_LIMIT
        ),
        cost_estimate=pl.CostEstimate(
            flops=0, bytes_accessed=sum(4 * v.size * v.dtype.itemsize for v in inputs), transcendentals=0
        ),
        name=name,
    )(*inputs)


HIDDEN_WINDOW = 1664


def hidden_columns(ref, owner):
    return ref.at[:, pl.ds(pl.multiple_of(owner // 2 * 3200 + owner % 2 * 1536, LANES), HIDDEN_WINDOW)]


QUERY_WINDOW = 1024


def query_window(ref, owner):
    return ref.at[:, pl.ds(pl.multiple_of(owner // 2 * 1920 + owner % 2 * 896, LANES), QUERY_WINDOW)]


def latent_window(ref, owner):
    return ref.at[:, pl.ds(pl.multiple_of(owner * 1280, LANES), 1280)]


def first_move(query_down, latent_down, query_up, latent_up, segments, gate, up, count):
    if count != 4:
        gate, up = spread_hidden(gate, up, count)
        return (
            plain_gather(query_down), plain_gather(latent_down), pad_heads(spread(query_up, count)),
            spread(latent_up, count), plain_gather(segments), gate, up,
        )
    part = (gate.shape[0], HIDDEN_WINDOW)
    heads = [(query_up, (query_up.shape[0], QUERY_WINDOW), query_window),
             (latent_up, (latent_up.shape[0], 1280), latent_window)]
    relayed = []
    if shared_links(count):
        relayed = [entry + (True,) for entry in heads]
        relayed += [(gate, part, hidden_columns, True), (up, part, hidden_columns, False)]
        heads = []
    down_q, down_kv, groups, up_q, up_kv, *hidden = move(
        "first_move", 7, [query_down, latent_down, segments], heads, relayed, 2 if relayed else 0
    )
    merge = lambda value: value.reshape((-1,) + value.shape[2:])
    up_q = lax.dynamic_slice_in_dim(merge(up_q), lax.axis_index("shard") % 2 * 64, 960, 1)
    gate, up = hidden if relayed else spread_hidden(gate, up, count)
    return merge(down_q), merge(down_kv), pad_heads(up_q), merge(up_kv), merge(groups), gate, up


EXCHANGE_WIDTH = 1280


def last_move(grad_lat, gain_terms, query_part, latent_part, count):
    if count != 4:
        parts = (
            plain_gather(grad_lat), plain_gather(gain_terms), collect(cut_heads(query_part), count),
            collect(latent_part, count),
        )
        return parts, lambda parts: parts
    side = lambda value: value.transpose(1, 0, 2).reshape(value.shape[1], -1)
    same = lambda value: jnp.broadcast_to(value[None], (count,) + value.shape)
    wide = lambda value: jnp.pad(value, ((0, 0), (0, EXCHANGE_WIDTH - value.shape[1])))
    amount = gain_terms.shape[1]
    gain_rows = -(-amount // EXCHANGE_WIDTH)
    gain_rows += -gain_rows % 16
    gains = jnp.pad(gain_terms[0].astype(bf16), (0, gain_rows * EXCHANGE_WIDTH - amount)).reshape(gain_rows, -1)
    pieces = [
        query_part.reshape(count, -1, EXCHANGE_WIDTH), latent_part.reshape(count, -1, EXCHANGE_WIDTH),
        same(wide(grad_lat)), same(gains),
    ]
    got = lax.all_to_all(jnp.concatenate(pieces, axis=1), "shard", 0, 0, tiled=True)
    ends = [0]
    for piece in pieces:
        ends.append(ends[-1] + piece.shape[1])
    def finish(got):
        got_q, got_kv, lat, gains = (got[:, start:end] for start, end in zip(ends, ends[1:]))
        return (
            lat.reshape(-1, EXCHANGE_WIDTH)[:, :grad_lat.shape[1]],
            gains.reshape(count, -1)[:, :amount].astype(f32), cut_heads(side(got_q)), side(got_kv),
        )

    return got, finish


def place_kernel(*refs):
    me, core, sib, far = partners()
    *parts, out_ref = refs
    out_ref[...] = jnp.zeros_like(out_ref)
    for owner, part in zip((me, sib, far, far + 1 - 2 * core), parts):
        lanes = pl.ds(pl.multiple_of(owner // 2 * 3200 + owner % 2 * 1536, LANES), HIDDEN_WINDOW)
        out_ref[:, lanes] += part[...].astype(f32)


def head_lanes(value):
    return jnp.pad(value, ((0, 0), (NOPE, LANES - NOPE - ROPE)))


def layer_forward(hidden, own_tables, tables, gains, weights, passing, lacking, early):
    input_gain, query_gain, latent_gain, post_gain = gains
    down_both, query_up, latent_up, output_weight, gate_weight, up_weight, down_weight = weights
    scale_in = norm_scale(hidden)
    normed = (hidden * scale_in * input_gain).astype(bf16)
    down_q, down_kv = down_both
    latent_q = project(normed, down_q)
    latent_kv = project(normed, down_kv)
    latent = latent_kv[:, :KVRANK]
    scale_q = norm_scale(latent_q)
    scale_kv = norm_scale(latent)
    own_in = jnp.concatenate(
        [
            latent_q * scale_q * query_gain,
            latent * scale_kv * latent_gain,
            head_lanes(rotate(latent_kv[:, KVRANK:], *own_tables)),
        ],
        axis=1,
    ).astype(bf16)
    all_in = gather(own_in, 0, 384)
    all_in, early = together(all_in, early)
    if lacking is not None:
        early = plain_gather(early)
    query_in = all_in[:, :QRANK]
    kv_in = all_in[:, QRANK:QRANK + KVRANK]
    shared = all_in[:, QRANK + KVRANK:]
    attended, queries, keyval, logs = attend(
        project(query_in, query_up), project(kv_in, latent_up), shared, tables
    )
    if lacking:
        mixed, normed_two, up_weight = output_norm(attended, output_weight, hidden, post_gain, up_weight)
    else:
        mixed, normed_two = output_norm(attended, output_weight, hidden, post_gain)
    normed_two, early = together(normed_two, early)
    merge = lambda value: value.reshape(D, -1)
    gate = project(normed_two, merge(gate_weight)).astype(bf16)
    up = project(normed_two, merge(up_weight)).astype(bf16)
    activated = (jax.nn.silu(gate.astype(f32)) * up.astype(f32)).astype(bf16)
    def outputs(value):
        return down_project(value, down_weight, mixed, passing)

    kept = (hidden, scale_in, normed, latent_q, scale_q, latent, scale_kv, query_in, kv_in,
            shared, queries, keyval, logs, attended, mixed, normed_two, gate, up)
    return (outputs, activated, kept, merge(gate_weight), merge(up_weight), early)


def gate_backward(grad_act, gate, up):
    sigmoid = jax.nn.sigmoid(gate)
    grad_gate = (grad_act * up * sigmoid * (1.0 + gate * (1.0 - sigmoid))).astype(bf16)
    grad_up = (grad_act * gate * sigmoid).astype(bf16)
    return grad_gate, grad_up


def mlp_backward(grad_out, kept, gains, weights, gather_down, wanted):
    mixed, gate, up = kept[14], kept[16], kept[17]
    gate_weight, up_weight, down_weight = weights[4:]
    own_down = (residual_scale * grad_out).astype(bf16)
    grad_down, wanted = together(gather_down(own_down), wanted)
    grad_gate, grad_up = gate_backward(contract_cols(grad_down, down_weight), gate.astype(f32), up.astype(f32))
    grad_mixed, dgain_post, grad_branch = mlp_back(
        grad_gate, grad_up, gate_weight, up_weight, mixed, grad_out, gains[3]
    )
    return (grad_gate, grad_up), wanted, grad_down, grad_mixed, dgain_post[0], grad_branch


def attention_backward(grad_mixed, grad_branch, kept, own_tables, tables, gains, weights, wanted):
    (hidden, scale_in, normed, latent_q, scale_q, latent, scale_kv, query_in, kv_in,
     shared, queries, keyval, logs, attended, mixed, normed_two, gate, up) = kept
    input_gain, query_gain, latent_gain, post_gain = gains
    down_both, query_up, latent_up, output_weight = weights[:4]
    cosine, sine = own_tables
    grad_attended = contract_cols(grad_branch, output_weight).astype(bf16)
    grad_query, grad_keyval, grad_shared = attend_back(
        queries, keyval, shared, tables, grad_attended, attended, logs
    )
    grad_in = latent_back(grad_query, grad_keyval, grad_shared, query_up, latent_up)
    grad_in, wanted = together(grad_in, wanted)
    grad_latent_q, dgain_query = norm_back(latent_q, scale_q, query_gain, grad_in[:, :QRANK])
    grad_latent, dgain_latent = norm_back(
        latent, scale_kv, latent_gain, grad_in[:, QRANK:QRANK + KVRANK]
    )
    start = QRANK + KVRANK + NOPE
    grad_shared = rotate(grad_in[:, start:start + ROPE], cosine, -sine)
    grad_lat = jnp.concatenate(
        [grad_latent_q, grad_latent, jnp.pad(grad_shared, ((0, 0), (0, LANES - ROPE)))], axis=1
    ).astype(bf16)
    down_q, down_kv = down_both
    grad_normed = contract_cols(grad_lat[:, :QRANK], down_q) + contract_cols(
        grad_lat[:, QRANK:QRANK + KVRANK + ROPE], down_kv
    )
    grad_hidden_norm, dgain_input = norm_back(hidden, scale_in, input_gain, grad_normed)
    grad_hidden = grad_mixed + grad_hidden_norm
    found = (grad_branch, grad_query, grad_keyval, grad_lat)
    return (grad_hidden, found, (dgain_input, dgain_query, dgain_latent), wanted)


def spread(weight, count):
    rows, columns = weight.shape
    parts = weight.reshape(rows, count, columns // count).transpose(1, 0, 2)
    return lax.all_to_all(parts, "shard", 0, 0, tiled=True).reshape(rows * count, columns // count)


def collect(grad, count):
    rows, columns = grad.shape
    parts = lax.all_to_all(
        grad.reshape(count, rows // count, columns), "shard", 0, 0, tiled=True
    )
    return parts.transpose(1, 0, 2).reshape(rows // count, columns * count)


def pad_heads(weight):
    rows, columns = weight.shape
    heads = weight.reshape(rows, columns // (NOPE + ROPE), NOPE + ROPE)
    return jnp.pad(heads, ((0, 0), (0, 0), (0, LANES - NOPE - ROPE))).reshape(rows, -1)


def cut_heads(grad):
    rows, columns = grad.shape
    heads = grad.reshape(rows, columns // LANES, LANES)[:, :, :NOPE + ROPE]
    return heads.reshape(rows, -1)


def swap(value, step):
    count = lax.axis_size("shard")
    return lax.ppermute(value, "shard", [(source, source ^ step) for source in range(count)])


def hidden_window(count):
    size = FF // count
    width = -(-size // LANES) * LANES
    starts = [owner * size // LANES * LANES for owner in range(count)]
    starts = [min(start, FF - width) for start in starts]
    return size, width, starts, [owner * size - start for owner, start in enumerate(starts)]


def take_at(table, place):
    return jnp.asarray(table, jnp.int32)[place]


def shared_links(count):
    return count == 4 and lax.axis_size("rep") % 2 == 0


def spread_hidden(gate, up, count):
    me = lax.axis_index("shard")
    size, width, starts, offsets = hidden_window(count)
    rows = gate.shape[0]
    results = []
    for weight in (gate, up):
        whole = jnp.zeros((rows * count, width), bf16)
        for step in range(count):
            owner = me ^ step
            part = lax.dynamic_slice(weight, (0, take_at(starts, owner)), (rows, width))
            if step:
                part = swap(part, step)
            whole = lax.dynamic_update_slice(whole, part, (owner * rows, 0))
        results.append(whole)
    return results


def window_rows(down, count):
    size, width, starts, offsets = hidden_window(count)
    whole = jnp.zeros((width, down.shape[1]), bf16)
    return lax.dynamic_update_slice(whole, down, (take_at(offsets, lax.axis_index("shard")), 0))


def chip_gradients_kernel(order_ref, two_ref, gate_ref, up_ref, gate_out, up_out, turned):
    tokens, rows = two_ref.shape
    piece = 512
    for start in range(0, tokens, piece):
        size = min(piece, tokens - start)
        turned[:, start:start + size] = two_ref[start:start + size, :].T
    width = gate_ref.shape[1]
    whole = width // piece
    for grad, out in ((gate_ref, gate_out), (up_ref, up_out)):
        def tile(step):
            lanes = columns(step, piece)
            out[0, :, lanes] = project(turned[...], grad[:, lanes]).astype(bf16)

        each(whole, False, tile)
        if whole * piece < width:
            out[0, :, whole * piece:] = project(turned[...], grad[:, whole * piece:]).astype(bf16)


def chip_gradients(two_all, grad_gate, grad_up):
    me, core, sib, far = partners()
    tokens, width = grad_gate.shape
    rows = D // 4
    held = pl.BlockSpec((tokens, width), lambda i, order: (0, 0), pipeline_mode=pl.Buffered(1))
    part = pl.BlockSpec((1, rows, width), lambda i, order: (i, 0, 0))
    gate, up = pl.pallas_call(
        chip_gradients_kernel,
        grid_spec=pltpu.PrefetchScalarGridSpec(
            num_scalar_prefetch=1,
            grid=(2,),
            in_specs=[pl.BlockSpec((tokens, rows), lambda i, order: (0, order[i])), held, held],
            out_specs=[part, part],
            scratch_shapes=[pltpu.VMEM((rows, tokens), bf16)],
        ),
        out_shape=[jax.ShapeDtypeStruct((2, rows, width), bf16)] * 2,
        compiler_params=pltpu.CompilerParams(vmem_limit_bytes=VMEM_LIMIT),
        name="chip_gradients",
    )(jnp.stack([sib, me]).astype(jnp.int32), two_all, grad_gate, grad_up)
    return [gate[0], up[0], gate[1], up[1]]


def recompute_kernel(from_ref, own_ref, here_ref, two_ref, near_ref, beside_ref, gate_ref, up_ref, rows_ref,
                     act_own, gate_own, up_own, act_out, gate_out, up_out, down_ref):
    place = pl.program_id(0)
    width = gate_ref.shape[1]
    piece = 512

    @pl.when(own_ref[place] == 1)
    def _():
        act_out[...] = act_own[...]
        gate_out[...] = gate_own[...]
        up_out[...] = up_own[...]

    @pl.when((own_ref[place] == 0) & (here_ref[place] == 1))
    def _():
        down_ref[...] = near_ref[...]

    @pl.when((own_ref[place] == 0) & (here_ref[place] == 0))
    def _():
        down_ref[...] = beside_ref[...]

    @pl.when(own_ref[place] == 0)
    def _():
        def tile(lanes, some_rows):
            gate = project(two_ref[...], gate_ref[:, lanes])
            up = project(two_ref[...], up_ref[:, lanes])
            grad = contract_cols(down_ref[...], rows_ref[some_rows, :])
            sigmoid = jax.nn.sigmoid(gate)
            silu = gate * sigmoid
            act_out[:, lanes] = (silu * up).astype(bf16)
            gate_out[:, lanes] = (grad * up * sigmoid * (1.0 + gate * (1.0 - sigmoid))).astype(bf16)
            up_out[:, lanes] = (grad * silu).astype(bf16)

        each(width // piece, False, lambda step: tile(columns(step, piece), columns(step, piece)))
        if width % piece:
            rest = slice(width // piece * piece, width)
            tile(rest, rest)


def recompute(two_all, down_halves, gate_columns, up_columns, down_rows, own):
    reps = lax.axis_size("rep")
    tokens, width = two_all.shape[0], gate_columns.shape[1]
    tile = own[0].shape[0] // 2
    places = jnp.arange(tokens // tile, dtype=jnp.int32)
    half = places // reps
    is_own = places % reps == lax.axis_index("rep")
    is_here = half == lax.axis_index("shard") % 2
    whole = lambda value: pl.BlockSpec(value.shape, lambda i, a, b, c: (0, 0), pipeline_mode=pl.Buffered(1))
    wide = pl.BlockSpec((tile, D), lambda i, a, b, c: (i, 0))
    again = pl.BlockSpec((tile, D), lambda i, a, b, c: (i % reps, 0))
    mine = pl.BlockSpec((tile, width), lambda i, a, b, c: (a[i], 0), pipeline_mode=pl.Buffered(1))
    part = pl.BlockSpec((tile, width), lambda i, a, b, c: (i, 0))
    return pl.pallas_call(
        recompute_kernel,
        grid_spec=pltpu.PrefetchScalarGridSpec(
            num_scalar_prefetch=3,
            grid=(tokens // tile,),
            in_specs=[wide, again, again, whole(gate_columns), whole(up_columns), whole(down_rows), mine, mine, mine],
            out_specs=[part] * 3,
            scratch_shapes=[pltpu.VMEM((tile, D), bf16)],
        ),
        out_shape=[jax.ShapeDtypeStruct((tokens, width), bf16)] * 3,
        compiler_params=pltpu.CompilerParams(vmem_limit_bytes=VMEM_LIMIT),
        name="recompute",
    )(half, is_own.astype(jnp.int32), is_here.astype(jnp.int32), two_all, *down_halves,
      gate_columns, up_columns, down_rows, *own)


def down_gradient_kernel(act_ref, near_ref, beside_ref, out_ref, turned):
    tokens, width = act_ref.shape
    size = out_ref.shape[0]
    piece = 512

    @pl.when(pl.program_id(0) == 0)
    def _():
        for start in range(0, tokens, piece):
            turned[:, start:start + piece] = act_ref[start:start + piece, :].T

    core = lax.axis_index("shard") % 2
    offset = core * (width - size)
    half = size // 2
    some = tokens // 2
    near = pl.ds(pl.multiple_of(core * some, LANES), some)
    beside = pl.ds(pl.multiple_of((1 - core) * some, LANES), some)

    def tile(step):
        rows = pl.ds(pl.multiple_of(step * half, 16), half)
        source = pl.ds(pl.multiple_of(step * half + offset, 16), half)
        out_ref[rows, :] = project(turned[source, near], near_ref[...]) + project(turned[source, beside], beside_ref[...])

    each(2, False, tile)


def down_gradient(activated_all, down_halves):
    tokens, width = activated_all.shape
    size, piece = FF // 4, 512
    return pl.pallas_call(
        down_gradient_kernel,
        grid=(D // piece,),
        in_specs=[pl.BlockSpec((tokens, width), lambda i: (0, 0), pipeline_mode=pl.Buffered(1)),
                  pl.BlockSpec((tokens // 2, piece), lambda i: (0, i)), pl.BlockSpec((tokens // 2, piece), lambda i: (0, i))],
        out_specs=pl.BlockSpec((size, piece), lambda i: (0, i)),
        out_shape=jax.ShapeDtypeStruct((size, D), f32),
        scratch_shapes=[pltpu.VMEM((width, tokens), bf16)],
        compiler_params=pltpu.CompilerParams(vmem_limit_bytes=VMEM_LIMIT),
        name="down_gradient",
    )(activated_all, *down_halves)


def half_everywhere(group, count):
    if count != 4:
        return group
    rows = group.shape[0] // 2
    half = lax.dynamic_slice_in_dim(group, lax.axis_index("shard") % 2 * rows, rows, 0)
    return lax.all_gather(half, "rep", axis=0, tiled=True)


def everyone(half, count):
    if count != 4:
        return lax.all_gather(half, "rep", axis=0, tiled=True)
    return lax.all_gather(half, "shard", axis=0, tiled=True, axis_index_groups=[[0, 1], [2, 3]])


def owner_gradient(two_all, grad, owner, count):
    rows = D // count
    left = lax.dynamic_slice(two_all, (0, owner * rows), (two_all.shape[0], rows))
    return contract_rows(left, grad).astype(bf16)


def place_windows(parts, count):
    size, width, starts, offsets = hidden_window(count)
    rows = parts[0].shape[0]
    if count == 4:
        tile = 64
        return pl.pallas_call(
            place_kernel,
            grid=(rows // tile,),
            in_specs=[pl.BlockSpec((tile, width), lambda i: (i, 0))] * 4,
            out_specs=pl.BlockSpec((tile, FF), lambda i: (i, 0)),
            out_shape=jax.ShapeDtypeStruct((rows, FF), f32),
            compiler_params=pltpu.CompilerParams(vmem_limit_bytes=VMEM_LIMIT),
            cost_estimate=pl.CostEstimate(flops=0, bytes_accessed=rows * FF * 8, transcendentals=0),
            name="place_windows",
        )(*parts)
    me = lax.axis_index("shard")
    gathered = jnp.zeros((count, rows, width), bf16)
    for step, part in enumerate(parts):
        gathered = lax.dynamic_update_slice(gathered, part[None], (me ^ step, 0, 0))
    pieces = [gathered[owner, :, offset:offset + size] for owner, offset in enumerate(offsets)]
    return jnp.concatenate(pieces, axis=1).astype(f32)


def together(*values):
    return lax.optimization_barrier(values)


def body(tokens, segment_ids, input_gain, query_gain, latent_gain, post_gain, query_down, query_up,
         latent_down, latent_up, output_weight, gate_weight, up_weight, down_weight, cotangent):
    at_start = lax.axis_index("section") == 0
    count = lax.axis_size("shard")
    size, width, starts, offsets = hidden_window(count)
    gains = (input_gain[0], query_gain[0], latent_gain[0], post_gain[0])
    down_q, down_kv, query_up_all, latent_up_all, groups, gate_columns, up_columns = first_move(
        query_down[0], latent_down[0], query_up[0], latent_up[0], segment_ids, gate_weight[0], up_weight[0], count
    )
    down_both = (down_q, down_kv)
    own_tables = tuple(t.reshape(-1, ROPE // 2) for t in slot_tables(segment_ids))
    tables = head_tables(groups)

    weights = (down_both, query_up_all, latent_up_all, output_weight[0], gate_columns, up_columns, down_weight[0])
    start = tokens.astype(f32)
    last = cotangent.astype(f32)
    last_down = (residual_scale * last).astype(bf16)
    outputs, activated, _, gate_columns, up_columns, all_last = layer_forward(
        start, own_tables, tables, gains, weights, True, shared_links(count), last_down
    )
    leaving, low, received, down_rows = outputs(activated)
    weights = weights[:4] + (gate_columns, up_columns, down_rows)
    entering = jnp.where(at_start, start, received.astype(f32))
    _, kept_activated, kept, _, _, _ = layer_forward(
        entering, own_tables, tables, gains, weights, False, None, all_last
    )

    (hidden, scale_in, normed, latent_q, scale_q, latent, scale_kv, query_in, kv_in,
     shared, queries, keyval, logs, attended, mixed, normed_two, gate, up) = kept
    half_two = half_everywhere(normed_two, count)
    _, _, _, grad_mixed, _, grad_branch = mlp_backward(last, kept, gains, weights, lambda own: all_last, at_start)
    grad, _, _, half_two = attention_backward(
        grad_mixed, grad_branch, kept, own_tables, tables, gains, weights, half_two
    )
    two_all = everyone(half_two, count)
    grad_low, kept_activated = together(grad.astype(bf16), kept_activated)
    returned = lax.ppermute(grad_low, "section", [(1, 0)])
    leaving, boundary = down_project(kept_activated, down_rows, mixed, False)
    incoming = jnp.where(at_start, returned.astype(f32), last)
    incoming, boundary = together(incoming, boundary)

    own_grads, two_all, grad_down, grad_mixed, dgain_post, grad_branch = mlp_backward(
        incoming, kept, gains, weights, lambda own: gather(own, 1, 512), two_all
    )
    half_down = half_everywhere(grad_down, count)
    part_output = contract_rows(attended, grad_branch).astype(bf16)
    grad_branch, part_output = together(grad_branch, part_output)

    grad, found, (dgain_input, dgain_query, dgain_latent), _ = attention_backward(
        grad_mixed, grad_branch, kept, own_tables, tables, gains, weights, at_start
    )
    grad_branch, grad_query, grad_keyval, grad_lat = found
    gain_terms = jnp.concatenate([dgain_input, dgain_query, dgain_latent, dgain_post])[None]
    normed_rows = lax.all_to_all(
        normed.reshape(normed.shape[0], count, -1).transpose(1, 0, 2), "shard", 0, 0, tiled=True
    ).reshape(normed.shape[0] * count, -1)
    part_query = contract_rows(query_in, grad_query).astype(bf16)
    part_latent = contract_rows(kv_in, grad_keyval).astype(bf16)
    gain_terms, half_down = together(gain_terms, half_down)
    exchanged, exchange_end = last_move(grad_lat, gain_terms, part_query, part_latent, count)
    part_output, half_down = together(part_output, half_down)
    down_all = [half_down, swap(half_down, 1)] if count == 4 else everyone(half_down, count)
    total_output = lax.psum(part_output, "rep")
    down_all, two_all, own_grads, normed_rows = together(down_all, two_all, own_grads, normed_rows)
    if count == 4:
        activated_all, grad_gate, grad_up = recompute(
            two_all, down_all, gate_columns, up_columns, down_rows, (kept_activated, *own_grads)
        )
    else:
        gate_all = project(two_all, gate_columns)
        up_all = project(two_all, up_columns)
        activated_all = (jax.nn.silu(gate_all) * up_all).astype(bf16)
        grad_gate, grad_up = gate_backward(contract_cols(down_all, down_rows), gate_all, up_all)
    def attention_shares(exchanged):
        lat_all, gains_all, part_query, part_latent = exchange_end(exchanged)
        part_down = contract_rows(normed_rows, lat_all[:, :QRANK + KVRANK + ROPE]).astype(bf16)
        part_gains = jnp.sum(gains_all, axis=0).astype(bf16)
        side = part_down.shape[1]
        gain_rows = -(-part_gains.shape[0] // side)
        part_gains = jnp.pad(part_gains, (0, gain_rows * side - part_gains.shape[0])).reshape(gain_rows, side)
        part_down = jnp.concatenate([part_down, part_gains], axis=0)
        return part_down, part_latent, part_query

    me = lax.axis_index("shard")
    if count == 4:
        grad_gate, grad_up, total_output = together(grad_gate, grad_up, total_output)
        away = [owner_gradient(two_all, grad_gate, me ^ step, count) for step in (2, 3)]
        brought = [[swap(part, 2 + i) for i, part in enumerate(away)]]
        two_all, _, exchanged, total_output = together(two_all, away, exchanged, total_output)
        shares = attention_shares(exchanged)
        two_all, *shares = together(two_all, *shares)
        total_down_both, total_latent, total_query = lax.psum(tuple(shares), "rep")
        away = [owner_gradient(two_all, grad_up, me ^ step, count) for step in (2, 3)]
        brought.append([swap(part, 2 + i) for i, part in enumerate(away)])
        two_all, _ = together(two_all, away)
        near = chip_gradients(two_all, grad_gate, grad_up)
        activated_all, near[0], brought[0] = together(activated_all, near[0], brought[0])
        total_down = down_gradient(activated_all, down_all)
        hidden_parts = [[near[2 + i], swap(near[i], 1), *brought[i]] for i in range(2)]
        total_down, hidden_parts[0] = together(total_down, hidden_parts[0])
    else:
        parts = [
            [owner_gradient(two_all, grad, me ^ step, count) for grad in (grad_gate, grad_up)] for step in range(count)
        ]
        hidden_parts = [
            [swap(parts[step][i], step) if step else parts[step][i] for step in range(count)] for i in range(2)
        ]
        total_down_both, total_latent, total_query = lax.psum(attention_shares(exchanged), "rep")
        total_down = contract_rows(activated_all, down_all)
        total_down = lax.dynamic_slice_in_dim(total_down, take_at(offsets, me), size, 0)
    total_gate = place_windows(hidden_parts[0], count)
    total_gate, hidden_parts[1][0] = together(total_gate, hidden_parts[1][0])
    total_up = place_windows(hidden_parts[1], count)
    total_up, total_down_both, total_latent, total_query = together(
        total_up, total_down_both, total_latent, total_query
    )
    gain_rows = total_down_both.shape[0] - D // count
    gain_totals = total_down_both[-gain_rows:].reshape(-1).astype(f32)
    total_down_both = total_down_both[:-gain_rows].astype(f32)
    total_query, total_latent = total_query.astype(f32), total_latent.astype(f32)
    first, second, third = D, D + QRANK, D + QRANK + KVRANK
    gain_totals = (gain_totals[:first], gain_totals[first:second], gain_totals[second:third], gain_totals[third:third + D])
    return (
        boundary[None],
        grad[None],
        gain_totals[0][None],
        gain_totals[1][None],
        gain_totals[2][None],
        gain_totals[3][None],
        total_down_both[None, :, :QRANK],
        total_query[None],
        total_down_both[None, :, QRANK:],
        total_latent[None],
        total_output.astype(f32)[None],
        total_gate[None],
        total_up[None],
        total_down[None],
    )


def solution(mesh):
    tokens = P(("rep", "shard"), None)
    gain = P("section", None)
    weight = P("section", "shard", None)
    out = P("section", ("rep", "shard"), None)
    return jax.shard_map(
        body,
        mesh=mesh,
        in_specs=(tokens, tokens) + (gain,) * 4 + (weight,) * 8 + (tokens,),
        out_specs=(out, out) + (gain,) * 4 + (weight,) * 8,
        check_vma=False,
    )
```

```python
import functools
import math

import jax
import jax.numpy as jnp
from jax import lax
from jax.experimental import pallas as pl
from jax.experimental.pallas import tpu as pltpu
from jax.sharding import PartitionSpec as P

D = 2560
HEADS = 40
NOPE = 64
ROPE = 32
VDIM = 64
QRANK = 768
KVRANK = 256
FF = 6400
SLOT = 96
LANES = 128

epsilon = 1e-05
residual_scale = 1.4 / math.sqrt(62.0)
masked_score = -1e30
score_scale = 1.0 / math.sqrt(NOPE + ROPE)
bf16 = jnp.bfloat16
f32 = jnp.float32


def norm_scale(value):
    return lax.rsqrt(jnp.mean(value * value, axis=-1, keepdims=True) + epsilon)


def norm_back(value, scale, gain, grad):
    weighted = grad * gain
    inner = jnp.mean(value * weighted, axis=-1, keepdims=True)
    grad_value = scale * weighted - value * (scale * scale * scale) * inner
    return (grad_value, jnp.sum(grad * value * scale, axis=0))


def rotate(value, cosine, sine):
    half = value.shape[-1] // 2
    front = value[..., :half]
    back = value[..., half:]
    return jnp.concatenate([front * cosine - back * sine, back * cosine + front * sine], axis=-1)


def slot_tables(segments):
    index = jnp.arange(SLOT, dtype=jnp.int32)
    first_index = jnp.sum((segments[:, None, :] < segments[:, :, None]).astype(jnp.int32), axis=-1)
    position = (index - first_index).astype(f32)
    freq = jnp.exp(jnp.arange(ROPE // 2, dtype=f32) * (-2.0 * math.log(10000.0) / ROPE))
    angle = position[..., None] * freq
    return (jnp.cos(angle), jnp.sin(angle))


def head_tables(segments):
    cosine, sine = slot_tables(segments)
    slots = segments.shape[0]
    ones = jnp.ones((slots, SLOT, NOPE), f32)
    tail = jnp.zeros((slots, SLOT, LANES - NOPE - ROPE), f32)
    half = jnp.zeros_like(sine)
    keep = jnp.concatenate([ones, cosine, cosine, tail], axis=-1)
    left = jnp.concatenate([0.0 * ones, -sine, half, tail], axis=-1)
    right = jnp.concatenate([0.0 * ones, half, sine, tail], axis=-1)
    index = jnp.arange(SLOT, dtype=jnp.int32)
    allowed = (segments[:, :, None] == segments[:, None, :]) & (index[None, :] <= index[:, None])
    mask = jnp.where(allowed, 0.0, masked_score).astype(f32)
    flat = lambda table: table.reshape(slots * SLOT, LANES)
    return (flat(keep), flat(left), flat(right), mask, mask.transpose(0, 2, 1))


def contract_rows(left, right):
    return lax.dot_general(left, right, (((0,), (0,)), ((), ())), preferred_element_type=f32)


def contract_cols(left, right):
    return lax.dot_general(left, right, (((1,), (1,)), ((), ())), preferred_element_type=f32)


def project(left, weight):
    return jnp.dot(left, weight, preferred_element_type=f32)


def low_lanes():
    return lax.broadcasted_iota(jnp.int32, (SLOT, LANES), 1) < NOPE


HEAD_GROUP = 5
HEAD_ROWS = 16


def attend_kernel(heads, q_ref, kv_ref, sh_ref, keep_ref, left_ref, right_ref, mask_ref,
                  att_ref, qo_ref, kvo_ref, log_ref):
    low = low_lanes()
    lane = lax.broadcasted_iota(jnp.int32, (SLOT, LANES), 1)
    shared = sh_ref[...].astype(f32)
    keep, left, right = keep_ref[...], left_ref[...], right_ref[...]
    mask = mask_ref[0]
    tallest = jnp.zeros((SLOT, LANES), f32)
    sums = jnp.ones((SLOT, LANES), f32)
    for first in range(0, heads, HEAD_GROUP):
        group = range(first, min(first + HEAD_GROUP, heads))
        scores, values = [], []
        for head in group:
            lanes = slice(head * LANES, (head + 1) * LANES)
            q = q_ref[:, lanes]
            q = q * keep + pltpu.roll(q, LANES - 16, 1) * left + pltpu.roll(q, 16, 1) * right
            q = q.astype(bf16)
            qo_ref[:, lanes] = q
            kv = kv_ref[:, lanes]
            kvo_ref[:, lanes] = kv.astype(bf16)
            k = jnp.where(low, kv, shared).astype(bf16)
            values.append(jnp.where(low, 1.0, kv).astype(bf16))
            scores.append(contract_cols(q, k) * score_scale + mask)
        tops = [jnp.max(score, axis=-1, keepdims=True) for score in scores]
        terms = [jnp.exp(score - top).astype(bf16) for score, top in zip(scores, tops)]
        outs = [project(term, value) for term, value in zip(terms, values)]
        for head, top, out in zip(group, tops, outs):
            turned = pltpu.roll(out, NOPE, 1)
            tallest = jnp.where(lane == head, top, tallest)
            sums = jnp.where(lane == head, out, sums)
            pair = (head // 2) * LANES
            if head % 2 == 0:
                att = turned / out
                att_ref[:, pair:pair + VDIM] = att[:, :VDIM].astype(bf16)
            else:
                att = out / turned
                att_ref[:, pair + VDIM:pair + LANES] = att[:, VDIM:].astype(bf16)
    log_ref[0] = (tallest + jnp.log(sums)).T[:HEAD_ROWS, :]


def attention_cost(tokens, heads, passes):
    return pl.CostEstimate(
        flops=passes * tokens * heads * SLOT * LANES * 20, bytes_accessed=tokens * heads * LANES * 12,
        transcendentals=tokens * heads * SLOT,
    )


def attend(query, keyval, shared, tables):
    tokens = query.shape[0]
    heads = query.shape[1] // LANES
    wide = pl.BlockSpec((SLOT, heads * LANES), lambda s: (s, 0))
    one = pl.BlockSpec((SLOT, LANES), lambda s: (s, 0))
    square = pl.BlockSpec((1, SLOT, SLOT), lambda s: (s, 0, 0))
    return pl.pallas_call(
        functools.partial(attend_kernel, heads),
        grid=(tokens // SLOT,),
        in_specs=[wide, wide, one, one, one, one, square],
        out_specs=[pl.BlockSpec((SLOT, heads * VDIM), lambda s: (s, 0)), wide, wide,
                   pl.BlockSpec((1, HEAD_ROWS, SLOT), lambda s: (s, 0, 0))],
        out_shape=[
            jax.ShapeDtypeStruct((tokens, heads * VDIM), bf16),
            jax.ShapeDtypeStruct(query.shape, bf16),
            jax.ShapeDtypeStruct(keyval.shape, bf16),
            jax.ShapeDtypeStruct((tokens // SLOT, HEAD_ROWS, SLOT), f32),
        ],
        cost_estimate=attention_cost(tokens, heads, 4),
        name="attend",
    )(query, keyval, shared, *tables[:4])


def attend_back_kernel(heads, q_ref, kv_ref, sh_ref, keep_ref, left_ref, right_ref, mask_ref,
                       ga_ref, att_ref, log_ref, gq_ref, gkv_ref, gsh_ref):
    low = low_lanes()
    shared = sh_ref[...].astype(f32)
    keep, left, right = keep_ref[...], left_ref[...], right_ref[...]
    mask = mask_ref[0]
    total = jnp.zeros((SLOT, LANES), f32)
    product = ga_ref[...].astype(f32) * att_ref[...].astype(f32)
    high = product.astype(bf16)
    rest = (product - high.astype(f32)).astype(bf16)
    shape = (HEAD_ROWS, product.shape[1])
    chosen = lax.broadcasted_iota(jnp.int32, shape, 1) // VDIM == lax.broadcasted_iota(jnp.int32, shape, 0)
    chosen = jnp.where(chosen, 1.0, 0.0).astype(bf16)
    inner = contract_cols(chosen, high) + contract_cols(chosen, rest)
    for first in range(0, heads, HEAD_GROUP):
        group = range(first, min(first + HEAD_GROUP, heads))
        queries, keys, grads, scores, grad_probs = [], [], [], [], []
        for head in group:
            lanes = slice(head * LANES, (head + 1) * LANES)
            q = q_ref[:, lanes]
            kvb = kv_ref[:, lanes]
            k = jnp.where(low, kvb.astype(f32), shared).astype(bf16)
            if head % 2 == 0 and head == heads - 1:
                ga = ga_ref[:, head * VDIM:(head + 1) * VDIM].astype(f32)
                ga = jnp.concatenate([jnp.zeros_like(ga), ga], axis=1)
            else:
                start = (head // 2) * LANES
                ga = ga_ref[:, start:start + LANES].astype(f32)
                if head % 2 == 0:
                    ga = pltpu.roll(ga, NOPE, 1)
                ga = jnp.where(low, 0.0, ga)
            ga = ga.astype(bf16)
            queries.append(q)
            keys.append(k)
            grads.append(ga)
            scores.append(contract_cols(k, q) * score_scale + mask)
            grad_probs.append(contract_cols(kvb, ga))
        probs = [jnp.exp(score - log_ref[0, head:head + 1, :]) for head, score in zip(group, scores)]
        changes = [
            (prob * (grad - inner[head:head + 1, :]) * score_scale).astype(bf16)
            for head, prob, grad in zip(group, probs, grad_probs)
        ]
        grad_values = [project(prob.astype(bf16), ga) for prob, ga in zip(probs, grads)]
        grad_keys = [project(change, q) for change, q in zip(changes, queries)]
        grad_queries = [contract_rows(change, k) for change, k in zip(changes, keys)]
        for head, gv, gk, gq in zip(group, grad_values, grad_keys, grad_queries):
            lanes = slice(head * LANES, (head + 1) * LANES)
            gq = gq * keep - pltpu.roll(gq, LANES - 16, 1) * left - pltpu.roll(gq, 16, 1) * right
            gq_ref[:, lanes] = gq.astype(bf16)
            total = total + gk
            gkv_ref[:, lanes] = jnp.where(low, gk, gv).astype(bf16)
    gsh_ref[...] = total


def attend_back(query, keyval, shared, tables, grad_attended, attended, logs):
    tokens = query.shape[0]
    heads = query.shape[1] // LANES
    wide = pl.BlockSpec((SLOT, heads * LANES), lambda s: (s, 0))
    one = pl.BlockSpec((SLOT, LANES), lambda s: (s, 0))
    half = pl.BlockSpec((SLOT, heads * VDIM), lambda s: (s, 0))
    return pl.pallas_call(
        functools.partial(attend_back_kernel, heads),
        grid=(tokens // SLOT,),
        in_specs=[wide, wide, one, one, one, one, pl.BlockSpec((1, SLOT, SLOT), lambda s: (s, 0, 0)),
                  half, half, pl.BlockSpec((1, HEAD_ROWS, SLOT), lambda s: (s, 0, 0))],
        out_specs=[wide, wide, one],
        out_shape=[
            jax.ShapeDtypeStruct(query.shape, bf16),
            jax.ShapeDtypeStruct(keyval.shape, bf16),
            jax.ShapeDtypeStruct((tokens, LANES), f32),
        ],
        cost_estimate=attention_cost(tokens, heads, 10),
        name="attend_back",
    )(query, keyval, shared, *tables[:3], tables[4], grad_attended, attended, logs)


MESH = pl.DeviceIdType.MESH
VMEM_LIMIT = 60 * 1024 * 1024


def partners():
    me = lax.axis_index("shard")
    core = me % 2
    return me, core, me + 1 - 2 * core, (me + 2) % 4


def greet(devices):
    barrier = pltpu.get_barrier_semaphore()
    for device in devices:
        pl.semaphore_signal(barrier, inc=1, device_id=device, device_id_type=MESH)
    pl.semaphore_wait(barrier, len(devices))


def columns(step, width):
    return pl.ds(pl.multiple_of(step * width, LANES), width)


def rows_at(start, rows):
    return pl.ds(pl.multiple_of(start * rows, 16), rows)


def remote(source, target, sems, step, device):
    return pltpu.make_async_remote_copy(
        src_ref=source, dst_ref=target, send_sem=sems.at[0, step], recv_sem=sems.at[1, step],
        device_id={"shard": device}, device_id_type=MESH,
    )


def exchange_scratch(rows, steps, width):
    part = pltpu.VMEM((steps, rows, width), bf16)
    return [part] * 6 + [
        pltpu.VMEM((steps, rows, width), f32),
        pltpu.VMEM((2 * rows, width), f32),
        pltpu.SemaphoreType.DMA((3, 2, steps)),
    ]


def each(steps, unrolled, do):
    if unrolled:
        for step in range(steps):
            do(step)
    else:
        def again(step, carry):
            do(step)
            return carry
        lax.fori_loop(0, steps, again, 0)


def sum_scatter(rows, steps, unrolled, partial, scratch, use):
    (to_sib, from_sib, to_far, from_far, own_sib, own_from, hold, stage, sems) = scratch
    me, core, sib, far = partners()
    mine = rows_at(core, rows)
    other = rows_at(1 - core, rows)

    def first(step):
        return remote(to_sib.at[step], from_sib.at[step], sems.at[0], step, sib)

    def across(step):
        return remote(to_far.at[step], from_far.at[step], sems.at[1], step, far)

    def beside(step):
        return remote(own_sib.at[step], own_from.at[step], sems.at[2], step, sib)

    def far_part(step):
        stage[...] = partial(rows_at(far // 2, 2 * rows), step)
        to_sib[step] = stage[other, :].astype(bf16)
        first(step).start()
        hold[step] = stage[mine, :]

    def far_send(step):
        first(step).wait_recv()
        to_far[step] = (hold[step] + from_sib[step].astype(f32)).astype(bf16)
        across(step).start()

    def far_step(step):
        far_part(step)
        if unrolled:
            if step > 0:
                far_send(step - 1)
        else:
            @pl.when(step > 0)
            def _():
                far_send(step - 1)

    each(steps, unrolled, far_step)
    far_send(steps - 1)

    def near_part(step):
        stage[...] = partial(rows_at(me // 2, 2 * rows), step)
        own_sib[step] = stage[other, :].astype(bf16)
        beside(step).start()
        hold[step] = stage[mine, :]

    each(steps, unrolled, near_part)

    def finish(step):
        beside(step).wait_recv()
        across(step).wait_recv()
        use(step, hold[step] + own_from[step].astype(f32) + from_far[step].astype(f32))

    each(steps, unrolled, finish)

    def settle(step):
        first(step).wait_send()
        across(step).wait_send()
        beside(step).wait_send()

    each(steps, unrolled, settle)


def spread_rows(rows, steps, width, place, all_ref, sems):
    me, core, sib, far = partners()

    def part(owner, step):
        return all_ref.at[rows_at(owner, rows), columns(step, width)]

    def across(step):
        return remote(part(me, step), part(me, step), sems.at[0], step, far)

    def beside(step):
        return remote(part(me, step), part(me, step), sems.at[1], step, sib)

    def onward(step):
        return remote(part(far, step), part(far, step), sems.at[2], step, sib)

    def send(step):
        place(step)
        across(step).start()
        beside(step).start()

    each(steps, False, send)

    def forward(step):
        across(step).wait_recv()
        onward(step).start()

    each(steps, False, forward)

    def settle(step):
        beside(step).wait_recv()
        onward(step).wait_recv()
        across(step).wait_send()
        beside(step).wait_send()
        onward(step).wait_send()

    each(steps, False, settle)


def vmem(count):
    return [pl.BlockSpec(memory_space=pltpu.VMEM)] * count


def comm_call(kernel, name, number, inputs, out_shape, scratch, flops=0, aliased={}):
    nbytes = sum(v.size * v.dtype.itemsize for v in (*inputs, *out_shape))
    return pl.pallas_call(
        kernel,
        in_specs=vmem(len(inputs) - len(aliased)) + any_space(len(aliased)),
        out_specs=vmem(len(out_shape) - len(aliased)) + any_space(len(aliased)),
        out_shape=out_shape,
        scratch_shapes=scratch,
        input_output_aliases=aliased,
        compiler_params=pltpu.CompilerParams(
            collective_id=number, has_side_effects=True, vmem_limit_bytes=VMEM_LIMIT
        ),
        cost_estimate=pl.CostEstimate(flops=0, bytes_accessed=0 * nbytes, transcendentals=0),
        name=name,
    )(*inputs)


def shape(rows, width, dtype):
    return jax.ShapeDtypeStruct((rows, width), dtype)


def gather_kernel(steps, width, own_ref, all_ref, sems):
    rows = own_ref.shape[0]
    me, core, sib, far = partners()
    greet([{"shard": sib}, {"shard": far}])

    def place(step):
        all_ref[rows_at(me, rows), columns(step, width)] = own_ref[:, columns(step, width)]

    spread_rows(rows, steps, width, place, all_ref, sems)


def gather(value, number, width):
    if lax.axis_size("shard") != 4:
        return lax.all_gather(value, "shard", axis=0, tiled=True)
    rows, total = value.shape
    steps = total // width
    (out,) = comm_call(
        functools.partial(gather_kernel, steps, width), "gather_rows", number, [value],
        [shape(4 * rows, total, bf16)], [pltpu.SemaphoreType.DMA((3, 2, steps))],
    )
    return out


def plain_gather(value):
    return lax.all_gather(value, "shard", axis=0, tiled=True)


def plain_scatter(value):
    return lax.psum_scatter(value.astype(bf16), "shard", scatter_dimension=0, tiled=True).astype(f32)


MODEL_STEP = 512


def output_kernel(relaying, att_ref, weight_ref, hidden_ref, gain_ref, *refs):
    if relaying:
        _, mixed_ref, two_ref, up_ref, *scratch, passed = refs
    else:
        mixed_ref, two_ref, *scratch = refs
    *parts, sems = scratch
    rows = hidden_ref.shape[0]
    width = MODEL_STEP
    steps = D // width
    me, core, sib, far = partners()
    devices = [{"shard": sib}, {"shard": far}]
    if relaying:
        partner, away = replica_pair()
        devices.append({"rep": partner})
    greet(devices)
    if relaying:
        @pl.when(away == 0)
        def _():
            for slot, owner in enumerate((far, far + 1 - 2 * core)):
                pass_on(up_ref, passed, slot, owner).start()

    def partial(where, step):
        return project(att_ref[where, :], weight_ref[:, columns(step, width)])

    def use(step, total):
        lanes = columns(step, width)
        mixed_ref[:, lanes] = hidden_ref[:, lanes] + residual_scale * total

    sum_scatter(rows, steps, False, partial, parts, use)
    mixed = mixed_ref[...]
    scale = norm_scale(mixed)

    def place(step):
        lanes = columns(step, width)
        two_ref[rows_at(me, rows), lanes] = (mixed_ref[:, lanes] * scale * gain_ref[:, lanes]).astype(bf16)

    spread_rows(rows, steps, width, place, two_ref, sems)
    if relaying:
        @pl.when(away == 0)
        def _():
            for slot, owner in enumerate((far, far + 1 - 2 * core)):
                pass_on(up_ref, passed, slot, owner).wait_send()

        @pl.when(away == 1)
        def _():
            for slot, owner in enumerate((far, far + 1 - 2 * core)):
                pass_on(up_ref, passed, slot, owner).wait_recv()


def output_norm(attended, weight, hidden, gain, up=None):
    if lax.axis_size("shard") != 4:
        mixed = hidden + residual_scale * plain_scatter(project(attended, weight))
        return mixed, plain_gather((mixed * norm_scale(mixed) * gain).astype(bf16))
    rows = hidden.shape[0]
    steps = D // MODEL_STEP
    scratch = exchange_scratch(rows, steps, MODEL_STEP) + [pltpu.SemaphoreType.DMA((3, 2, steps))]
    inputs = [attended, weight, hidden, gain[None]]
    outputs = [shape(rows, D, f32), shape(4 * rows, D, bf16)]
    flops = 2 * attended.size * D
    if up is None:
        return comm_call(functools.partial(output_kernel, False), "output_norm", 2, inputs, outputs, scratch, flops)
    return comm_call(
        functools.partial(output_kernel, True), "output_norm", 9, inputs + [up],
        outputs + [jax.ShapeDtypeStruct(up.shape, bf16)], scratch + [pltpu.SemaphoreType.DMA((2, 2))], flops,
        aliased={4: 2},
    )


def down_kernel(passing, act_ref, given_ref, mixed_ref, out_ref, low_ref, *scratch):
    rows = mixed_ref.shape[0]
    width = MODEL_STEP
    steps = D // width
    me, core, sib, far = partners()
    devices = [{"shard": sib}, {"shard": far}]
    weight_ref = given_ref
    if passing:
        got_ref, weight_ref, *parts, sems = scratch
        size, more = given_ref.shape[0], weight_ref.shape[0] - given_ref.shape[0]
        weight_ref[pl.ds(pl.multiple_of((1 - core) * size, 16), more), :] = jnp.zeros((more, D), bf16)
        piece = 64

        def fill(step):
            source = pl.ds(pl.multiple_of(step * piece, 16), piece)
            target = pl.ds(pl.multiple_of(step * piece + core * more, 16), piece)
            weight_ref[target, :] = given_ref[source, :]

        each(size // piece, False, fill)
        section = lax.axis_index("section")
        devices.append({"section": 1 - section})
    else:
        parts = scratch
    greet(devices)

    def onward(step):
        lanes = columns(step, width)
        return pltpu.make_async_remote_copy(
            src_ref=low_ref.at[:, lanes], dst_ref=got_ref.at[:, lanes], send_sem=sems.at[0, step],
            recv_sem=sems.at[1, step], device_id={"section": 1 - section}, device_id_type=MESH,
        )

    def partial(where, step):
        return project(act_ref[where, :], weight_ref[:, columns(step, width)])

    def use(step, total):
        lanes = columns(step, width)
        out = mixed_ref[:, lanes] + residual_scale * total
        out_ref[:, lanes] = out
        low_ref[:, lanes] = out.astype(bf16)
        if passing:
            onward(step).start()

    sum_scatter(rows, steps, False, partial, parts, use)
    if passing:
        each(steps, False, lambda step: onward(step).wait())


def down_project(activated, weight, mixed, passing):
    count = lax.axis_size("shard")
    if count != 4:
        if passing:
            weight = window_rows(weight, count)
        output = mixed + residual_scale * plain_scatter(project(activated, weight))
        low = output.astype(bf16)
        return (output, low) + ((lax.ppermute(low, "section", [(0, 1)]), weight) if passing else ())
    rows = mixed.shape[0]
    steps = D // MODEL_STEP
    scratch = exchange_scratch(rows, steps, MODEL_STEP)
    return comm_call(
        functools.partial(down_kernel, passing), "down_project", 3 if passing else 4,
        [activated, weight, mixed],
        [shape(rows, D, f32)] + [shape(rows, D, bf16)] * (2 if passing else 1)
        + [shape(HIDDEN_WINDOW, D, bf16)] * passing,
        scratch + ([pltpu.SemaphoreType.DMA((2, steps))] if passing else []),
        flops=2 * activated.size * D,
    )


def mlp_back_kernel(gate_ref, up_ref, gate_weight_ref, up_weight_ref, mixed_ref, grad_ref, gain_ref, out_ref, dgain_ref, branch_ref,
                    *scratch):
    *parts, sems = scratch
    rows = mixed_ref.shape[0]
    width = MODEL_STEP
    steps = D // width
    me, core, sib, far = partners()
    greet([{"shard": sib}, {"shard": far}])

    def partial(where, step):
        rows_of = columns(step, width)
        return contract_cols(gate_ref[where, :], gate_weight_ref[rows_of, :]) + contract_cols(
            up_ref[where, :], up_weight_ref[rows_of, :]
        )

    def use(step, total):
        out_ref[:, columns(step, width)] = total

    sum_scatter(rows, steps, False, partial, parts, use)
    mixed = mixed_ref[...]
    scale = norm_scale(mixed)
    inner = jnp.mean(mixed * out_ref[...] * gain_ref[...], axis=-1, keepdims=True)
    slope = scale * scale * scale * inner

    def place(step):
        lanes = columns(step, width)
        grad, value = out_ref[:, lanes], mixed_ref[:, lanes]
        dgain_ref[:, lanes] = jnp.sum(grad * value * scale, axis=0, keepdims=True)
        total = grad_ref[:, lanes] + scale * (grad * gain_ref[:, lanes]) - value * slope
        out_ref[:, lanes] = total
        branch_ref[rows_at(me, rows), lanes] = (residual_scale * total).astype(bf16)

    spread_rows(rows, steps, width, place, branch_ref, sems)


def mlp_back(grad_gate, grad_up, gate_weight, up_weight, mixed, grad_out, gain):
    if lax.axis_size("shard") != 4:
        grad = plain_scatter(contract_cols(grad_gate, gate_weight) + contract_cols(grad_up, up_weight))
        back, dgain = norm_back(mixed, norm_scale(mixed), gain, grad)
        grad_mixed = grad_out + back
        return grad_mixed, dgain[None], plain_gather((residual_scale * grad_mixed).astype(bf16))
    rows = mixed.shape[0]
    steps = D // MODEL_STEP
    return comm_call(
        mlp_back_kernel, "mlp_back", 5,
        [grad_gate, grad_up, gate_weight, up_weight, mixed, grad_out, gain[None]],
        [shape(rows, D, f32), shape(1, D, f32), shape(4 * rows, D, bf16)],
        exchange_scratch(rows, steps, MODEL_STEP) + [pltpu.SemaphoreType.DMA((3, 2, steps))],
        flops=4 * grad_gate.size * D,
    )


LATENT_STEP = 256


def latent_back_kernel(gq_ref, gkv_ref, gsh_ref, qup_ref, lup_ref, out_ref, *scratch):
    rows = out_ref.shape[0]
    width = LATENT_STEP
    me, core, sib, far = partners()
    greet([{"shard": sib}, {"shard": far}])

    def partial(where, step):
        if step < QRANK // width:
            return contract_cols(gq_ref[where, :], qup_ref[step * width:(step + 1) * width, :])
        if step == QRANK // width:
            return contract_cols(gkv_ref[where, :], lup_ref[...])
        shared = gsh_ref[where, :]
        return jnp.concatenate([shared, jnp.zeros_like(shared)], axis=1)

    def use(step, total):
        out_ref[:, step * width:(step + 1) * width] = total

    sum_scatter(rows, out_ref.shape[1] // width, True, partial, scratch, use)


def latent_back(grad_query, grad_keyval, grad_shared, query_up, latent_up):
    if lax.axis_size("shard") != 4:
        return plain_scatter(
            jnp.concatenate(
                [contract_cols(grad_query, query_up), contract_cols(grad_keyval, latent_up), grad_shared],
                axis=1,
            )
        )
    rows = grad_query.shape[0] // 4
    steps = QRANK // LATENT_STEP + 2
    (out,) = comm_call(
        latent_back_kernel, "latent_back", 6, [grad_query, grad_keyval, grad_shared, query_up, latent_up],
        [shape(rows, steps * LATENT_STEP, f32)], exchange_scratch(rows, steps, LATENT_STEP),
        flops=2 * grad_query.size * QRANK + 2 * grad_keyval.size * KVRANK,
    )
    return out


def any_space(count):
    return [pl.BlockSpec(memory_space=pl.ANY)] * count


def pair(value, index):
    return value.at[0, index], value.at[1, index]


def send_to(source, target, sems, index, device):
    send, receive = pair(sems, index)
    return pltpu.make_async_remote_copy(
        src_ref=source, dst_ref=target, send_sem=send, recv_sem=receive,
        device_id={"shard": device}, device_id_type=MESH,
    )


def replica_pair():
    replica = lax.axis_index("rep")
    return replica + 1 - 2 * (replica % 2), (lax.axis_index("shard") + replica) % 2


def pass_on(target, sems, step, owner):
    partner, _ = replica_pair()
    return pltpu.make_async_remote_copy(
        src_ref=target.at[owner], dst_ref=target.at[owner], send_sem=sems.at[0, step], recv_sem=sems.at[1, step],
        device_id={"rep": partner}, device_id_type=MESH,
    )


def move_kernel(whole, alike, split, relayed, *refs):
    amount = whole + len(split) + len(relayed)
    inputs, outputs, held = refs[:amount], refs[amount:2 * amount], refs[2 * amount:3 * amount]
    sems, local, *relays = refs[3 * amount:]
    me, core, sib, far = partners()
    diagonal = far + 1 - 2 * core
    devices = [{"shard": sib}, {"shard": far}, {"shard": diagonal}]
    if relayed:
        partner, away = replica_pair()
        devices.append({"rep": partner})
    greet(devices)
    waits, forwards, keeps, bulk = [], [], [], []
    number = 0
    for i, (source, target) in enumerate(zip(inputs, outputs)):
        if i < whole:
            to_far = send_to(source, target.at[me], sems, number, far)
            to_sib = send_to(source, target.at[me], sems, number + 1, sib)
            onward = send_to(target.at[far], target.at[far], sems, number + 2, sib)
            if i < alike:
                @pl.when(away == 0)
                def _():
                    to_far.start()
            else:
                to_far.start()
            to_sib.start()
            forwards.append((target, to_far, onward))
            waits.append(to_sib)
            kept = source
        elif i < whole + len(split):
            part = split[i - whole]
            for j, device in enumerate((far, diagonal, sib)):
                copy = send_to(part(source, device), target.at[me], sems, number + j, device)
                copy.start()
                waits.append(copy)
            kept = part(source, me)
        else:
            begin, arrive, passed = relays
            place = i - whole - len(split)
            part = relayed[place][0]
            taker = far // 2 * 2 + lax.axis_index("rep") % 2

            def across(owner, slot, source=source, target=target, part=part, place=place):
                return pltpu.make_async_remote_copy(
                    src_ref=part(source, taker), dst_ref=target.at[owner], send_sem=begin.at[place],
                    recv_sem=arrive.at[place, slot], device_id={"shard": taker}, device_id_type=MESH,
                )

            across(me, away).start()
            beside = send_to(part(source, sib), target.at[me], sems, number, sib)
            beside.start()
            waits.append(beside)
            bulk.append((place, target, across))
            kept = part(source, me)
        number += 3
        keep = pltpu.make_async_copy(kept, held[i], local.at[0, i])
        keep.start()
        keeps.append((keep, pltpu.make_async_copy(held[i], target.at[me], local.at[1, i])))
    for keep, store in keeps:
        keep.wait()
        store.start()
    for step, (target, to_far, onward) in enumerate(forwards):
        if step < alike:
            hop = pass_on(target, relays[2], 2 * len(relayed) + step, far)

            @pl.when(away == 0)
            def _():
                to_far.wait_recv()
                hop.start()

            @pl.when(away == 1)
            def _():
                hop.wait_recv()
        else:
            to_far.wait_recv()
        onward.start()
    for step, (target, to_far, onward) in enumerate(forwards):
        if step < alike:
            hop = pass_on(target, relays[2], 2 * len(relayed) + step, far)

            @pl.when(away == 0)
            def _():
                to_far.wait_send()
                hop.wait_send()
        else:
            to_far.wait_send()
        onward.wait()
    for copy in waits:
        copy.wait()
    for keep, store in keeps:
        store.wait()
    for place, target, across in bulk:
        passing = relayed[place][1]
        passed = relays[2]

        @pl.when(away == 0)
        def _():
            for slot, owner in enumerate((far, diagonal)):
                across(owner, slot).wait_recv()
                if passing:
                    pass_on(target, passed, 2 * place + slot, owner).start()

    for place, target, across in bulk:
        passing = relayed[place][1]
        passed = relays[2]
        across(me, away).wait_send()
        if passing:
            @pl.when(away == 0)
            def _():
                for slot, owner in enumerate((far, diagonal)):
                    pass_on(target, passed, 2 * place + slot, owner).wait_send()

            @pl.when(away == 1)
            def _():
                for slot, owner in enumerate((far, diagonal)):
                    pass_on(target, passed, 2 * place + slot, owner).wait_recv()


def move(name, number, wholes, splits, relayed=(), alike=0):
    inputs = list(wholes) + [entry[0] for entry in (*splits, *relayed)]
    shapes = [w.shape for w in wholes] + [entry[1] for entry in (*splits, *relayed)]
    out_shape = [jax.ShapeDtypeStruct((4,) + tuple(sh), v.dtype) for sh, v in zip(shapes, inputs)]
    scratch = [pltpu.VMEM(sh, v.dtype) for sh, v in zip(shapes, inputs)]
    scratch += [pltpu.SemaphoreType.DMA((2, 3 * len(inputs))), pltpu.SemaphoreType.DMA((2, len(inputs)))]
    if relayed:
        amount = len(relayed)
        scratch += [
            pltpu.SemaphoreType.DMA((amount,)), pltpu.SemaphoreType.DMA((amount, 2)),
            pltpu.SemaphoreType.DMA((2, 2 * amount + len(wholes))),
        ]
    return pl.pallas_call(
        functools.partial(move_kernel, len(wholes), alike, [f for _, _, f in splits], [entry[2:] for entry in relayed]),
        in_specs=any_space(len(inputs)),
        out_specs=any_space(len(inputs)),
        out_shape=out_shape,
        scratch_shapes=scratch,
        compiler_params=pltpu.CompilerParams(
            collective_id=number, has_side_effects=True, vmem_limit_bytes=VMEM_LIMIT
        ),
        cost_estimate=pl.CostEstimate(
            flops=0, bytes_accessed=sum(4 * v.size * v.dtype.itemsize for v in inputs), transcendentals=0
        ),
        name=name,
    )(*inputs)


HIDDEN_WINDOW = 1664


def hidden_columns(ref, owner):
    return ref.at[:, pl.ds(pl.multiple_of(owner // 2 * 3200 + owner % 2 * 1536, LANES), HIDDEN_WINDOW)]


QUERY_WINDOW = 1024


def query_window(ref, owner):
    return ref.at[:, pl.ds(pl.multiple_of(owner // 2 * 1920 + owner % 2 * 896, LANES), QUERY_WINDOW)]


def latent_window(ref, owner):
    return ref.at[:, pl.ds(pl.multiple_of(owner * 1280, LANES), 1280)]


def first_move(query_down, latent_down, query_up, latent_up, segments, gate, up, count):
    if count != 4:
        gate, up = spread_hidden(gate, up, count)
        return (
            plain_gather(query_down), plain_gather(latent_down), pad_heads(spread(query_up, count)),
            spread(latent_up, count), plain_gather(segments), gate, up,
        )
    part = (gate.shape[0], HIDDEN_WINDOW)
    heads = [(query_up, (query_up.shape[0], QUERY_WINDOW), query_window),
             (latent_up, (latent_up.shape[0], 1280), latent_window)]
    relayed = []
    if shared_links(count):
        relayed = [entry + (True,) for entry in heads]
        relayed += [(gate, part, hidden_columns, True), (up, part, hidden_columns, False)]
        heads = []
    down_q, down_kv, groups, up_q, up_kv, *hidden = move(
        "first_move", 7, [query_down, latent_down, segments], heads, relayed, 2 if relayed else 0
    )
    merge = lambda value: value.reshape((-1,) + value.shape[2:])
    up_q = lax.dynamic_slice_in_dim(merge(up_q), lax.axis_index("shard") % 2 * 64, 960, 1)
    gate, up = hidden if relayed else spread_hidden(gate, up, count)
    return merge(down_q), merge(down_kv), pad_heads(up_q), merge(up_kv), merge(groups), gate, up


EXCHANGE_WIDTH = 1280


def last_move(grad_lat, gain_terms, query_part, latent_part, count):
    if count != 4:
        parts = (
            plain_gather(grad_lat), plain_gather(gain_terms), collect(cut_heads(query_part), count),
            collect(latent_part, count),
        )
        return parts, lambda parts: parts
    side = lambda value: value.transpose(1, 0, 2).reshape(value.shape[1], -1)
    same = lambda value: jnp.broadcast_to(value[None], (count,) + value.shape)
    wide = lambda value: jnp.pad(value, ((0, 0), (0, EXCHANGE_WIDTH - value.shape[1])))
    amount = gain_terms.shape[1]
    gain_rows = -(-amount // EXCHANGE_WIDTH)
    gain_rows += -gain_rows % 16
    gains = jnp.pad(gain_terms[0].astype(bf16), (0, gain_rows * EXCHANGE_WIDTH - amount)).reshape(gain_rows, -1)
    pieces = [
        query_part.reshape(count, -1, EXCHANGE_WIDTH), latent_part.reshape(count, -1, EXCHANGE_WIDTH),
        same(wide(grad_lat)), same(gains),
    ]
    got = lax.all_to_all(jnp.concatenate(pieces, axis=1), "shard", 0, 0, tiled=True)
    ends = [0]
    for piece in pieces:
        ends.append(ends[-1] + piece.shape[1])
    def finish(got):
        got_q, got_kv, lat, gains = (got[:, start:end] for start, end in zip(ends, ends[1:]))
        return (
            lat.reshape(-1, EXCHANGE_WIDTH)[:, :grad_lat.shape[1]],
            gains.reshape(count, -1)[:, :amount].astype(f32), cut_heads(side(got_q)), side(got_kv),
        )

    return got, finish


def place_kernel(*refs):
    me, core, sib, far = partners()
    *parts, out_ref = refs
    out_ref[...] = jnp.zeros_like(out_ref)
    for owner, part in zip((me, sib, far, far + 1 - 2 * core), parts):
        lanes = pl.ds(pl.multiple_of(owner // 2 * 3200 + owner % 2 * 1536, LANES), HIDDEN_WINDOW)
        out_ref[:, lanes] += part[...].astype(f32)


def head_lanes(value):
    return jnp.pad(value, ((0, 0), (NOPE, LANES - NOPE - ROPE)))


def layer_forward(hidden, own_tables, tables, gains, weights, passing, lacking, early):
    input_gain, query_gain, latent_gain, post_gain = gains
    down_both, query_up, latent_up, output_weight, gate_weight, up_weight, down_weight = weights
    scale_in = norm_scale(hidden)
    normed = (hidden * scale_in * input_gain).astype(bf16)
    down_q, down_kv = down_both
    latent_q = project(normed, down_q)
    latent_kv = project(normed, down_kv)
    latent = latent_kv[:, :KVRANK]
    scale_q = norm_scale(latent_q)
    scale_kv = norm_scale(latent)
    own_in = jnp.concatenate(
        [
            latent_q * scale_q * query_gain,
            latent * scale_kv * latent_gain,
            head_lanes(rotate(latent_kv[:, KVRANK:], *own_tables)),
        ],
        axis=1,
    ).astype(bf16)
    all_in = gather(own_in, 0, 384)
    all_in, early = together(all_in, early)
    if lacking is not None:
        early = plain_gather(early)
    query_in = all_in[:, :QRANK]
    kv_in = all_in[:, QRANK:QRANK + KVRANK]
    shared = all_in[:, QRANK + KVRANK:]
    attended, queries, keyval, logs = attend(
        project(query_in, query_up), project(kv_in, latent_up), shared, tables
    )
    if lacking:
        mixed, normed_two, up_weight = output_norm(attended, output_weight, hidden, post_gain, up_weight)
    else:
        mixed, normed_two = output_norm(attended, output_weight, hidden, post_gain)
    normed_two, early = together(normed_two, early)
    merge = lambda value: value.reshape(D, -1)
    gate = project(normed_two, merge(gate_weight)).astype(bf16)
    up = project(normed_two, merge(up_weight)).astype(bf16)
    activated = (jax.nn.silu(gate.astype(f32)) * up.astype(f32)).astype(bf16)
    def outputs(value):
        return down_project(value, down_weight, mixed, passing)

    kept = (hidden, scale_in, normed, latent_q, scale_q, latent, scale_kv, query_in, kv_in,
            shared, queries, keyval, logs, attended, mixed, normed_two, gate, up)
    return (outputs, activated, kept, merge(gate_weight), merge(up_weight), early)


def gate_backward(grad_act, gate, up):
    sigmoid = jax.nn.sigmoid(gate)
    grad_gate = (grad_act * up * sigmoid * (1.0 + gate * (1.0 - sigmoid))).astype(bf16)
    grad_up = (grad_act * gate * sigmoid).astype(bf16)
    return grad_gate, grad_up


def mlp_backward(grad_out, kept, gains, weights, gather_down, wanted):
    mixed, gate, up = kept[14], kept[16], kept[17]
    gate_weight, up_weight, down_weight = weights[4:]
    own_down = (residual_scale * grad_out).astype(bf16)
    grad_down, wanted = together(gather_down(own_down), wanted)
    grad_gate, grad_up = gate_backward(contract_cols(grad_down, down_weight), gate.astype(f32), up.astype(f32))
    grad_mixed, dgain_post, grad_branch = mlp_back(
        grad_gate, grad_up, gate_weight, up_weight, mixed, grad_out, gains[3]
    )
    return (grad_gate, grad_up), wanted, grad_down, grad_mixed, dgain_post[0], grad_branch


def attention_backward(grad_mixed, grad_branch, kept, own_tables, tables, gains, weights, wanted):
    (hidden, scale_in, normed, latent_q, scale_q, latent, scale_kv, query_in, kv_in,
     shared, queries, keyval, logs, attended, mixed, normed_two, gate, up) = kept
    input_gain, query_gain, latent_gain, post_gain = gains
    down_both, query_up, latent_up, output_weight = weights[:4]
    cosine, sine = own_tables
    grad_attended = contract_cols(grad_branch, output_weight).astype(bf16)
    grad_query, grad_keyval, grad_shared = attend_back(
        queries, keyval, shared, tables, grad_attended, attended, logs
    )
    grad_in = latent_back(grad_query, grad_keyval, grad_shared, query_up, latent_up)
    grad_in, wanted = together(grad_in, wanted)
    grad_latent_q, dgain_query = norm_back(latent_q, scale_q, query_gain, grad_in[:, :QRANK])
    grad_latent, dgain_latent = norm_back(
        latent, scale_kv, latent_gain, grad_in[:, QRANK:QRANK + KVRANK]
    )
    start = QRANK + KVRANK + NOPE
    grad_shared = rotate(grad_in[:, start:start + ROPE], cosine, -sine)
    grad_lat = jnp.concatenate(
        [grad_latent_q, grad_latent, jnp.pad(grad_shared, ((0, 0), (0, LANES - ROPE)))], axis=1
    ).astype(bf16)
    down_q, down_kv = down_both
    grad_normed = contract_cols(grad_lat[:, :QRANK], down_q) + contract_cols(
        grad_lat[:, QRANK:QRANK + KVRANK + ROPE], down_kv
    )
    grad_hidden_norm, dgain_input = norm_back(hidden, scale_in, input_gain, grad_normed)
    grad_hidden = grad_mixed + grad_hidden_norm
    found = (grad_branch, grad_query, grad_keyval, grad_lat)
    return (grad_hidden, found, (dgain_input, dgain_query, dgain_latent), wanted)


def spread(weight, count):
    rows, columns = weight.shape
    parts = weight.reshape(rows, count, columns // count).transpose(1, 0, 2)
    return lax.all_to_all(parts, "shard", 0, 0, tiled=True).reshape(rows * count, columns // count)


def collect(grad, count):
    rows, columns = grad.shape
    parts = lax.all_to_all(
        grad.reshape(count, rows // count, columns), "shard", 0, 0, tiled=True
    )
    return parts.transpose(1, 0, 2).reshape(rows // count, columns * count)


def pad_heads(weight):
    rows, columns = weight.shape
    heads = weight.reshape(rows, columns // (NOPE + ROPE), NOPE + ROPE)
    return jnp.pad(heads, ((0, 0), (0, 0), (0, LANES - NOPE - ROPE))).reshape(rows, -1)


def cut_heads(grad):
    rows, columns = grad.shape
    heads = grad.reshape(rows, columns // LANES, LANES)[:, :, :NOPE + ROPE]
    return heads.reshape(rows, -1)


def swap(value, step):
    count = lax.axis_size("shard")
    return lax.ppermute(value, "shard", [(source, source ^ step) for source in range(count)])


def hidden_window(count):
    size = FF // count
    width = -(-size // LANES) * LANES
    starts = [owner * size // LANES * LANES for owner in range(count)]
    starts = [min(start, FF - width) for start in starts]
    return size, width, starts, [owner * size - start for owner, start in enumerate(starts)]


def take_at(table, place):
    return jnp.asarray(table, jnp.int32)[place]


def shared_links(count):
    return count == 4 and lax.axis_size("rep") % 2 == 0


def spread_hidden(gate, up, count):
    me = lax.axis_index("shard")
    size, width, starts, offsets = hidden_window(count)
    rows = gate.shape[0]
    results = []
    for weight in (gate, up):
        whole = jnp.zeros((rows * count, width), bf16)
        for step in range(count):
            owner = me ^ step
            part = lax.dynamic_slice(weight, (0, take_at(starts, owner)), (rows, width))
            if step:
                part = swap(part, step)
            whole = lax.dynamic_update_slice(whole, part, (owner * rows, 0))
        results.append(whole)
    return results


def window_rows(down, count):
    size, width, starts, offsets = hidden_window(count)
    whole = jnp.zeros((width, down.shape[1]), bf16)
    return lax.dynamic_update_slice(whole, down, (take_at(offsets, lax.axis_index("shard")), 0))


def chip_gradients_kernel(order_ref, two_ref, gate_ref, up_ref, gate_out, up_out, turned):
    tokens, rows = two_ref.shape
    piece = 512
    for start in range(0, tokens, piece):
        size = min(piece, tokens - start)
        turned[:, start:start + size] = two_ref[start:start + size, :].T
    width = gate_ref.shape[1]
    whole = width // piece
    for grad, out in ((gate_ref, gate_out), (up_ref, up_out)):
        def tile(step):
            lanes = columns(step, piece)
            out[0, :, lanes] = project(turned[...], grad[:, lanes]).astype(bf16)

        each(whole, False, tile)
        if whole * piece < width:
            out[0, :, whole * piece:] = project(turned[...], grad[:, whole * piece:]).astype(bf16)


def chip_gradients(two_all, grad_gate, grad_up):
    me, core, sib, far = partners()
    tokens, width = grad_gate.shape
    rows = D // 4
    held = pl.BlockSpec((tokens, width), lambda i, order: (0, 0), pipeline_mode=pl.Buffered(1))
    part = pl.BlockSpec((1, rows, width), lambda i, order: (i, 0, 0))
    gate, up = pl.pallas_call(
        chip_gradients_kernel,
        grid_spec=pltpu.PrefetchScalarGridSpec(
            num_scalar_prefetch=1,
            grid=(2,),
            in_specs=[pl.BlockSpec((tokens, rows), lambda i, order: (0, order[i])), held, held],
            out_specs=[part, part],
            scratch_shapes=[pltpu.VMEM((rows, tokens), bf16)],
        ),
        out_shape=[jax.ShapeDtypeStruct((2, rows, width), bf16)] * 2,
        compiler_params=pltpu.CompilerParams(vmem_limit_bytes=VMEM_LIMIT),
        name="chip_gradients",
    )(jnp.stack([sib, me]).astype(jnp.int32), two_all, grad_gate, grad_up)
    return [gate[0], up[0], gate[1], up[1]]


def recompute_kernel(from_ref, own_ref, here_ref, two_ref, near_ref, beside_ref, gate_ref, up_ref, rows_ref,
                     act_own, gate_own, up_own, act_out, gate_out, up_out, down_ref):
    place = pl.program_id(0)
    width = gate_ref.shape[1]
    piece = 512

    @pl.when(own_ref[place] == 1)
    def _():
        act_out[...] = act_own[...]
        gate_out[...] = gate_own[...]
        up_out[...] = up_own[...]

    @pl.when((own_ref[place] == 0) & (here_ref[place] == 1))
    def _():
        down_ref[...] = near_ref[...]

    @pl.when((own_ref[place] == 0) & (here_ref[place] == 0))
    def _():
        down_ref[...] = beside_ref[...]

    @pl.when(own_ref[place] == 0)
    def _():
        def tile(lanes, some_rows):
            gate = project(two_ref[...], gate_ref[:, lanes])
            up = project(two_ref[...], up_ref[:, lanes])
            grad = contract_cols(down_ref[...], rows_ref[some_rows, :])
            sigmoid = jax.nn.sigmoid(gate)
            silu = gate * sigmoid
            act_out[:, lanes] = (silu * up).astype(bf16)
            gate_out[:, lanes] = (grad * up * sigmoid * (1.0 + gate * (1.0 - sigmoid))).astype(bf16)
            up_out[:, lanes] = (grad * silu).astype(bf16)

        each(width // piece, False, lambda step: tile(columns(step, piece), columns(step, piece)))
        if width % piece:
            rest = slice(width // piece * piece, width)
            tile(rest, rest)


def recompute(two_all, down_halves, gate_columns, up_columns, down_rows, own):
    reps = lax.axis_size("rep")
    tokens, width = two_all.shape[0], gate_columns.shape[1]
    tile = own[0].shape[0] // 2
    places = jnp.arange(tokens // tile, dtype=jnp.int32)
    half = places // reps
    is_own = places % reps == lax.axis_index("rep")
    is_here = half == lax.axis_index("shard") % 2
    whole = lambda value: pl.BlockSpec(value.shape, lambda i, a, b, c: (0, 0), pipeline_mode=pl.Buffered(1))
    wide = pl.BlockSpec((tile, D), lambda i, a, b, c: (i, 0))
    again = pl.BlockSpec((tile, D), lambda i, a, b, c: (i % reps, 0))
    mine = pl.BlockSpec((tile, width), lambda i, a, b, c: (a[i], 0), pipeline_mode=pl.Buffered(1))
    part = pl.BlockSpec((tile, width), lambda i, a, b, c: (i, 0))
    return pl.pallas_call(
        recompute_kernel,
        grid_spec=pltpu.PrefetchScalarGridSpec(
            num_scalar_prefetch=3,
            grid=(tokens // tile,),
            in_specs=[wide, again, again, whole(gate_columns), whole(up_columns), whole(down_rows), mine, mine, mine],
            out_specs=[part] * 3,
            scratch_shapes=[pltpu.VMEM((tile, D), bf16)],
        ),
        out_shape=[jax.ShapeDtypeStruct((tokens, width), bf16)] * 3,
        compiler_params=pltpu.CompilerParams(vmem_limit_bytes=VMEM_LIMIT),
        name="recompute",
    )(half, is_own.astype(jnp.int32), is_here.astype(jnp.int32), two_all, *down_halves,
      gate_columns, up_columns, down_rows, *own)


def down_gradient_kernel(act_ref, near_ref, beside_ref, out_ref, turned):
    tokens, width = act_ref.shape
    size = out_ref.shape[0]
    piece = 512

    @pl.when(pl.program_id(0) == 0)
    def _():
        for start in range(0, tokens, piece):
            turned[:, start:start + piece] = act_ref[start:start + piece, :].T

    core = lax.axis_index("shard") % 2
    offset = core * (width - size)
    half = size // 2
    some = tokens // 2
    near = pl.ds(pl.multiple_of(core * some, LANES), some)
    beside = pl.ds(pl.multiple_of((1 - core) * some, LANES), some)

    def tile(step):
        rows = pl.ds(pl.multiple_of(step * half, 16), half)
        source = pl.ds(pl.multiple_of(step * half + offset, 16), half)
        out_ref[rows, :] = project(turned[source, near], near_ref[...]) + project(turned[source, beside], beside_ref[...])

    each(2, False, tile)


def down_gradient(activated_all, down_halves):
    tokens, width = activated_all.shape
    size, piece = FF // 4, 512
    return pl.pallas_call(
        down_gradient_kernel,
        grid=(D // piece,),
        in_specs=[pl.BlockSpec((tokens, width), lambda i: (0, 0), pipeline_mode=pl.Buffered(1)),
                  pl.BlockSpec((tokens // 2, piece), lambda i: (0, i)), pl.BlockSpec((tokens // 2, piece), lambda i: (0, i))],
        out_specs=pl.BlockSpec((size, piece), lambda i: (0, i)),
        out_shape=jax.ShapeDtypeStruct((size, D), f32),
        scratch_shapes=[pltpu.VMEM((width, tokens), bf16)],
        compiler_params=pltpu.CompilerParams(vmem_limit_bytes=VMEM_LIMIT),
        name="down_gradient",
    )(activated_all, *down_halves)


def half_everywhere(group, count):
    if count != 4:
        return group
    rows = group.shape[0] // 2
    half = lax.dynamic_slice_in_dim(group, lax.axis_index("shard") % 2 * rows, rows, 0)
    return lax.all_gather(half, "rep", axis=0, tiled=True)


def everyone(half, count):
    if count != 4:
        return lax.all_gather(half, "rep", axis=0, tiled=True)
    return lax.all_gather(half, "shard", axis=0, tiled=True, axis_index_groups=[[0, 1], [2, 3]])


def owner_gradient(two_all, grad, owner, count):
    rows = D // count
    left = lax.dynamic_slice(two_all, (0, owner * rows), (two_all.shape[0], rows))
    return contract_rows(left, grad).astype(bf16)


def place_windows(parts, count):
    size, width, starts, offsets = hidden_window(count)
    rows = parts[0].shape[0]
    if count == 4:
        tile = 64
        return pl.pallas_call(
            place_kernel,
            grid=(rows // tile,),
            in_specs=[pl.BlockSpec((tile, width), lambda i: (i, 0))] * 4,
            out_specs=pl.BlockSpec((tile, FF), lambda i: (i, 0)),
            out_shape=jax.ShapeDtypeStruct((rows, FF), f32),
            compiler_params=pltpu.CompilerParams(vmem_limit_bytes=VMEM_LIMIT),
            cost_estimate=pl.CostEstimate(flops=0, bytes_accessed=rows * FF * 8, transcendentals=0),
            name="place_windows",
        )(*parts)
    me = lax.axis_index("shard")
    gathered = jnp.zeros((count, rows, width), bf16)
    for step, part in enumerate(parts):
        gathered = lax.dynamic_update_slice(gathered, part[None], (me ^ step, 0, 0))
    pieces = [gathered[owner, :, offset:offset + size] for owner, offset in enumerate(offsets)]
    return jnp.concatenate(pieces, axis=1).astype(f32)


def together(*values):
    return lax.optimization_barrier(values)


def body(tokens, segment_ids, input_gain, query_gain, latent_gain, post_gain, query_down, query_up,
         latent_down, latent_up, output_weight, gate_weight, up_weight, down_weight, cotangent):
    at_start = lax.axis_index("section") == 0
    count = lax.axis_size("shard")
    size, width, starts, offsets = hidden_window(count)
    gains = (input_gain[0], query_gain[0], latent_gain[0], post_gain[0])
    down_q, down_kv, query_up_all, latent_up_all, groups, gate_columns, up_columns = first_move(
        query_down[0], latent_down[0], query_up[0], latent_up[0], segment_ids, gate_weight[0], up_weight[0], count
    )
    down_both = (down_q, down_kv)
    own_tables = tuple(t.reshape(-1, ROPE // 2) for t in slot_tables(segment_ids))
    tables = head_tables(groups)

    weights = (down_both, query_up_all, latent_up_all, output_weight[0], gate_columns, up_columns, down_weight[0])
    start = tokens.astype(f32)
    last = cotangent.astype(f32)
    last_down = (residual_scale * last).astype(bf16)
    outputs, activated, _, gate_columns, up_columns, all_last = layer_forward(
        start, own_tables, tables, gains, weights, True, shared_links(count), last_down
    )
    leaving, low, received, down_rows = outputs(activated)
    weights = weights[:4] + (gate_columns, up_columns, down_rows)
    entering = jnp.where(at_start, start, received.astype(f32))
    _, kept_activated, kept, _, _, _ = layer_forward(
        entering, own_tables, tables, gains, weights, False, None, all_last
    )

    (hidden, scale_in, normed, latent_q, scale_q, latent, scale_kv, query_in, kv_in,
     shared, queries, keyval, logs, attended, mixed, normed_two, gate, up) = kept
    half_two = half_everywhere(normed_two, count)
    _, _, _, grad_mixed, _, grad_branch = mlp_backward(last, kept, gains, weights, lambda own: all_last, at_start)
    grad, _, _, half_two = attention_backward(
        grad_mixed, grad_branch, kept, own_tables, tables, gains, weights, half_two
    )
    two_all = everyone(half_two, count)
    grad_low, kept_activated = together(grad.astype(bf16), kept_activated)
    returned = lax.ppermute(grad_low, "section", [(1, 0)])
    leaving, boundary = down_project(kept_activated, down_rows, mixed, False)
    incoming = jnp.where(at_start, returned.astype(f32), last)
    incoming, boundary = together(incoming, boundary)

    own_grads, two_all, grad_down, grad_mixed, dgain_post, grad_branch = mlp_backward(
        incoming, kept, gains, weights, lambda own: gather(own, 1, 512), two_all
    )
    half_down = half_everywhere(grad_down, count)
    part_output = contract_rows(attended, grad_branch).astype(bf16)
    grad_branch, part_output = together(grad_branch, part_output)

    grad, found, (dgain_input, dgain_query, dgain_latent), _ = attention_backward(
        grad_mixed, grad_branch, kept, own_tables, tables, gains, weights, at_start
    )
    grad_branch, grad_query, grad_keyval, grad_lat = found
    gain_terms = jnp.concatenate([dgain_input, dgain_query, dgain_latent, dgain_post])[None]
    normed_rows = lax.all_to_all(
        normed.reshape(normed.shape[0], count, -1).transpose(1, 0, 2), "shard", 0, 0, tiled=True
    ).reshape(normed.shape[0] * count, -1)
    part_query = contract_rows(query_in, grad_query).astype(bf16)
    part_latent = contract_rows(kv_in, grad_keyval).astype(bf16)
    gain_terms, half_down = together(gain_terms, half_down)
    exchanged, exchange_end = last_move(grad_lat, gain_terms, part_query, part_latent, count)
    part_output, half_down = together(part_output, half_down)
    down_all = [half_down, swap(half_down, 1)] if count == 4 else everyone(half_down, count)
    total_output = lax.psum(part_output, "rep")
    down_all, two_all, own_grads, normed_rows = together(down_all, two_all, own_grads, normed_rows)
    if count == 4:
        activated_all, grad_gate, grad_up = recompute(
            two_all, down_all, gate_columns, up_columns, down_rows, (kept_activated, *own_grads)
        )
    else:
        gate_all = project(two_all, gate_columns)
        up_all = project(two_all, up_columns)
        activated_all = (jax.nn.silu(gate_all) * up_all).astype(bf16)
        grad_gate, grad_up = gate_backward(contract_cols(down_all, down_rows), gate_all, up_all)
    def attention_shares(exchanged):
        lat_all, gains_all, part_query, part_latent = exchange_end(exchanged)
        part_down = contract_rows(normed_rows, lat_all[:, :QRANK + KVRANK + ROPE]).astype(bf16)
        part_gains = jnp.sum(gains_all, axis=0).astype(bf16)
        side = part_down.shape[1]
        gain_rows = -(-part_gains.shape[0] // side)
        part_gains = jnp.pad(part_gains, (0, gain_rows * side - part_gains.shape[0])).reshape(gain_rows, side)
        part_down = jnp.concatenate([part_down, part_gains], axis=0)
        return part_down, part_latent, part_query

    me = lax.axis_index("shard")
    if count == 4:
        grad_gate, grad_up, total_output = together(grad_gate, grad_up, total_output)
        away = [owner_gradient(two_all, grad_gate, me ^ step, count) for step in (2, 3)]
        brought = [[swap(part, 2 + i) for i, part in enumerate(away)]]
        two_all, _, exchanged, total_output = together(two_all, away, exchanged, total_output)
        shares = attention_shares(exchanged)
        two_all, *shares = together(two_all, *shares)
        total_down_both, total_latent, total_query = lax.psum(tuple(shares), "rep")
        away = [owner_gradient(two_all, grad_up, me ^ step, count) for step in (2, 3)]
        brought.append([swap(part, 2 + i) for i, part in enumerate(away)])
        two_all, _ = together(two_all, away)
        near = chip_gradients(two_all, grad_gate, grad_up)
        activated_all, near[0], brought[0] = together(activated_all, near[0], brought[0])
        total_down = down_gradient(activated_all, down_all)
        hidden_parts = [[near[2 + i], swap(near[i], 1), *brought[i]] for i in range(2)]
        total_down, hidden_parts[0] = together(total_down, hidden_parts[0])
    else:
        parts = [
            [owner_gradient(two_all, grad, me ^ step, count) for grad in (grad_gate, grad_up)] for step in range(count)
        ]
        hidden_parts = [
            [swap(parts[step][i], step) if step else parts[step][i] for step in range(count)] for i in range(2)
        ]
        total_down_both, total_latent, total_query = lax.psum(attention_shares(exchanged), "rep")
        total_down = contract_rows(activated_all, down_all)
        total_down = lax.dynamic_slice_in_dim(total_down, take_at(offsets, me), size, 0)
    total_gate = place_windows(hidden_parts[0], count)
    total_gate, total_down_both, total_latent, total_query = together(
        total_gate, total_down_both, total_latent, total_query
    )
    gain_rows = total_down_both.shape[0] - D // count
    gain_totals = total_down_both[-gain_rows:].reshape(-1).astype(f32)
    total_down_both = total_down_both[:-gain_rows].astype(f32)
    first, second, third = D, D + QRANK, D + QRANK + KVRANK
    hidden_parts[1][0], total_gate, *finished = together(
        hidden_parts[1][0], total_gate, total_down_both[:, :QRANK], total_down_both[:, QRANK:],
        total_query.astype(f32), total_latent.astype(f32), gain_totals[:first], gain_totals[first:second],
        gain_totals[second:third], gain_totals[third:third + D],
    )
    total_down_q, total_down_kv, total_query, total_latent, *gain_totals = finished
    total_up = place_windows(hidden_parts[1], count)
    return (
        boundary[None],
        grad[None],
        gain_totals[0][None],
        gain_totals[1][None],
        gain_totals[2][None],
        gain_totals[3][None],
        total_down_q[None],
        total_query[None],
        total_down_kv[None],
        total_latent[None],
        total_output.astype(f32)[None],
        total_gate[None],
        total_up[None],
        total_down[None],
    )


def solution(mesh):
    tokens = P(("rep", "shard"), None)
    gain = P("section", None)
    weight = P("section", "shard", None)
    out = P("section", ("rep", "shard"), None)
    return jax.shard_map(
        body,
        mesh=mesh,
        in_specs=(tokens, tokens) + (gain,) * 4 + (weight,) * 8 + (tokens,),
        out_specs=(out, out) + (gain,) * 4 + (weight,) * 8,
        check_vma=False,
    )
```

```python
import functools
import math

import jax
import jax.numpy as jnp
from jax import lax
from jax.experimental import pallas as pl
from jax.experimental.pallas import tpu as pltpu
from jax.sharding import PartitionSpec as P

D = 2560
HEADS = 40
NOPE = 64
ROPE = 32
VDIM = 64
QRANK = 768
KVRANK = 256
FF = 6400
SLOT = 96
LANES = 128

epsilon = 1e-05
residual_scale = 1.4 / math.sqrt(62.0)
masked_score = -1e30
score_scale = 1.0 / math.sqrt(NOPE + ROPE)
bf16 = jnp.bfloat16
f32 = jnp.float32


def norm_scale(value):
    return lax.rsqrt(jnp.mean(value * value, axis=-1, keepdims=True) + epsilon)


def norm_back(value, scale, gain, grad):
    weighted = grad * gain
    inner = jnp.mean(value * weighted, axis=-1, keepdims=True)
    grad_value = scale * weighted - value * (scale * scale * scale) * inner
    return (grad_value, jnp.sum(grad * value * scale, axis=0))


def rotate(value, cosine, sine):
    half = value.shape[-1] // 2
    front = value[..., :half]
    back = value[..., half:]
    return jnp.concatenate([front * cosine - back * sine, back * cosine + front * sine], axis=-1)


def slot_tables(segments):
    index = jnp.arange(SLOT, dtype=jnp.int32)
    first_index = jnp.sum((segments[:, None, :] < segments[:, :, None]).astype(jnp.int32), axis=-1)
    position = (index - first_index).astype(f32)
    freq = jnp.exp(jnp.arange(ROPE // 2, dtype=f32) * (-2.0 * math.log(10000.0) / ROPE))
    angle = position[..., None] * freq
    return (jnp.cos(angle), jnp.sin(angle))


def head_tables(segments):
    cosine, sine = slot_tables(segments)
    slots = segments.shape[0]
    ones = jnp.ones((slots, SLOT, NOPE), f32)
    tail = jnp.zeros((slots, SLOT, LANES - NOPE - ROPE), f32)
    half = jnp.zeros_like(sine)
    keep = jnp.concatenate([ones, cosine, cosine, tail], axis=-1)
    left = jnp.concatenate([0.0 * ones, -sine, half, tail], axis=-1)
    right = jnp.concatenate([0.0 * ones, half, sine, tail], axis=-1)
    index = jnp.arange(SLOT, dtype=jnp.int32)
    allowed = (segments[:, :, None] == segments[:, None, :]) & (index[None, :] <= index[:, None])
    mask = jnp.where(allowed, 0.0, masked_score).astype(f32)
    flat = lambda table: table.reshape(slots * SLOT, LANES)
    return (flat(keep), flat(left), flat(right), mask, mask.transpose(0, 2, 1))


def contract_rows(left, right):
    return lax.dot_general(left, right, (((0,), (0,)), ((), ())), preferred_element_type=f32)


def contract_cols(left, right):
    return lax.dot_general(left, right, (((1,), (1,)), ((), ())), preferred_element_type=f32)


def project(left, weight):
    return jnp.dot(left, weight, preferred_element_type=f32)


def low_lanes():
    return lax.broadcasted_iota(jnp.int32, (SLOT, LANES), 1) < NOPE


HEAD_GROUP = 5
HEAD_ROWS = 16


def attend_kernel(heads, q_ref, kv_ref, sh_ref, keep_ref, left_ref, right_ref, mask_ref,
                  att_ref, qo_ref, kvo_ref, log_ref):
    low = low_lanes()
    lane = lax.broadcasted_iota(jnp.int32, (SLOT, LANES), 1)
    shared = sh_ref[...].astype(f32)
    keep, left, right = keep_ref[...], left_ref[...], right_ref[...]
    mask = mask_ref[0]
    tallest = jnp.zeros((SLOT, LANES), f32)
    sums = jnp.ones((SLOT, LANES), f32)
    for first in range(0, heads, HEAD_GROUP):
        group = range(first, min(first + HEAD_GROUP, heads))
        scores, values = [], []
        for head in group:
            lanes = slice(head * LANES, (head + 1) * LANES)
            q = q_ref[:, lanes]
            q = q * keep + pltpu.roll(q, LANES - 16, 1) * left + pltpu.roll(q, 16, 1) * right
            q = q.astype(bf16)
            qo_ref[:, lanes] = q
            kv = kv_ref[:, lanes]
            kvo_ref[:, lanes] = kv.astype(bf16)
            k = jnp.where(low, kv, shared).astype(bf16)
            values.append(jnp.where(low, 1.0, kv).astype(bf16))
            scores.append(contract_cols(q, k) * score_scale + mask)
        tops = [jnp.max(score, axis=-1, keepdims=True) for score in scores]
        terms = [jnp.exp(score - top).astype(bf16) for score, top in zip(scores, tops)]
        outs = [project(term, value) for term, value in zip(terms, values)]
        for head, top, out in zip(group, tops, outs):
            turned = pltpu.roll(out, NOPE, 1)
            tallest = jnp.where(lane == head, top, tallest)
            sums = jnp.where(lane == head, out, sums)
            pair = (head // 2) * LANES
            if head % 2 == 0:
                att = turned / out
                att_ref[:, pair:pair + VDIM] = att[:, :VDIM].astype(bf16)
            else:
                att = out / turned
                att_ref[:, pair + VDIM:pair + LANES] = att[:, VDIM:].astype(bf16)
    log_ref[0] = (tallest + jnp.log(sums)).T[:HEAD_ROWS, :]


def attention_cost(tokens, heads, passes):
    return pl.CostEstimate(
        flops=passes * tokens * heads * SLOT * LANES * 20, bytes_accessed=tokens * heads * LANES * 12,
        transcendentals=tokens * heads * SLOT,
    )


def attend(query, keyval, shared, tables):
    tokens = query.shape[0]
    heads = query.shape[1] // LANES
    wide = pl.BlockSpec((SLOT, heads * LANES), lambda s: (s, 0))
    one = pl.BlockSpec((SLOT, LANES), lambda s: (s, 0))
    square = pl.BlockSpec((1, SLOT, SLOT), lambda s: (s, 0, 0))
    return pl.pallas_call(
        functools.partial(attend_kernel, heads),
        grid=(tokens // SLOT,),
        in_specs=[wide, wide, one, one, one, one, square],
        out_specs=[pl.BlockSpec((SLOT, heads * VDIM), lambda s: (s, 0)), wide, wide,
                   pl.BlockSpec((1, HEAD_ROWS, SLOT), lambda s: (s, 0, 0))],
        out_shape=[
            jax.ShapeDtypeStruct((tokens, heads * VDIM), bf16),
            jax.ShapeDtypeStruct(query.shape, bf16),
            jax.ShapeDtypeStruct(keyval.shape, bf16),
            jax.ShapeDtypeStruct((tokens // SLOT, HEAD_ROWS, SLOT), f32),
        ],
        cost_estimate=attention_cost(tokens, heads, 4),
        name="attend",
    )(query, keyval, shared, *tables[:4])


def attend_back_kernel(heads, q_ref, kv_ref, sh_ref, keep_ref, left_ref, right_ref, mask_ref,
                       ga_ref, att_ref, log_ref, gq_ref, gkv_ref, gsh_ref):
    low = low_lanes()
    shared = sh_ref[...].astype(f32)
    keep, left, right = keep_ref[...], left_ref[...], right_ref[...]
    mask = mask_ref[0]
    total = jnp.zeros((SLOT, LANES), f32)
    product = ga_ref[...].astype(f32) * att_ref[...].astype(f32)
    high = product.astype(bf16)
    rest = (product - high.astype(f32)).astype(bf16)
    shape = (HEAD_ROWS, product.shape[1])
    chosen = lax.broadcasted_iota(jnp.int32, shape, 1) // VDIM == lax.broadcasted_iota(jnp.int32, shape, 0)
    chosen = jnp.where(chosen, 1.0, 0.0).astype(bf16)
    inner = contract_cols(chosen, high) + contract_cols(chosen, rest)
    for first in range(0, heads, HEAD_GROUP):
        group = range(first, min(first + HEAD_GROUP, heads))
        queries, keys, grads, scores, grad_probs = [], [], [], [], []
        for head in group:
            lanes = slice(head * LANES, (head + 1) * LANES)
            q = q_ref[:, lanes]
            kvb = kv_ref[:, lanes]
            k = jnp.where(low, kvb.astype(f32), shared).astype(bf16)
            if head % 2 == 0 and head == heads - 1:
                ga = ga_ref[:, head * VDIM:(head + 1) * VDIM].astype(f32)
                ga = jnp.concatenate([jnp.zeros_like(ga), ga], axis=1)
            else:
                start = (head // 2) * LANES
                ga = ga_ref[:, start:start + LANES].astype(f32)
                if head % 2 == 0:
                    ga = pltpu.roll(ga, NOPE, 1)
                ga = jnp.where(low, 0.0, ga)
            ga = ga.astype(bf16)
            queries.append(q)
            keys.append(k)
            grads.append(ga)
            scores.append(contract_cols(k, q) * score_scale + mask)
            grad_probs.append(contract_cols(kvb, ga))
        probs = [jnp.exp(score - log_ref[0, head:head + 1, :]) for head, score in zip(group, scores)]
        changes = [
            (prob * (grad - inner[head:head + 1, :]) * score_scale).astype(bf16)
            for head, prob, grad in zip(group, probs, grad_probs)
        ]
        grad_values = [project(prob.astype(bf16), ga) for prob, ga in zip(probs, grads)]
        grad_keys = [project(change, q) for change, q in zip(changes, queries)]
        grad_queries = [contract_rows(change, k) for change, k in zip(changes, keys)]
        for head, gv, gk, gq in zip(group, grad_values, grad_keys, grad_queries):
            lanes = slice(head * LANES, (head + 1) * LANES)
            gq = gq * keep - pltpu.roll(gq, LANES - 16, 1) * left - pltpu.roll(gq, 16, 1) * right
            gq_ref[:, lanes] = gq.astype(bf16)
            total = total + gk
            gkv_ref[:, lanes] = jnp.where(low, gk, gv).astype(bf16)
    gsh_ref[...] = total


def attend_back(query, keyval, shared, tables, grad_attended, attended, logs):
    tokens = query.shape[0]
    heads = query.shape[1] // LANES
    wide = pl.BlockSpec((SLOT, heads * LANES), lambda s: (s, 0))
    one = pl.BlockSpec((SLOT, LANES), lambda s: (s, 0))
    half = pl.BlockSpec((SLOT, heads * VDIM), lambda s: (s, 0))
    return pl.pallas_call(
        functools.partial(attend_back_kernel, heads),
        grid=(tokens // SLOT,),
        in_specs=[wide, wide, one, one, one, one, pl.BlockSpec((1, SLOT, SLOT), lambda s: (s, 0, 0)),
                  half, half, pl.BlockSpec((1, HEAD_ROWS, SLOT), lambda s: (s, 0, 0))],
        out_specs=[wide, wide, one],
        out_shape=[
            jax.ShapeDtypeStruct(query.shape, bf16),
            jax.ShapeDtypeStruct(keyval.shape, bf16),
            jax.ShapeDtypeStruct((tokens, LANES), f32),
        ],
        cost_estimate=attention_cost(tokens, heads, 10),
        name="attend_back",
    )(query, keyval, shared, *tables[:3], tables[4], grad_attended, attended, logs)


MESH = pl.DeviceIdType.MESH
VMEM_LIMIT = 60 * 1024 * 1024


def partners():
    me = lax.axis_index("shard")
    core = me % 2
    return me, core, me + 1 - 2 * core, (me + 2) % 4


def greet(devices):
    barrier = pltpu.get_barrier_semaphore()
    for device in devices:
        pl.semaphore_signal(barrier, inc=1, device_id=device, device_id_type=MESH)
    pl.semaphore_wait(barrier, len(devices))


def columns(step, width):
    return pl.ds(pl.multiple_of(step * width, LANES), width)


def rows_at(start, rows):
    return pl.ds(pl.multiple_of(start * rows, 16), rows)


def remote(source, target, sems, step, device):
    return pltpu.make_async_remote_copy(
        src_ref=source, dst_ref=target, send_sem=sems.at[0, step], recv_sem=sems.at[1, step],
        device_id={"shard": device}, device_id_type=MESH,
    )


def exchange_scratch(rows, steps, width):
    part = pltpu.VMEM((steps, rows, width), bf16)
    return [part] * 6 + [
        pltpu.VMEM((steps, rows, width), f32),
        pltpu.VMEM((2 * rows, width), f32),
        pltpu.SemaphoreType.DMA((3, 2, steps)),
    ]


def each(steps, unrolled, do):
    if unrolled:
        for step in range(steps):
            do(step)
    else:
        def again(step, carry):
            do(step)
            return carry
        lax.fori_loop(0, steps, again, 0)


def sum_scatter(rows, steps, unrolled, partial, scratch, use):
    (to_sib, from_sib, to_far, from_far, own_sib, own_from, hold, stage, sems) = scratch
    me, core, sib, far = partners()
    mine = rows_at(core, rows)
    other = rows_at(1 - core, rows)

    def first(step):
        return remote(to_sib.at[step], from_sib.at[step], sems.at[0], step, sib)

    def across(step):
        return remote(to_far.at[step], from_far.at[step], sems.at[1], step, far)

    def beside(step):
        return remote(own_sib.at[step], own_from.at[step], sems.at[2], step, sib)

    def far_part(step):
        stage[...] = partial(rows_at(far // 2, 2 * rows), step)
        to_sib[step] = stage[other, :].astype(bf16)
        first(step).start()
        hold[step] = stage[mine, :]

    def far_send(step):
        first(step).wait_recv()
        to_far[step] = (hold[step] + from_sib[step].astype(f32)).astype(bf16)
        across(step).start()

    def far_step(step):
        far_part(step)
        if unrolled:
            if step > 0:
                far_send(step - 1)
        else:
            @pl.when(step > 0)
            def _():
                far_send(step - 1)

    each(steps, unrolled, far_step)
    far_send(steps - 1)

    def near_part(step):
        stage[...] = partial(rows_at(me // 2, 2 * rows), step)
        own_sib[step] = stage[other, :].astype(bf16)
        beside(step).start()
        hold[step] = stage[mine, :]

    each(steps, unrolled, near_part)

    def finish(step):
        beside(step).wait_recv()
        across(step).wait_recv()
        use(step, hold[step] + own_from[step].astype(f32) + from_far[step].astype(f32))

    each(steps, unrolled, finish)

    def settle(step):
        first(step).wait_send()
        across(step).wait_send()
        beside(step).wait_send()

    each(steps, unrolled, settle)


def spread_rows(rows, steps, width, place, all_ref, sems):
    me, core, sib, far = partners()

    def part(owner, step):
        return all_ref.at[rows_at(owner, rows), columns(step, width)]

    def across(step):
        return remote(part(me, step), part(me, step), sems.at[0], step, far)

    def beside(step):
        return remote(part(me, step), part(me, step), sems.at[1], step, sib)

    def onward(step):
        return remote(part(far, step), part(far, step), sems.at[2], step, sib)

    def send(step):
        place(step)
        across(step).start()
        beside(step).start()

    each(steps, False, send)

    def forward(step):
        across(step).wait_recv()
        onward(step).start()

    each(steps, False, forward)

    def settle(step):
        beside(step).wait_recv()
        onward(step).wait_recv()
        across(step).wait_send()
        beside(step).wait_send()
        onward(step).wait_send()

    each(steps, False, settle)


def vmem(count):
    return [pl.BlockSpec(memory_space=pltpu.VMEM)] * count


def comm_call(kernel, name, number, inputs, out_shape, scratch, flops=0, aliased={}):
    nbytes = sum(v.size * v.dtype.itemsize for v in (*inputs, *out_shape))
    return pl.pallas_call(
        kernel,
        in_specs=vmem(len(inputs) - len(aliased)) + any_space(len(aliased)),
        out_specs=vmem(len(out_shape) - len(aliased)) + any_space(len(aliased)),
        out_shape=out_shape,
        scratch_shapes=scratch,
        input_output_aliases=aliased,
        compiler_params=pltpu.CompilerParams(
            collective_id=number, has_side_effects=True, vmem_limit_bytes=VMEM_LIMIT
        ),
        cost_estimate=pl.CostEstimate(flops=0, bytes_accessed=0 * nbytes, transcendentals=0),
        name=name,
    )(*inputs)


def shape(rows, width, dtype):
    return jax.ShapeDtypeStruct((rows, width), dtype)


def gather_kernel(steps, width, own_ref, all_ref, sems):
    rows = own_ref.shape[0]
    me, core, sib, far = partners()
    greet([{"shard": sib}, {"shard": far}])

    def place(step):
        all_ref[rows_at(me, rows), columns(step, width)] = own_ref[:, columns(step, width)]

    spread_rows(rows, steps, width, place, all_ref, sems)


def gather(value, number, width):
    if lax.axis_size("shard") != 4:
        return lax.all_gather(value, "shard", axis=0, tiled=True)
    rows, total = value.shape
    steps = total // width
    (out,) = comm_call(
        functools.partial(gather_kernel, steps, width), "gather_rows", number, [value],
        [shape(4 * rows, total, bf16)], [pltpu.SemaphoreType.DMA((3, 2, steps))],
    )
    return out


def plain_gather(value):
    return lax.all_gather(value, "shard", axis=0, tiled=True)


def plain_scatter(value):
    return lax.psum_scatter(value.astype(bf16), "shard", scatter_dimension=0, tiled=True).astype(f32)


MODEL_STEP = 256


def output_kernel(relaying, att_ref, weight_ref, hidden_ref, gain_ref, *refs):
    if relaying:
        _, mixed_ref, two_ref, up_ref, *scratch, passed = refs
    else:
        mixed_ref, two_ref, *scratch = refs
    *parts, sems = scratch
    rows = hidden_ref.shape[0]
    width = MODEL_STEP
    steps = D // width
    me, core, sib, far = partners()
    devices = [{"shard": sib}, {"shard": far}]
    if relaying:
        partner, away = replica_pair()
        devices.append({"rep": partner})
    greet(devices)
    if relaying:
        @pl.when(away == 0)
        def _():
            for slot, owner in enumerate((far, far + 1 - 2 * core)):
                pass_on(up_ref, passed, slot, owner).start()

    def partial(where, step):
        return project(att_ref[where, :], weight_ref[:, columns(step, width)])

    def use(step, total):
        lanes = columns(step, width)
        mixed_ref[:, lanes] = hidden_ref[:, lanes] + residual_scale * total

    sum_scatter(rows, steps, False, partial, parts, use)
    mixed = mixed_ref[...]
    scale = norm_scale(mixed)

    def place(step):
        lanes = columns(step, width)
        two_ref[rows_at(me, rows), lanes] = (mixed_ref[:, lanes] * scale * gain_ref[:, lanes]).astype(bf16)

    spread_rows(rows, steps, width, place, two_ref, sems)
    if relaying:
        @pl.when(away == 0)
        def _():
            for slot, owner in enumerate((far, far + 1 - 2 * core)):
                pass_on(up_ref, passed, slot, owner).wait_send()

        @pl.when(away == 1)
        def _():
            for slot, owner in enumerate((far, far + 1 - 2 * core)):
                pass_on(up_ref, passed, slot, owner).wait_recv()


def output_norm(attended, weight, hidden, gain, up=None):
    if lax.axis_size("shard") != 4:
        mixed = hidden + residual_scale * plain_scatter(project(attended, weight))
        return mixed, plain_gather((mixed * norm_scale(mixed) * gain).astype(bf16))
    rows = hidden.shape[0]
    steps = D // MODEL_STEP
    scratch = exchange_scratch(rows, steps, MODEL_STEP) + [pltpu.SemaphoreType.DMA((3, 2, steps))]
    inputs = [attended, weight, hidden, gain[None]]
    outputs = [shape(rows, D, f32), shape(4 * rows, D, bf16)]
    flops = 2 * attended.size * D
    if up is None:
        return comm_call(functools.partial(output_kernel, False), "output_norm", 2, inputs, outputs, scratch, flops)
    return comm_call(
        functools.partial(output_kernel, True), "output_norm", 9, inputs + [up],
        outputs + [jax.ShapeDtypeStruct(up.shape, bf16)], scratch + [pltpu.SemaphoreType.DMA((2, 2))], flops,
        aliased={4: 2},
    )


def down_kernel(passing, act_ref, given_ref, mixed_ref, out_ref, low_ref, *scratch):
    rows = mixed_ref.shape[0]
    width = MODEL_STEP
    steps = D // width
    me, core, sib, far = partners()
    devices = [{"shard": sib}, {"shard": far}]
    weight_ref = given_ref
    if passing:
        got_ref, weight_ref, *parts, sems = scratch
        size, more = given_ref.shape[0], weight_ref.shape[0] - given_ref.shape[0]
        weight_ref[pl.ds(pl.multiple_of((1 - core) * size, 16), more), :] = jnp.zeros((more, D), bf16)
        piece = 64

        def fill(step):
            source = pl.ds(pl.multiple_of(step * piece, 16), piece)
            target = pl.ds(pl.multiple_of(step * piece + core * more, 16), piece)
            weight_ref[target, :] = given_ref[source, :]

        each(size // piece, False, fill)
        section = lax.axis_index("section")
        devices.append({"section": 1 - section})
    else:
        parts = scratch
    greet(devices)

    def onward(step):
        lanes = columns(step, width)
        return pltpu.make_async_remote_copy(
            src_ref=low_ref.at[:, lanes], dst_ref=got_ref.at[:, lanes], send_sem=sems.at[0, step],
            recv_sem=sems.at[1, step], device_id={"section": 1 - section}, device_id_type=MESH,
        )

    def partial(where, step):
        return project(act_ref[where, :], weight_ref[:, columns(step, width)])

    def use(step, total):
        lanes = columns(step, width)
        out = mixed_ref[:, lanes] + residual_scale * total
        out_ref[:, lanes] = out
        low_ref[:, lanes] = out.astype(bf16)
        if passing:
            onward(step).start()

    sum_scatter(rows, steps, False, partial, parts, use)
    if passing:
        each(steps, False, lambda step: onward(step).wait())


def down_project(activated, weight, mixed, passing):
    count = lax.axis_size("shard")
    if count != 4:
        if passing:
            weight = window_rows(weight, count)
        output = mixed + residual_scale * plain_scatter(project(activated, weight))
        low = output.astype(bf16)
        return (output, low) + ((lax.ppermute(low, "section", [(0, 1)]), weight) if passing else ())
    rows = mixed.shape[0]
    steps = D // MODEL_STEP
    scratch = exchange_scratch(rows, steps, MODEL_STEP)
    return comm_call(
        functools.partial(down_kernel, passing), "down_project", 3 if passing else 4,
        [activated, weight, mixed],
        [shape(rows, D, f32)] + [shape(rows, D, bf16)] * (2 if passing else 1)
        + [shape(HIDDEN_WINDOW, D, bf16)] * passing,
        scratch + ([pltpu.SemaphoreType.DMA((2, steps))] if passing else []),
        flops=2 * activated.size * D,
    )


def mlp_back_kernel(gate_ref, up_ref, gate_weight_ref, up_weight_ref, mixed_ref, grad_ref, gain_ref, out_ref, dgain_ref, branch_ref,
                    *scratch):
    *parts, sems = scratch
    rows = mixed_ref.shape[0]
    width = MODEL_STEP
    steps = D // width
    me, core, sib, far = partners()
    greet([{"shard": sib}, {"shard": far}])

    def partial(where, step):
        rows_of = columns(step, width)
        return contract_cols(gate_ref[where, :], gate_weight_ref[rows_of, :]) + contract_cols(
            up_ref[where, :], up_weight_ref[rows_of, :]
        )

    def use(step, total):
        out_ref[:, columns(step, width)] = total

    sum_scatter(rows, steps, False, partial, parts, use)
    mixed = mixed_ref[...]
    scale = norm_scale(mixed)
    inner = jnp.mean(mixed * out_ref[...] * gain_ref[...], axis=-1, keepdims=True)
    slope = scale * scale * scale * inner

    def place(step):
        lanes = columns(step, width)
        grad, value = out_ref[:, lanes], mixed_ref[:, lanes]
        dgain_ref[:, lanes] = jnp.sum(grad * value * scale, axis=0, keepdims=True)
        total = grad_ref[:, lanes] + scale * (grad * gain_ref[:, lanes]) - value * slope
        out_ref[:, lanes] = total
        branch_ref[rows_at(me, rows), lanes] = (residual_scale * total).astype(bf16)

    spread_rows(rows, steps, width, place, branch_ref, sems)


def mlp_back(grad_gate, grad_up, gate_weight, up_weight, mixed, grad_out, gain):
    if lax.axis_size("shard") != 4:
        grad = plain_scatter(contract_cols(grad_gate, gate_weight) + contract_cols(grad_up, up_weight))
        back, dgain = norm_back(mixed, norm_scale(mixed), gain, grad)
        grad_mixed = grad_out + back
        return grad_mixed, dgain[None], plain_gather((residual_scale * grad_mixed).astype(bf16))
    rows = mixed.shape[0]
    steps = D // MODEL_STEP
    return comm_call(
        mlp_back_kernel, "mlp_back", 5,
        [grad_gate, grad_up, gate_weight, up_weight, mixed, grad_out, gain[None]],
        [shape(rows, D, f32), shape(1, D, f32), shape(4 * rows, D, bf16)],
        exchange_scratch(rows, steps, MODEL_STEP) + [pltpu.SemaphoreType.DMA((3, 2, steps))],
        flops=4 * grad_gate.size * D,
    )


LATENT_STEP = 256


def latent_back_kernel(gq_ref, gkv_ref, gsh_ref, qup_ref, lup_ref, out_ref, *scratch):
    rows = out_ref.shape[0]
    width = LATENT_STEP
    me, core, sib, far = partners()
    greet([{"shard": sib}, {"shard": far}])

    def partial(where, step):
        if step < QRANK // width:
            return contract_cols(gq_ref[where, :], qup_ref[step * width:(step + 1) * width, :])
        if step == QRANK // width:
            return contract_cols(gkv_ref[where, :], lup_ref[...])
        shared = gsh_ref[where, :]
        return jnp.concatenate([shared, jnp.zeros_like(shared)], axis=1)

    def use(step, total):
        out_ref[:, step * width:(step + 1) * width] = total

    sum_scatter(rows, out_ref.shape[1] // width, True, partial, scratch, use)


def latent_back(grad_query, grad_keyval, grad_shared, query_up, latent_up):
    if lax.axis_size("shard") != 4:
        return plain_scatter(
            jnp.concatenate(
                [contract_cols(grad_query, query_up), contract_cols(grad_keyval, latent_up), grad_shared],
                axis=1,
            )
        )
    rows = grad_query.shape[0] // 4
    steps = QRANK // LATENT_STEP + 2
    (out,) = comm_call(
        latent_back_kernel, "latent_back", 6, [grad_query, grad_keyval, grad_shared, query_up, latent_up],
        [shape(rows, steps * LATENT_STEP, f32)], exchange_scratch(rows, steps, LATENT_STEP),
        flops=2 * grad_query.size * QRANK + 2 * grad_keyval.size * KVRANK,
    )
    return out


def any_space(count):
    return [pl.BlockSpec(memory_space=pl.ANY)] * count


def pair(value, index):
    return value.at[0, index], value.at[1, index]


def send_to(source, target, sems, index, device):
    send, receive = pair(sems, index)
    return pltpu.make_async_remote_copy(
        src_ref=source, dst_ref=target, send_sem=send, recv_sem=receive,
        device_id={"shard": device}, device_id_type=MESH,
    )


def replica_pair():
    replica = lax.axis_index("rep")
    return replica + 1 - 2 * (replica % 2), (lax.axis_index("shard") + replica) % 2


def pass_on(target, sems, step, owner):
    partner, _ = replica_pair()
    return pltpu.make_async_remote_copy(
        src_ref=target.at[owner], dst_ref=target.at[owner], send_sem=sems.at[0, step], recv_sem=sems.at[1, step],
        device_id={"rep": partner}, device_id_type=MESH,
    )


def move_kernel(whole, alike, split, relayed, *refs):
    amount = whole + len(split) + len(relayed)
    inputs, outputs, held = refs[:amount], refs[amount:2 * amount], refs[2 * amount:3 * amount]
    sems, local, *relays = refs[3 * amount:]
    me, core, sib, far = partners()
    diagonal = far + 1 - 2 * core
    devices = [{"shard": sib}, {"shard": far}, {"shard": diagonal}]
    if relayed:
        partner, away = replica_pair()
        devices.append({"rep": partner})
    greet(devices)
    waits, forwards, keeps, bulk = [], [], [], []
    number = 0
    for i, (source, target) in enumerate(zip(inputs, outputs)):
        if i < whole:
            to_far = send_to(source, target.at[me], sems, number, far)
            to_sib = send_to(source, target.at[me], sems, number + 1, sib)
            onward = send_to(target.at[far], target.at[far], sems, number + 2, sib)
            if i < alike:
                @pl.when(away == 0)
                def _():
                    to_far.start()
            else:
                to_far.start()
            to_sib.start()
            forwards.append((target, to_far, onward))
            waits.append(to_sib)
            kept = source
        elif i < whole + len(split):
            part = split[i - whole]
            for j, device in enumerate((far, diagonal, sib)):
                copy = send_to(part(source, device), target.at[me], sems, number + j, device)
                copy.start()
                waits.append(copy)
            kept = part(source, me)
        else:
            begin, arrive, passed = relays
            place = i - whole - len(split)
            part = relayed[place][0]
            taker = far // 2 * 2 + lax.axis_index("rep") % 2

            def across(owner, slot, source=source, target=target, part=part, place=place):
                return pltpu.make_async_remote_copy(
                    src_ref=part(source, taker), dst_ref=target.at[owner], send_sem=begin.at[place],
                    recv_sem=arrive.at[place, slot], device_id={"shard": taker}, device_id_type=MESH,
                )

            across(me, away).start()
            beside = send_to(part(source, sib), target.at[me], sems, number, sib)
            beside.start()
            waits.append(beside)
            bulk.append((place, target, across))
            kept = part(source, me)
        number += 3
        keep = pltpu.make_async_copy(kept, held[i], local.at[0, i])
        keep.start()
        keeps.append((keep, pltpu.make_async_copy(held[i], target.at[me], local.at[1, i])))
    for keep, store in keeps:
        keep.wait()
        store.start()
    for step, (target, to_far, onward) in enumerate(forwards):
        if step < alike:
            hop = pass_on(target, relays[2], 2 * len(relayed) + step, far)

            @pl.when(away == 0)
            def _():
                to_far.wait_recv()
                hop.start()

            @pl.when(away == 1)
            def _():
                hop.wait_recv()
        else:
            to_far.wait_recv()
        onward.start()
    for step, (target, to_far, onward) in enumerate(forwards):
        if step < alike:
            hop = pass_on(target, relays[2], 2 * len(relayed) + step, far)

            @pl.when(away == 0)
            def _():
                to_far.wait_send()
                hop.wait_send()
        else:
            to_far.wait_send()
        onward.wait()
    for copy in waits:
        copy.wait()
    for keep, store in keeps:
        store.wait()
    for place, target, across in bulk:
        passing = relayed[place][1]
        passed = relays[2]

        @pl.when(away == 0)
        def _():
            for slot, owner in enumerate((far, diagonal)):
                across(owner, slot).wait_recv()
                if passing:
                    pass_on(target, passed, 2 * place + slot, owner).start()

    for place, target, across in bulk:
        passing = relayed[place][1]
        passed = relays[2]
        across(me, away).wait_send()
        if passing:
            @pl.when(away == 0)
            def _():
                for slot, owner in enumerate((far, diagonal)):
                    pass_on(target, passed, 2 * place + slot, owner).wait_send()

            @pl.when(away == 1)
            def _():
                for slot, owner in enumerate((far, diagonal)):
                    pass_on(target, passed, 2 * place + slot, owner).wait_recv()


def move(name, number, wholes, splits, relayed=(), alike=0):
    inputs = list(wholes) + [entry[0] for entry in (*splits, *relayed)]
    shapes = [w.shape for w in wholes] + [entry[1] for entry in (*splits, *relayed)]
    out_shape = [jax.ShapeDtypeStruct((4,) + tuple(sh), v.dtype) for sh, v in zip(shapes, inputs)]
    scratch = [pltpu.VMEM(sh, v.dtype) for sh, v in zip(shapes, inputs)]
    scratch += [pltpu.SemaphoreType.DMA((2, 3 * len(inputs))), pltpu.SemaphoreType.DMA((2, len(inputs)))]
    if relayed:
        amount = len(relayed)
        scratch += [
            pltpu.SemaphoreType.DMA((amount,)), pltpu.SemaphoreType.DMA((amount, 2)),
            pltpu.SemaphoreType.DMA((2, 2 * amount + len(wholes))),
        ]
    return pl.pallas_call(
        functools.partial(move_kernel, len(wholes), alike, [f for _, _, f in splits], [entry[2:] for entry in relayed]),
        in_specs=any_space(len(inputs)),
        out_specs=any_space(len(inputs)),
        out_shape=out_shape,
        scratch_shapes=scratch,
        compiler_params=pltpu.CompilerParams(
            collective_id=number, has_side_effects=True, vmem_limit_bytes=VMEM_LIMIT
        ),
        cost_estimate=pl.CostEstimate(
            flops=0, bytes_accessed=sum(4 * v.size * v.dtype.itemsize for v in inputs), transcendentals=0
        ),
        name=name,
    )(*inputs)


HIDDEN_WINDOW = 1664


def hidden_columns(ref, owner):
    return ref.at[:, pl.ds(pl.multiple_of(owner // 2 * 3200 + owner % 2 * 1536, LANES), HIDDEN_WINDOW)]


QUERY_WINDOW = 1024


def query_window(ref, owner):
    return ref.at[:, pl.ds(pl.multiple_of(owner // 2 * 1920 + owner % 2 * 896, LANES), QUERY_WINDOW)]


def latent_window(ref, owner):
    return ref.at[:, pl.ds(pl.multiple_of(owner * 1280, LANES), 1280)]


def first_move(query_down, latent_down, query_up, latent_up, segments, gate, up, count):
    if count != 4:
        gate, up = spread_hidden(gate, up, count)
        return (
            plain_gather(query_down), plain_gather(latent_down), pad_heads(spread(query_up, count)),
            spread(latent_up, count), plain_gather(segments), gate, up,
        )
    part = (gate.shape[0], HIDDEN_WINDOW)
    heads = [(query_up, (query_up.shape[0], QUERY_WINDOW), query_window),
             (latent_up, (latent_up.shape[0], 1280), latent_window)]
    relayed = []
    if shared_links(count):
        relayed = [entry + (True,) for entry in heads]
        relayed += [(gate, part, hidden_columns, True), (up, part, hidden_columns, False)]
        heads = []
    down_q, down_kv, groups, up_q, up_kv, *hidden = move(
        "first_move", 7, [query_down, latent_down, segments], heads, relayed, 2 if relayed else 0
    )
    merge = lambda value: value.reshape((-1,) + value.shape[2:])
    up_q = lax.dynamic_slice_in_dim(merge(up_q), lax.axis_index("shard") % 2 * 64, 960, 1)
    gate, up = hidden if relayed else spread_hidden(gate, up, count)
    return merge(down_q), merge(down_kv), pad_heads(up_q), merge(up_kv), merge(groups), gate, up


EXCHANGE_WIDTH = 1280


def last_move(grad_lat, gain_terms, query_part, latent_part, count):
    if count != 4:
        parts = (
            plain_gather(grad_lat), plain_gather(gain_terms), collect(cut_heads(query_part), count),
            collect(latent_part, count),
        )
        return parts, lambda parts: parts
    side = lambda value: value.transpose(1, 0, 2).reshape(value.shape[1], -1)
    same = lambda value: jnp.broadcast_to(value[None], (count,) + value.shape)
    wide = lambda value: jnp.pad(value, ((0, 0), (0, EXCHANGE_WIDTH - value.shape[1])))
    amount = gain_terms.shape[1]
    gain_rows = -(-amount // EXCHANGE_WIDTH)
    gain_rows += -gain_rows % 16
    gains = jnp.pad(gain_terms[0].astype(bf16), (0, gain_rows * EXCHANGE_WIDTH - amount)).reshape(gain_rows, -1)
    pieces = [
        query_part.reshape(count, -1, EXCHANGE_WIDTH), latent_part.reshape(count, -1, EXCHANGE_WIDTH),
        same(wide(grad_lat)), same(gains),
    ]
    got = lax.all_to_all(jnp.concatenate(pieces, axis=1), "shard", 0, 0, tiled=True)
    ends = [0]
    for piece in pieces:
        ends.append(ends[-1] + piece.shape[1])
    def finish(got):
        got_q, got_kv, lat, gains = (got[:, start:end] for start, end in zip(ends, ends[1:]))
        return (
            lat.reshape(-1, EXCHANGE_WIDTH)[:, :grad_lat.shape[1]],
            gains.reshape(count, -1)[:, :amount].astype(f32), cut_heads(side(got_q)), side(got_kv),
        )

    return got, finish


def place_kernel(*refs):
    me, core, sib, far = partners()
    *parts, out_ref = refs
    out_ref[...] = jnp.zeros_like(out_ref)
    for owner, part in zip((me, sib, far, far + 1 - 2 * core), parts):
        lanes = pl.ds(pl.multiple_of(owner // 2 * 3200 + owner % 2 * 1536, LANES), HIDDEN_WINDOW)
        out_ref[:, lanes] += part[...].astype(f32)


def head_lanes(value):
    return jnp.pad(value, ((0, 0), (NOPE, LANES - NOPE - ROPE)))


def layer_forward(hidden, own_tables, tables, gains, weights, passing, lacking, early):
    input_gain, query_gain, latent_gain, post_gain = gains
    down_both, query_up, latent_up, output_weight, gate_weight, up_weight, down_weight = weights
    scale_in = norm_scale(hidden)
    normed = (hidden * scale_in * input_gain).astype(bf16)
    down_q, down_kv = down_both
    latent_q = project(normed, down_q)
    latent_kv = project(normed, down_kv)
    latent = latent_kv[:, :KVRANK]
    scale_q = norm_scale(latent_q)
    scale_kv = norm_scale(latent)
    own_in = jnp.concatenate(
        [
            latent_q * scale_q * query_gain,
            latent * scale_kv * latent_gain,
            head_lanes(rotate(latent_kv[:, KVRANK:], *own_tables)),
        ],
        axis=1,
    ).astype(bf16)
    all_in = gather(own_in, 0, 384)
    all_in, early = together(all_in, early)
    if lacking is not None:
        early = plain_gather(early)
    query_in = all_in[:, :QRANK]
    kv_in = all_in[:, QRANK:QRANK + KVRANK]
    shared = all_in[:, QRANK + KVRANK:]
    attended, queries, keyval, logs = attend(
        project(query_in, query_up), project(kv_in, latent_up), shared, tables
    )
    if lacking:
        mixed, normed_two, up_weight = output_norm(attended, output_weight, hidden, post_gain, up_weight)
    else:
        mixed, normed_two = output_norm(attended, output_weight, hidden, post_gain)
    normed_two, early = together(normed_two, early)
    merge = lambda value: value.reshape(D, -1)
    gate = project(normed_two, merge(gate_weight)).astype(bf16)
    up = project(normed_two, merge(up_weight)).astype(bf16)
    activated = (jax.nn.silu(gate.astype(f32)) * up.astype(f32)).astype(bf16)
    def outputs(value):
        return down_project(value, down_weight, mixed, passing)

    kept = (hidden, scale_in, normed, latent_q, scale_q, latent, scale_kv, query_in, kv_in,
            shared, queries, keyval, logs, attended, mixed, normed_two, gate, up)
    return (outputs, activated, kept, merge(gate_weight), merge(up_weight), early)


def gate_backward(grad_act, gate, up):
    sigmoid = jax.nn.sigmoid(gate)
    grad_gate = (grad_act * up * sigmoid * (1.0 + gate * (1.0 - sigmoid))).astype(bf16)
    grad_up = (grad_act * gate * sigmoid).astype(bf16)
    return grad_gate, grad_up


def mlp_backward(grad_out, kept, gains, weights, gather_down, wanted):
    mixed, gate, up = kept[14], kept[16], kept[17]
    gate_weight, up_weight, down_weight = weights[4:]
    own_down = (residual_scale * grad_out).astype(bf16)
    grad_down, wanted = together(gather_down(own_down), wanted)
    grad_gate, grad_up = gate_backward(contract_cols(grad_down, down_weight), gate.astype(f32), up.astype(f32))
    grad_mixed, dgain_post, grad_branch = mlp_back(
        grad_gate, grad_up, gate_weight, up_weight, mixed, grad_out, gains[3]
    )
    return (grad_gate, grad_up), wanted, grad_down, grad_mixed, dgain_post[0], grad_branch


def attention_backward(grad_mixed, grad_branch, kept, own_tables, tables, gains, weights, wanted):
    (hidden, scale_in, normed, latent_q, scale_q, latent, scale_kv, query_in, kv_in,
     shared, queries, keyval, logs, attended, mixed, normed_two, gate, up) = kept
    input_gain, query_gain, latent_gain, post_gain = gains
    down_both, query_up, latent_up, output_weight = weights[:4]
    cosine, sine = own_tables
    grad_attended = contract_cols(grad_branch, output_weight).astype(bf16)
    grad_query, grad_keyval, grad_shared = attend_back(
        queries, keyval, shared, tables, grad_attended, attended, logs
    )
    grad_in = latent_back(grad_query, grad_keyval, grad_shared, query_up, latent_up)
    grad_in, wanted = together(grad_in, wanted)
    grad_latent_q, dgain_query = norm_back(latent_q, scale_q, query_gain, grad_in[:, :QRANK])
    grad_latent, dgain_latent = norm_back(
        latent, scale_kv, latent_gain, grad_in[:, QRANK:QRANK + KVRANK]
    )
    start = QRANK + KVRANK + NOPE
    grad_shared = rotate(grad_in[:, start:start + ROPE], cosine, -sine)
    grad_lat = jnp.concatenate(
        [grad_latent_q, grad_latent, jnp.pad(grad_shared, ((0, 0), (0, LANES - ROPE)))], axis=1
    ).astype(bf16)
    down_q, down_kv = down_both
    grad_normed = contract_cols(grad_lat[:, :QRANK], down_q) + contract_cols(
        grad_lat[:, QRANK:QRANK + KVRANK + ROPE], down_kv
    )
    grad_hidden_norm, dgain_input = norm_back(hidden, scale_in, input_gain, grad_normed)
    grad_hidden = grad_mixed + grad_hidden_norm
    found = (grad_branch, grad_query, grad_keyval, grad_lat)
    return (grad_hidden, found, (dgain_input, dgain_query, dgain_latent), wanted)


def spread(weight, count):
    rows, columns = weight.shape
    parts = weight.reshape(rows, count, columns // count).transpose(1, 0, 2)
    return lax.all_to_all(parts, "shard", 0, 0, tiled=True).reshape(rows * count, columns // count)


def collect(grad, count):
    rows, columns = grad.shape
    parts = lax.all_to_all(
        grad.reshape(count, rows // count, columns), "shard", 0, 0, tiled=True
    )
    return parts.transpose(1, 0, 2).reshape(rows // count, columns * count)


def pad_heads(weight):
    rows, columns = weight.shape
    heads = weight.reshape(rows, columns // (NOPE + ROPE), NOPE + ROPE)
    return jnp.pad(heads, ((0, 0), (0, 0), (0, LANES - NOPE - ROPE))).reshape(rows, -1)


def cut_heads(grad):
    rows, columns = grad.shape
    heads = grad.reshape(rows, columns // LANES, LANES)[:, :, :NOPE + ROPE]
    return heads.reshape(rows, -1)


def swap(value, step):
    count = lax.axis_size("shard")
    return lax.ppermute(value, "shard", [(source, source ^ step) for source in range(count)])


def hidden_window(count):
    size = FF // count
    width = -(-size // LANES) * LANES
    starts = [owner * size // LANES * LANES for owner in range(count)]
    starts = [min(start, FF - width) for start in starts]
    return size, width, starts, [owner * size - start for owner, start in enumerate(starts)]


def take_at(table, place):
    return jnp.asarray(table, jnp.int32)[place]


def shared_links(count):
    return count == 4 and lax.axis_size("rep") % 2 == 0


def spread_hidden(gate, up, count):
    me = lax.axis_index("shard")
    size, width, starts, offsets = hidden_window(count)
    rows = gate.shape[0]
    results = []
    for weight in (gate, up):
        whole = jnp.zeros((rows * count, width), bf16)
        for step in range(count):
            owner = me ^ step
            part = lax.dynamic_slice(weight, (0, take_at(starts, owner)), (rows, width))
            if step:
                part = swap(part, step)
            whole = lax.dynamic_update_slice(whole, part, (owner * rows, 0))
        results.append(whole)
    return results


def window_rows(down, count):
    size, width, starts, offsets = hidden_window(count)
    whole = jnp.zeros((width, down.shape[1]), bf16)
    return lax.dynamic_update_slice(whole, down, (take_at(offsets, lax.axis_index("shard")), 0))


def chip_gradients_kernel(order_ref, two_ref, gate_ref, up_ref, gate_out, up_out, turned):
    tokens, rows = two_ref.shape
    piece = 512
    for start in range(0, tokens, piece):
        size = min(piece, tokens - start)
        turned[:, start:start + size] = two_ref[start:start + size, :].T
    width = gate_ref.shape[1]
    whole = width // piece
    for grad, out in ((gate_ref, gate_out), (up_ref, up_out)):
        def tile(step):
            lanes = columns(step, piece)
            out[0, :, lanes] = project(turned[...], grad[:, lanes]).astype(bf16)

        each(whole, False, tile)
        if whole * piece < width:
            out[0, :, whole * piece:] = project(turned[...], grad[:, whole * piece:]).astype(bf16)


def chip_gradients(two_all, grad_gate, grad_up):
    me, core, sib, far = partners()
    tokens, width = grad_gate.shape
    rows = D // 4
    held = pl.BlockSpec((tokens, width), lambda i, order: (0, 0), pipeline_mode=pl.Buffered(1))
    part = pl.BlockSpec((1, rows, width), lambda i, order: (i, 0, 0))
    gate, up = pl.pallas_call(
        chip_gradients_kernel,
        grid_spec=pltpu.PrefetchScalarGridSpec(
            num_scalar_prefetch=1,
            grid=(2,),
            in_specs=[pl.BlockSpec((tokens, rows), lambda i, order: (0, order[i])), held, held],
            out_specs=[part, part],
            scratch_shapes=[pltpu.VMEM((rows, tokens), bf16)],
        ),
        out_shape=[jax.ShapeDtypeStruct((2, rows, width), bf16)] * 2,
        compiler_params=pltpu.CompilerParams(vmem_limit_bytes=VMEM_LIMIT),
        name="chip_gradients",
    )(jnp.stack([sib, me]).astype(jnp.int32), two_all, grad_gate, grad_up)
    return [gate[0], up[0], gate[1], up[1]]


def recompute_kernel(from_ref, own_ref, here_ref, two_ref, near_ref, beside_ref, gate_ref, up_ref, rows_ref,
                     act_own, gate_own, up_own, act_out, gate_out, up_out, down_ref):
    place = pl.program_id(0)
    width = gate_ref.shape[1]
    piece = 512

    @pl.when(own_ref[place] == 1)
    def _():
        act_out[...] = act_own[...]
        gate_out[...] = gate_own[...]
        up_out[...] = up_own[...]

    @pl.when((own_ref[place] == 0) & (here_ref[place] == 1))
    def _():
        down_ref[...] = near_ref[...]

    @pl.when((own_ref[place] == 0) & (here_ref[place] == 0))
    def _():
        down_ref[...] = beside_ref[...]

    @pl.when(own_ref[place] == 0)
    def _():
        def tile(lanes, some_rows):
            gate = project(two_ref[...], gate_ref[:, lanes])
            up = project(two_ref[...], up_ref[:, lanes])
            grad = contract_cols(down_ref[...], rows_ref[some_rows, :])
            sigmoid = jax.nn.sigmoid(gate)
            silu = gate * sigmoid
            act_out[:, lanes] = (silu * up).astype(bf16)
            gate_out[:, lanes] = (grad * up * sigmoid * (1.0 + gate * (1.0 - sigmoid))).astype(bf16)
            up_out[:, lanes] = (grad * silu).astype(bf16)

        each(width // piece, False, lambda step: tile(columns(step, piece), columns(step, piece)))
        if width % piece:
            rest = slice(width // piece * piece, width)
            tile(rest, rest)


def recompute(two_all, down_halves, gate_columns, up_columns, down_rows, own):
    reps = lax.axis_size("rep")
    tokens, width = two_all.shape[0], gate_columns.shape[1]
    tile = own[0].shape[0] // 2
    places = jnp.arange(tokens // tile, dtype=jnp.int32)
    half = places // reps
    is_own = places % reps == lax.axis_index("rep")
    is_here = half == lax.axis_index("shard") % 2
    whole = lambda value: pl.BlockSpec(value.shape, lambda i, a, b, c: (0, 0), pipeline_mode=pl.Buffered(1))
    wide = pl.BlockSpec((tile, D), lambda i, a, b, c: (i, 0))
    again = pl.BlockSpec((tile, D), lambda i, a, b, c: (i % reps, 0))
    mine = pl.BlockSpec((tile, width), lambda i, a, b, c: (a[i], 0), pipeline_mode=pl.Buffered(1))
    part = pl.BlockSpec((tile, width), lambda i, a, b, c: (i, 0))
    return pl.pallas_call(
        recompute_kernel,
        grid_spec=pltpu.PrefetchScalarGridSpec(
            num_scalar_prefetch=3,
            grid=(tokens // tile,),
            in_specs=[wide, again, again, whole(gate_columns), whole(up_columns), whole(down_rows), mine, mine, mine],
            out_specs=[part] * 3,
            scratch_shapes=[pltpu.VMEM((tile, D), bf16)],
        ),
        out_shape=[jax.ShapeDtypeStruct((tokens, width), bf16)] * 3,
        compiler_params=pltpu.CompilerParams(vmem_limit_bytes=VMEM_LIMIT),
        name="recompute",
    )(half, is_own.astype(jnp.int32), is_here.astype(jnp.int32), two_all, *down_halves,
      gate_columns, up_columns, down_rows, *own)


def down_gradient_kernel(act_ref, near_ref, beside_ref, out_ref, turned):
    tokens, width = act_ref.shape
    size = out_ref.shape[0]
    piece = 512

    @pl.when(pl.program_id(0) == 0)
    def _():
        for start in range(0, tokens, piece):
            turned[:, start:start + piece] = act_ref[start:start + piece, :].T

    core = lax.axis_index("shard") % 2
    offset = core * (width - size)
    half = size // 2
    some = tokens // 2
    near = pl.ds(pl.multiple_of(core * some, LANES), some)
    beside = pl.ds(pl.multiple_of((1 - core) * some, LANES), some)

    def tile(step):
        rows = pl.ds(pl.multiple_of(step * half, 16), half)
        source = pl.ds(pl.multiple_of(step * half + offset, 16), half)
        out_ref[rows, :] = project(turned[source, near], near_ref[...]) + project(turned[source, beside], beside_ref[...])

    each(2, False, tile)


def down_gradient(activated_all, down_halves):
    tokens, width = activated_all.shape
    size, piece = FF // 4, 512
    return pl.pallas_call(
        down_gradient_kernel,
        grid=(D // piece,),
        in_specs=[pl.BlockSpec((tokens, width), lambda i: (0, 0), pipeline_mode=pl.Buffered(1)),
                  pl.BlockSpec((tokens // 2, piece), lambda i: (0, i)), pl.BlockSpec((tokens // 2, piece), lambda i: (0, i))],
        out_specs=pl.BlockSpec((size, piece), lambda i: (0, i)),
        out_shape=jax.ShapeDtypeStruct((size, D), f32),
        scratch_shapes=[pltpu.VMEM((width, tokens), bf16)],
        compiler_params=pltpu.CompilerParams(vmem_limit_bytes=VMEM_LIMIT),
        name="down_gradient",
    )(activated_all, *down_halves)


def half_everywhere(group, count):
    if count != 4:
        return group
    rows = group.shape[0] // 2
    half = lax.dynamic_slice_in_dim(group, lax.axis_index("shard") % 2 * rows, rows, 0)
    return lax.all_gather(half, "rep", axis=0, tiled=True)


def everyone(half, count):
    if count != 4:
        return lax.all_gather(half, "rep", axis=0, tiled=True)
    return lax.all_gather(half, "shard", axis=0, tiled=True, axis_index_groups=[[0, 1], [2, 3]])


def owner_gradient(two_all, grad, owner, count):
    rows = D // count
    left = lax.dynamic_slice(two_all, (0, owner * rows), (two_all.shape[0], rows))
    return contract_rows(left, grad).astype(bf16)


def place_windows(parts, count):
    size, width, starts, offsets = hidden_window(count)
    rows = parts[0].shape[0]
    if count == 4:
        tile = 64
        return pl.pallas_call(
            place_kernel,
            grid=(rows // tile,),
            in_specs=[pl.BlockSpec((tile, width), lambda i: (i, 0))] * 4,
            out_specs=pl.BlockSpec((tile, FF), lambda i: (i, 0)),
            out_shape=jax.ShapeDtypeStruct((rows, FF), f32),
            compiler_params=pltpu.CompilerParams(vmem_limit_bytes=VMEM_LIMIT),
            cost_estimate=pl.CostEstimate(flops=0, bytes_accessed=rows * FF * 8, transcendentals=0),
            name="place_windows",
        )(*parts)
    me = lax.axis_index("shard")
    gathered = jnp.zeros((count, rows, width), bf16)
    for step, part in enumerate(parts):
        gathered = lax.dynamic_update_slice(gathered, part[None], (me ^ step, 0, 0))
    pieces = [gathered[owner, :, offset:offset + size] for owner, offset in enumerate(offsets)]
    return jnp.concatenate(pieces, axis=1).astype(f32)


def together(*values):
    return lax.optimization_barrier(values)


def body(tokens, segment_ids, input_gain, query_gain, latent_gain, post_gain, query_down, query_up,
         latent_down, latent_up, output_weight, gate_weight, up_weight, down_weight, cotangent):
    at_start = lax.axis_index("section") == 0
    count = lax.axis_size("shard")
    size, width, starts, offsets = hidden_window(count)
    gains = (input_gain[0], query_gain[0], latent_gain[0], post_gain[0])
    down_q, down_kv, query_up_all, latent_up_all, groups, gate_columns, up_columns = first_move(
        query_down[0], latent_down[0], query_up[0], latent_up[0], segment_ids, gate_weight[0], up_weight[0], count
    )
    down_both = (down_q, down_kv)
    own_tables = tuple(t.reshape(-1, ROPE // 2) for t in slot_tables(segment_ids))
    tables = head_tables(groups)

    weights = (down_both, query_up_all, latent_up_all, output_weight[0], gate_columns, up_columns, down_weight[0])
    start = tokens.astype(f32)
    last = cotangent.astype(f32)
    last_down = (residual_scale * last).astype(bf16)
    outputs, activated, _, gate_columns, up_columns, all_last = layer_forward(
        start, own_tables, tables, gains, weights, True, shared_links(count), last_down
    )
    leaving, low, received, down_rows = outputs(activated)
    weights = weights[:4] + (gate_columns, up_columns, down_rows)
    entering = jnp.where(at_start, start, received.astype(f32))
    _, kept_activated, kept, _, _, _ = layer_forward(
        entering, own_tables, tables, gains, weights, False, None, all_last
    )

    (hidden, scale_in, normed, latent_q, scale_q, latent, scale_kv, query_in, kv_in,
     shared, queries, keyval, logs, attended, mixed, normed_two, gate, up) = kept
    half_two = half_everywhere(normed_two, count)
    _, _, _, grad_mixed, _, grad_branch = mlp_backward(last, kept, gains, weights, lambda own: all_last, at_start)
    grad, _, _, half_two = attention_backward(
        grad_mixed, grad_branch, kept, own_tables, tables, gains, weights, half_two
    )
    two_all = everyone(half_two, count)
    grad_low, kept_activated = together(grad.astype(bf16), kept_activated)
    returned = lax.ppermute(grad_low, "section", [(1, 0)])
    leaving, boundary = down_project(kept_activated, down_rows, mixed, False)
    incoming = jnp.where(at_start, returned.astype(f32), last)
    incoming, boundary = together(incoming, boundary)

    own_grads, two_all, grad_down, grad_mixed, dgain_post, grad_branch = mlp_backward(
        incoming, kept, gains, weights, lambda own: gather(own, 1, 256), two_all
    )
    half_down = half_everywhere(grad_down, count)
    part_output = contract_rows(attended, grad_branch).astype(bf16)
    grad_branch, part_output = together(grad_branch, part_output)

    grad, found, (dgain_input, dgain_query, dgain_latent), _ = attention_backward(
        grad_mixed, grad_branch, kept, own_tables, tables, gains, weights, at_start
    )
    grad_branch, grad_query, grad_keyval, grad_lat = found
    gain_terms = jnp.concatenate([dgain_input, dgain_query, dgain_latent, dgain_post])[None]
    normed_rows = lax.all_to_all(
        normed.reshape(normed.shape[0], count, -1).transpose(1, 0, 2), "shard", 0, 0, tiled=True
    ).reshape(normed.shape[0] * count, -1)
    part_query = contract_rows(query_in, grad_query).astype(bf16)
    part_latent = contract_rows(kv_in, grad_keyval).astype(bf16)
    gain_terms, half_down = together(gain_terms, half_down)
    exchanged, exchange_end = last_move(grad_lat, gain_terms, part_query, part_latent, count)
    part_output, half_down = together(part_output, half_down)
    down_all = [half_down, swap(half_down, 1)] if count == 4 else everyone(half_down, count)
    total_output = lax.psum(part_output, "rep")
    down_all, two_all, own_grads, normed_rows = together(down_all, two_all, own_grads, normed_rows)
    if count == 4:
        activated_all, grad_gate, grad_up = recompute(
            two_all, down_all, gate_columns, up_columns, down_rows, (kept_activated, *own_grads)
        )
    else:
        gate_all = project(two_all, gate_columns)
        up_all = project(two_all, up_columns)
        activated_all = (jax.nn.silu(gate_all) * up_all).astype(bf16)
        grad_gate, grad_up = gate_backward(contract_cols(down_all, down_rows), gate_all, up_all)
    def attention_shares(exchanged):
        lat_all, gains_all, part_query, part_latent = exchange_end(exchanged)
        part_down = contract_rows(normed_rows, lat_all[:, :QRANK + KVRANK + ROPE]).astype(bf16)
        part_gains = jnp.sum(gains_all, axis=0).astype(bf16)
        side = part_down.shape[1]
        gain_rows = -(-part_gains.shape[0] // side)
        part_gains = jnp.pad(part_gains, (0, gain_rows * side - part_gains.shape[0])).reshape(gain_rows, side)
        part_down = jnp.concatenate([part_down, part_gains], axis=0)
        return part_down, part_latent, part_query

    me = lax.axis_index("shard")
    if count == 4:
        grad_gate, grad_up, total_output = together(grad_gate, grad_up, total_output)
        away = [owner_gradient(two_all, grad_gate, me ^ step, count) for step in (2, 3)]
        brought = [[swap(part, 2 + i) for i, part in enumerate(away)]]
        two_all, _, exchanged, total_output = together(two_all, away, exchanged, total_output)
        shares = attention_shares(exchanged)
        two_all, *shares = together(two_all, *shares)
        total_down_both, total_latent, total_query = lax.psum(tuple(shares), "rep")
        away = [owner_gradient(two_all, grad_up, me ^ step, count) for step in (2, 3)]
        brought.append([swap(part, 2 + i) for i, part in enumerate(away)])
        two_all, _ = together(two_all, away)
        near = chip_gradients(two_all, grad_gate, grad_up)
        activated_all, near[0], brought[0] = together(activated_all, near[0], brought[0])
        total_down = down_gradient(activated_all, down_all)
        hidden_parts = [[near[2 + i], swap(near[i], 1), *brought[i]] for i in range(2)]
        total_down, hidden_parts[0] = together(total_down, hidden_parts[0])
    else:
        parts = [
            [owner_gradient(two_all, grad, me ^ step, count) for grad in (grad_gate, grad_up)] for step in range(count)
        ]
        hidden_parts = [
            [swap(parts[step][i], step) if step else parts[step][i] for step in range(count)] for i in range(2)
        ]
        total_down_both, total_latent, total_query = lax.psum(attention_shares(exchanged), "rep")
        total_down = contract_rows(activated_all, down_all)
        total_down = lax.dynamic_slice_in_dim(total_down, take_at(offsets, me), size, 0)
    total_gate = place_windows(hidden_parts[0], count)
    total_gate, total_down_both, total_latent, total_query = together(
        total_gate, total_down_both, total_latent, total_query
    )
    gain_rows = total_down_both.shape[0] - D // count
    gain_totals = total_down_both[-gain_rows:].reshape(-1).astype(f32)
    total_down_both = total_down_both[:-gain_rows].astype(f32)
    first, second, third = D, D + QRANK, D + QRANK + KVRANK
    hidden_parts[1][0], total_gate, *finished = together(
        hidden_parts[1][0], total_gate, total_down_both[:, :QRANK], total_down_both[:, QRANK:],
        total_query.astype(f32), total_latent.astype(f32), gain_totals[:first], gain_totals[first:second],
        gain_totals[second:third], gain_totals[third:third + D],
    )
    total_down_q, total_down_kv, total_query, total_latent, *gain_totals = finished
    total_up = place_windows(hidden_parts[1], count)
    return (
        boundary[None],
        grad[None],
        gain_totals[0][None],
        gain_totals[1][None],
        gain_totals[2][None],
        gain_totals[3][None],
        total_down_q[None],
        total_query[None],
        total_down_kv[None],
        total_latent[None],
        total_output.astype(f32)[None],
        total_gate[None],
        total_up[None],
        total_down[None],
    )


def solution(mesh):
    tokens = P(("rep", "shard"), None)
    gain = P("section", None)
    weight = P("section", "shard", None)
    out = P("section", ("rep", "shard"), None)
    return jax.shard_map(
        body,
        mesh=mesh,
        in_specs=(tokens, tokens) + (gain,) * 4 + (weight,) * 8 + (tokens,),
        out_specs=(out, out) + (gain,) * 4 + (weight,) * 8,
        check_vma=False,
    )
```
